32 devices in a mesh: wide: 8 (over y, x, core), narrow: 4 (over z).
Axes of the slice: x: 2, y: 2, z: 4, core: 2. Of those that a mesh axis runs over, the one named last changes fastest.
Arguments:
- tokens: bfloat16 [32768, 768], P(('wide', 'narrow')), may hold values from -6 to 6
- doc_lengths: int32 [64, 4], P(('wide', 'narrow')), may hold values from 1 to 256, 512 in all within a row
- cotangent: bfloat16 [32768, 768], P(('wide', 'narrow')), may hold values from -6 to 6
- owners: int32 [12], replicated, may hold values from 0 to 3, as said below
- step_count: int32 [1], replicated, may hold values from 1 to 20
- master: float32 [768, 24, 768], P('wide', 'narrow')
- moment_one: float32 [768, 24, 768], P('wide', 'narrow')
- moment_two: float32 [768, 24, 768], P('wide', 'narrow'), as said below
- vectors: float32 [13, 768], replicated
- vector_one: float32 [13, 768], replicated
- vector_two: float32 [13, 768], replicated, as said below
Outputs:
- layer_out: bfloat16 [32768, 768], P(('wide', 'narrow'))
- input_grad: float32 [32768, 768], P(('wide', 'narrow'))
- grad_norm: float32 [], replicated
- block_grads: float32 [768, 24, 768], P('wide', 'narrow')
- new_master: float32 [768, 24, 768], P('wide', 'narrow')
- new_first: float32 [768, 24, 768], P('wide', 'narrow')
- new_second: float32 [768, 24, 768], P('wide', 'narrow')
- new_copies: bfloat16 [768, 24, 768], P('wide', 'narrow')
- vector_grads: float32 [13, 768], replicated
- new_vectors: float32 [13, 768], replicated
- vector_first: float32 [13, 768], replicated
- vector_second: float32 [13, 768], replicated
The draws below stay inside these ranges and needn't reach their ends.
Inputs may be any that keep to these rules, and one draw needn't show every extreme that they name: `owners`: each index of narrow owns at most 6 of the 12 blocks, and one owns exactly 6. `doc_lengths`: each row sums to 512; its longest document has exactly 256 tokens. `moment_two`: Positive. `vector_two`: Positive.
All inputs are finite; a program needn't handle non-finite values.
Results may differ from the reference program's by a relative error of at most 0.0098.
Values may be sent and summed in bfloat16 or wider, within the bound.
No kernel may reach another device: no remote copies, remote signals or barrier semaphores. Data moves between devices by JAX's collectives and lax.ppermute only.
A program may use at most 256 MiB of HBM per device.

```python
import math
import jax
import jax.numpy as jnp
import numpy as np
from jax import lax

D = 768
HEADS = 12
HEAD = 64
ROT = 16
FF = 3072
LENGTH = 512
DOCS = 4
DOC_MOST = 256
SEQS = 64
TOKENS = 32768
BLOCKS = 12
CAP = 6
SLOTS = 24
SMALL = 13
N_NARROW = 4


def owner_table(key):
    base = jax.random.fold_in(key, 101)
    order = jax.random.permutation(jax.random.fold_in(base, 1), BLOCKS)
    busiest = jax.random.randint(jax.random.fold_in(base, 2), (), 0, N_NARROW)
    others = (busiest + 1 + jax.random.randint(jax.random.fold_in(base, 3), (BLOCKS,), 0, N_NARROW - 1)) % N_NARROW
    chosen = jnp.where(jnp.arange(BLOCKS) < CAP, busiest, others).astype(jnp.int32)
    return jnp.zeros((BLOCKS,), jnp.int32).at[order].set(chosen)


def slot_scales(key):
    owners = owner_table(key)
    order = jnp.arange(BLOCKS, dtype=jnp.int32)
    before = (owners[:, None] == owners[None, :]) & (order[None, :] < order[:, None])
    slot_of = owners * CAP + jnp.sum(before.astype(jnp.int32), axis=1)
    hit = slot_of[None, :] == jnp.arange(SLOTS, dtype=jnp.int32)[:, None]
    block_at = jnp.sum(jnp.where(hit, order[None, :], 0), axis=1)
    drawn = D ** (-0.5)
    scales = jnp.where(block_at == 3, 4.0 * drawn, drawn)
    return jnp.where(block_at >= 4 + FF // D, FF ** (-0.5), scales).astype(jnp.float32)


def grad_scale():
    return (BLOCKS * D * D + SMALL * D) ** (-0.5)


def draw_owners(key, part):
    return owner_table(key)


def draw_master(key, part):
    noise = jnp.clip(jax.random.normal(jax.random.fold_in(key, 201), (D, SLOTS, D), jnp.float32), -6.0, 6.0)
    return noise * slot_scales(key)[None, :, None]


def draw_moment_one(key, part):
    noise = jnp.clip(jax.random.normal(jax.random.fold_in(key, 202), (D, SLOTS, D), jnp.float32), -6.0, 6.0)
    return noise * grad_scale()


def draw_moment_two(key, part):
    factor = jnp.exp(jax.random.uniform(jax.random.fold_in(key, 203), (D, SLOTS, D), jnp.float32, 0.0, math.log(4.0)))
    return factor * grad_scale() ** 2


def draw_vectors(key, part):
    rows = jnp.arange(SMALL)[:, None]
    gains = 1.0 + jax.random.uniform(jax.random.fold_in(key, 204), (SMALL, D), jnp.float32, -0.3, 0.3)
    biases = 0.3 * jnp.clip(jax.random.normal(jax.random.fold_in(key, 205), (SMALL, D), jnp.float32), -6.0, 6.0)
    return jnp.where((rows == 0) | (rows == 2), gains, biases)


def draw_vector_one(key, part):
    noise = jnp.clip(jax.random.normal(jax.random.fold_in(key, 206), (SMALL, D), jnp.float32), -6.0, 6.0)
    return noise * (3.0 * grad_scale())


def draw_vector_two(key, part):
    factor = jnp.exp(jax.random.uniform(jax.random.fold_in(key, 207), (SMALL, D), jnp.float32, 0.0, math.log(4.0)))
    return factor * (9.0 * grad_scale() ** 2)


def levels(stream_key, shape, split, least, high):
    loudness, own = 1.0, jax.random.fold_in(stream_key, 6)
    for dim, blocks in split:
        heights = jnp.exp(jax.random.uniform(jax.random.fold_in(own, dim), (blocks,), jnp.float32, least / len(split), high / len(split)))
        loudness = loudness * jnp.repeat(heights, shape[dim] // blocks).reshape([-1 if axis == dim else 1 for axis in range(len(shape))])
    return loudness


def split_up(count, total, bound, skew):
    loads = [(1 << 20) // math.isqrt(standing ** skew) + 1 for standing in range(2, count + 1)]
    surplus, holding = total - bound - (count - 1), [1] * (count - 1)
    while surplus > 0:
        free = [i for i in range(count - 1) if holding[i] < bound]
        mass, remaining = sum([loads[i] for i in free]), surplus
        for i in free:
            addition = min(bound - holding[i], max(1, remaining * loads[i] // mass), surplus)
            holding[i] = holding[i] + addition
            surplus = surplus - addition
    return np.array([bound] + holding)


def ragged_sizes(stream_key, number_of, total, most, skew):
    if number_of == 2:
        one = jax.random.randint(stream_key, (), max(1, total - most), min(most, total - 1) + 1)
        return jnp.stack([one, total - one])
    tallies = jnp.asarray(split_up(number_of, total, most, skew), jnp.int32)
    pairs = (number_of - 1) // 2
    source_of, taker = tallies[1:1 + 2 * pairs:2], tallies[2:2 + 2 * pairs:2]
    slack = jnp.minimum(source_of - 1, most - taker)
    moved = jax.random.randint(jax.random.fold_in(stream_key, 1), (pairs,), 0, 1 << 20) % (slack + 1)
    tallies = tallies.at[1:1 + 2 * pairs:2].set(source_of - moved).at[2:2 + 2 * pairs:2].set(taker + moved)
    return tallies[jax.random.permutation(jax.random.fold_in(stream_key, 2), number_of)]


def bell_draw(own_key, shape, deviation, reach, cuts=(), kind=jnp.bfloat16):
    array = deviation * jax.random.normal(own_key, shape, jnp.float32)
    if cuts:
        array = array * levels(own_key, shape, cuts, -0.22, 0.18)
    return jnp.clip(array, -reach, reach).astype(kind)


def setup_inputs(seed: int = 0) -> dict:
    arg_keys = jax.random.split(jax.random.key(seed), 12)
    tokens = bell_draw(arg_keys[0], (TOKENS, D), 1.0, 6.0, ((0, 32),))
    doc_lengths = jax.vmap(lambda own: ragged_sizes(own, DOCS, LENGTH, DOC_MOST, 2))(jax.random.split(arg_keys[1], SEQS)).reshape((SEQS, DOCS)).astype(jnp.int32)
    cotangent = bell_draw(arg_keys[2], (TOKENS, D), 1.0, 6.0, ((0, 32),))
    owners = draw_owners(jax.random.fold_in(arg_keys[11], 71), 0)
    step_count = jax.random.randint(arg_keys[4], (1,), 1, 21).astype(jnp.int32)
    master = draw_master(jax.random.fold_in(arg_keys[11], 71), 0)
    moment_one = draw_moment_one(jax.random.fold_in(arg_keys[11], 71), 0)
    moment_two = draw_moment_two(jax.random.fold_in(arg_keys[11], 71), 0)
    vectors = draw_vectors(jax.random.fold_in(arg_keys[11], 71), 0)
    vector_one = draw_vector_one(jax.random.fold_in(arg_keys[11], 71), 0)
    vector_two = draw_vector_two(jax.random.fold_in(arg_keys[11], 71), 0)
    return {"tokens": tokens, "doc_lengths": doc_lengths, "cotangent": cotangent, "owners": owners, "step_count": step_count, "master": master, "moment_one": moment_one, "moment_two": moment_two, "vectors": vectors, "vector_one": vector_one, "vector_two": vector_two}


highest = lax.Precision.HIGHEST
norm_epsilon = 1e-05
beta_first = 0.5
beta_second = 0.5
adam_epsilon = 1e-08
learn_rate = 0.02
vector_rate = 0.1
weight_decay = 0.1
masked_fill = -1e+30
rope_base = 10000.0

@jax.custom_vjp
def low(v):
    return lax.optimization_barrier(v.astype(jnp.bfloat16)).astype(jnp.float32)

@jax.custom_vjp
def low_back(v):
    return v

def low_keep(v):
    return (low(v), None)

def low_pass(kept, grad):
    return (grad,)

def back_keep(v):
    return (v, None)

def back_low(kept, grad):
    return (low(grad),)
low.defvjp(low_keep, low_pass)
low_back.defvjp(back_keep, back_low)

def slot_table(owners, capacity):
    number = owners.shape[0]
    order = jnp.arange(number, dtype=jnp.int32)
    before = (owners[:, None] == owners[None, :]) & (order[None, :] < order[:, None])
    return (owners * capacity + lax.optimization_barrier(jnp.sum(before.astype(jnp.int32), axis=1))).astype(jnp.int32)

def doc_layout(lengths, seq_length):
    ends = jnp.cumsum(lengths, axis=1)
    position = jnp.arange(seq_length, dtype=jnp.int32)
    passed = position[None, :, None] >= ends[:, None, :]
    doc_index = lax.optimization_barrier(jnp.sum(passed.astype(jnp.int32), axis=2))
    doc_start = lax.optimization_barrier(jnp.sum(jnp.where(passed, lengths[:, None, :], 0), axis=2))
    visible = (doc_index[:, :, None] == doc_index[:, None, :]) & (position[None, :, None] >= position[None, None, :])
    return (visible, position[None, :] - doc_start)

def angles(offsets, rotary):
    half = rotary // 2
    freqs = jnp.power(rope_base, -2.0 * jnp.arange(half, dtype=jnp.float32) / rotary)
    turned = offsets.astype(jnp.float32)[:, :, None] * freqs
    doubled = jnp.concatenate([turned, turned], axis=-1)[:, :, None, :]
    return (jnp.cos(doubled), jnp.sin(doubled))

def rotate(values, cosine, sine_part):
    rotary = cosine.shape[-1]
    half = rotary // 2
    head_part = values[..., :rotary]
    swapped = jnp.concatenate([-head_part[..., half:], head_part[..., :half]], axis=-1)
    return jnp.concatenate([head_part * cosine + swapped * sine_part, values[..., rotary:]], axis=-1)

def layer_norms(inputs, vectors):
    centred = inputs - lax.optimization_barrier(jnp.mean(inputs, axis=-1, keepdims=True))
    scaled = centred * lax.rsqrt(lax.optimization_barrier(jnp.mean(centred * centred, axis=-1, keepdims=True)) + norm_epsilon)
    return (scaled * vectors[0] + vectors[1], scaled * vectors[2] + vectors[3])

def block_forward(stream, w_qkv, w_out, w_up, w_down, vectors, lengths):
    seq_count = lengths.shape[0]
    seq_length = stream.shape[0] // seq_count
    model_width = stream.shape[1]
    spread = w_up.shape[1]
    norm_one, norm_two = layer_norms(stream, vectors)
    h_one = low(norm_one)
    h_two = low(norm_two)
    qkv = low_back(jnp.einsum('td,dkc->tkc', h_one, w_qkv, precision=highest) + vectors[4:7])
    shaped = qkv.reshape(seq_count, seq_length, 3, HEADS, HEAD)
    visible, offsets = doc_layout(lengths, seq_length)
    cosine, sine_part = angles(offsets, ROT)
    queries = low(rotate(shaped[:, :, 0], cosine, sine_part))
    key_low = low(rotate(shaped[:, :, 1], cosine, sine_part))
    value_low = low(shaped[:, :, 2])
    scores = low_back(jnp.einsum('sqhd,skhd->shqk', queries, key_low, precision=highest) * HEAD ** (-0.5))
    prob_rows = jax.nn.softmax(jnp.where(visible[:, None], scores, masked_fill), axis=-1)
    mixed = jnp.einsum('shqk,skhd->sqhd', low(prob_rows), value_low, precision=highest)
    attn_in = low(low_back(mixed.reshape(seq_count * seq_length, model_width)))
    attn_out = jnp.dot(attn_in, w_out, precision=highest) + vectors[7]
    pre_act = low_back(jnp.einsum('td,djc->tjc', h_two, w_up, precision=highest) + vectors[8:8 + spread])
    act_low = low(jax.nn.gelu(pre_act, approximate=False))
    mlp_out = jnp.einsum('tjr,rjc->tc', act_low, w_down, precision=highest) + vectors[8 + spread]
    return stream + attn_out + mlp_out

def adam_update(gradient, weight, moment, square, rate, decay, first_fix, second_fix):
    moment_new = beta_first * moment + (1.0 - beta_first) * gradient
    square_new = beta_second * square + (1.0 - beta_second) * gradient * gradient
    update = moment_new / first_fix / (jnp.sqrt(square_new / second_fix) + adam_epsilon)
    return (weight - rate * (update + decay * weight), moment_new, square_new)

def reference(tokens, doc_lengths, cotangent, owners, step_count, master, moment_one, moment_two, vectors, vector_one, vector_two):
    spread = FF // D
    slot_of = slot_table(owners, CAP)
    weights = low(jnp.take(master, slot_of, axis=1))
    w_qkv = weights[:, 0:3]
    w_out = weights[:, 3]
    w_up = weights[:, 4:4 + spread]
    w_down = weights[:, 4 + spread:]
    group = math.gcd(SEQS, 2 ** ((4096 // LENGTH).bit_length() - 1))
    rounds = SEQS // group
    inputs = tokens.astype(jnp.float32).reshape(rounds, group * LENGTH, D)
    upstream = cotangent.astype(jnp.float32).reshape(rounds, group * LENGTH, D)
    lengths = doc_lengths.reshape(rounds, group, DOCS)

    def one_round(carry, item):
        round_in, round_cot, round_len = item

        def forward(stream, qkv_w, out_w, up_w, down_w, vector_w):
            return block_forward(stream, qkv_w, out_w, up_w, down_w, vector_w, round_len)
        result, backward = jax.vjp(forward, round_in, w_qkv, w_out, w_up, w_down, vectors)
        grads = backward(round_cot)
        carry = tuple((total + extra for total, extra in zip(carry, grads[1:])))
        return (carry, (result.astype(jnp.bfloat16), grads[0]))
    begin = (jnp.zeros_like(w_qkv), jnp.zeros_like(w_out), jnp.zeros_like(w_up), jnp.zeros_like(w_down), jnp.zeros_like(vectors))
    sums, (results, input_grads) = lax.scan(one_round, begin, (inputs, upstream, lengths))
    all_grads = jnp.concatenate([sums[0], sums[1][:, None], sums[2], sums[3]], axis=1)
    grad_norm = jnp.sqrt(jnp.sum(all_grads * all_grads) + jnp.sum(sums[4] * sums[4]))
    clip_factor = jnp.minimum(1.0, 1.0 / (grad_norm + 1e-06))
    step_float = step_count[0].astype(jnp.float32)
    first_fix = 1.0 - jnp.power(beta_first, step_float)
    second_fix = 1.0 - jnp.power(beta_second, step_float)
    clipped = all_grads * clip_factor
    new_w, new_m, new_v = adam_update(clipped, jnp.take(master, slot_of, axis=1), jnp.take(moment_one, slot_of, axis=1), jnp.take(moment_two, slot_of, axis=1), learn_rate, weight_decay, first_fix, second_fix)

    def placed(values):
        return jnp.zeros((D, SLOTS, D), values.dtype).at[:, slot_of].set(values)
    new_master = placed(new_w)
    vector_grads = sums[4] * clip_factor
    new_vectors, vector_first, vector_second = adam_update(vector_grads, vectors, vector_one, vector_two, vector_rate, 0.0, first_fix, second_fix)
    return (results.reshape(TOKENS, D), input_grads.reshape(TOKENS, D), grad_norm, placed(clipped), new_master, placed(new_m), placed(new_v), new_master.astype(jnp.bfloat16), vector_grads, new_vectors, vector_first, vector_second)
```

```python
from functools import partial

import jax
import jax.numpy as jnp
from jax import lax
from jax.experimental import pallas as pl
from jax.experimental.pallas import tpu as pltpu
from jax.sharding import PartitionSpec as P

D = 768
HEADS = 12
HEAD = 64
ROT = 16
FF = 3072
SPREAD = FF // D

norm_epsilon = 1e-05
beta_first = 0.5
beta_second = 0.5
adam_epsilon = 1e-08
learn_rate = 0.02
vector_rate = 0.1
weight_decay = 0.1
masked_fill = -1e30
rope_base = 10000.0
LOG2E = 1.4426950408889634

BF = jnp.bfloat16
F32 = jnp.float32
MB = 1 << 20
ANY = pl.BlockSpec(memory_space=pl.ANY)
SMEM = pl.BlockSpec(memory_space=pltpu.SMEM)


def dot(a, b):
    return lax.dot_general(a, b, (((1,), (0,)), ((), ())), preferred_element_type=F32)


def dot_nt(a, b):
    return lax.dot_general(a, b, (((1,), (1,)), ((), ())), preferred_element_type=F32)


def dot_tn(a, b):
    return lax.dot_general(a, b, (((0,), (0,)), ((), ())), preferred_element_type=F32)


def params(mib, flops=0, moved=0, **more):
    return dict(
        compiler_params=pltpu.CompilerParams(vmem_limit_bytes=int(mib * MB), **more),
        cost_estimate=pl.CostEstimate(
            flops=int(flops), bytes_accessed=int(moved), transcendentals=0
        ),
    )


class Group:
    def __init__(self, arrays, plan):
        self.arrays = tuple(arrays)
        self.plan = plan


def row_of(spec, rows, me):
    if spec[0] == "at":
        return spec[1]
    return pl.multiple_of((me ^ spec[1]) * rows, rows)


def weight_copies(group, refs, i, dst, sems, me):
    copies = []
    for n, (array, lead, rows, spec) in enumerate(group.plan(i)):
        copies.append(
            pltpu.make_async_copy(
                refs[array].at[lead], dst.at[pl.ds(row_of(spec, rows, me), rows)], sems.at[n]
            )
        )
    return copies


def grad_copies(plan, refs, i, src, sems, me):
    copies = []
    for n, (array, lead, rows, spec) in enumerate(plan(i)):
        copies.append(
            pltpu.make_async_copy(
                src.at[pl.ds(row_of(spec, rows, me), rows)], refs[array].at[lead], sems.at[n]
            )
        )
    return copies


def norms_of(x):
    mean = jnp.mean(x, axis=-1, keepdims=True)
    centred = x - mean
    scale = lax.rsqrt(jnp.mean(centred * centred, axis=-1, keepdims=True) + norm_epsilon)
    return centred * scale, scale


def layer_norms(tokens, vectors):
    rows = tokens.shape[0]
    tile = 256

    def body(x_ref, v_ref, one_ref, two_ref):
        xhat, _ = norms_of(x_ref[...].astype(F32))
        one_ref[...] = (xhat * v_ref[0:1] + v_ref[1:2]).astype(BF)
        two_ref[...] = (xhat * v_ref[2:3] + v_ref[3:4]).astype(BF)

    spec = pl.BlockSpec((tile, D), lambda t: (t, 0))
    return pl.pallas_call(
        body,
        grid=(rows // tile,),
        in_specs=[spec, pl.BlockSpec(vectors.shape, lambda t: (0, 0))],
        out_specs=[spec, spec],
        out_shape=[jax.ShapeDtypeStruct((rows, D), BF)] * 2,
        **params(16, 20 * rows * D, 6 * rows * D),
    )(tokens, vectors)


def pack_owned(masters, table, groups):
    rows = masters.shape[1]

    def body(t_ref, m_ref, *outs):
        for out, blocks in zip(outs, groups):
            for i, b in enumerate(blocks):
                value = m_ref[t_ref[0, b]]
                out[i] = jnp.where(t_ref[1, b] > 0, value, 0.0).astype(BF)

    return pl.pallas_call(
        body,
        in_specs=[SMEM, pl.BlockSpec(memory_space=pltpu.VMEM)],
        out_specs=[pl.BlockSpec(memory_space=pltpu.VMEM)] * len(groups),
        out_shape=[jax.ShapeDtypeStruct((len(g), rows, D), BF) for g in groups],
        **params(16, rows * D * 12, rows * D * 4 * 12),
    )(table, masters)


def gelu_pair(z):
    size = jnp.abs(z)
    t = pl.reciprocal(1.0 + (0.3275911 * 0.7071067811865476) * size)
    bell = jnp.exp2((-0.5 * LOG2E) * (z * z))
    poly = 0.5 * 1.061405429
    for c in (-1.453152027, 1.421413741, -0.284496736, 0.254829592):
        poly = poly * t + 0.5 * c
    tail = poly * t * bell
    cdf = jnp.where(z >= 0.0, 1.0 - tail, tail)
    return z * cdf, cdf + z * (bell * 0.3989422804014327)


def mlp_chunk(me, h_two, cot, bias, group, i_up, i_down, outs, plan):
    rows = h_two.shape[0]
    tile = rows // 2
    na, no = len(group.arrays), len(outs)
    n_in, n_out = len(group.plan(0)), len(plan(0))

    def body(me_ref, h_ref, y_ref, b_ref, *rest):
        w_refs = rest[:na]
        act_ref, dz_ref, db_ref = rest[na : na + 3]
        o_refs = rest[na + 3 : na + 3 + no]
        w_up, w_down, acc_up, acc_down, low, in_sem, out_sem = rest[na + 3 + no :]
        step = pl.program_id(0)
        me_id = me_ref[0]

        @pl.when(step == 0)
        def _():
            ups = weight_copies(group, w_refs, i_up, w_up, in_sem.at[0], me_id)
            downs = weight_copies(group, w_refs, i_down, w_down, in_sem.at[1], me_id)
            for c in ups + downs:
                c.start()
            for c in ups + downs:
                c.wait()

        part = 256
        sums = jnp.zeros((1, D), F32)
        for p in range(tile // part):
            at = pl.ds(p * part, part)
            h = h_ref[at]
            y = y_ref[at]
            z = dot(h, w_up[...]) + b_ref[...]
            u = dot_nt(y, w_down[...])
            act, slope = gelu_pair(z)
            dz = (u * slope).astype(BF)
            act_ref[at] = act.astype(BF)
            dz_ref[at] = dz
            sums = sums + jnp.sum(dz.astype(F32), axis=0, keepdims=True)
        d_up = dot_tn(h_ref[...], dz_ref[...])
        d_down = dot_tn(act_ref[...], y_ref[...])

        @pl.when(step == 0)
        def _():
            acc_up[...] = d_up
            acc_down[...] = d_down
            db_ref[...] = sums

        @pl.when(step == 1)
        def _():
            db_ref[...] += sums
            low[0] = (acc_up[...] + d_up).astype(BF)
            low[1] = (acc_down[...] + d_down).astype(BF)
            ups = grad_copies(plan, o_refs, 0, low.at[0], out_sem.at[0], me_id)
            downs = grad_copies(plan, o_refs, 1, low.at[1], out_sem.at[1], me_id)
            for c in ups + downs:
                c.start()
            for c in ups + downs:
                c.wait()

    spec = pl.BlockSpec((tile, D), lambda t: (t, 0))
    row = pl.BlockSpec((1, D), lambda t: (0, 0))
    act, dz, db, *grads = pl.pallas_call(
        body,
        grid=(2,),
        in_specs=[SMEM, spec, spec, row] + [ANY] * na,
        out_specs=[spec, spec, row] + [ANY] * no,
        out_shape=[
            jax.ShapeDtypeStruct((rows, D), BF),
            jax.ShapeDtypeStruct((rows, D), BF),
            jax.ShapeDtypeStruct((1, D), F32),
            *outs,
        ],
        scratch_shapes=[
            pltpu.VMEM((D, D), BF),
            pltpu.VMEM((D, D), BF),
            pltpu.VMEM((D, D), F32),
            pltpu.VMEM((D, D), F32),
            pltpu.VMEM((2, D, D), BF),
            pltpu.SemaphoreType.DMA((2, n_in)),
            pltpu.SemaphoreType.DMA((2, n_out)),
        ],
        **params(40, 8 * rows * D * D, 16 * rows * D),
    )(me, h_two, cot, bias, *group.arrays)
    return act, dz, db, grads


def turned(x, cosine, from_right, from_left):
    return (
        x * cosine
        + pltpu.roll(x, 128 - ROT // 2, 1) * from_right
        + pltpu.roll(x, ROT // 2, 1) * from_left
    )


def project(me, h_one, cot, bias, tables, group):
    rows = h_one.shape[0]
    tile = 256
    na, n_in = len(group.arrays), len(group.plan(0))

    def body(me_ref, h_ref, y_ref, b_ref, c_ref, s_ref, *rest):
        w_refs = rest[:na]
        outs = rest[na : na + 4]
        w_all, sems = rest[na + 4 :]
        step = pl.program_id(0)

        def copies(i):
            return weight_copies(group, w_refs, i, w_all.at[i], sems.at[i], me_ref[0])

        @pl.when(step == 0)
        def _():
            for i in range(4):
                for c in copies(i):
                    c.start()

        for i in range(4):

            @pl.when(step == 0)
            def _(i=i):
                for c in copies(i):
                    c.wait()

            if i == 3:
                outs[3][...] = dot_nt(y_ref[...], w_all[3]).astype(BF)
                continue
            value = dot(h_ref[...], w_all[i]) + b_ref[i : i + 1]
            if i == 2:
                outs[2][...] = value.astype(BF)
                continue
            cosine, right, left = c_ref[...], s_ref[0], s_ref[1]
            for j in range(D // 128):
                outs[i][:, j * 128 : (j + 1) * 128] = turned(
                    value[:, j * 128 : (j + 1) * 128], cosine, -right, left
                ).astype(BF)

    spec = pl.BlockSpec((tile, D), lambda t: (t, 0))
    return pl.pallas_call(
        body,
        grid=(rows // tile,),
        in_specs=[
            SMEM,
            spec,
            spec,
            pl.BlockSpec((3, D), lambda t: (0, 0)),
            pl.BlockSpec((tile, 128), lambda t: (t, 0)),
            pl.BlockSpec((2, tile, 128), lambda t: (0, t, 0)),
        ]
        + [ANY] * na,
        out_specs=[spec] * 4,
        out_shape=[jax.ShapeDtypeStruct((rows, D), BF)] * 4,
        scratch_shapes=[pltpu.VMEM((4, D, D), BF), pltpu.SemaphoreType.DMA((4, n_in))],
        **params(32, 8 * rows * D * D, 20 * rows * D),
    )(me, h_one, cot, bias, *tables, *group.arrays)


def attention(q, k, v, da, starts, tables, half_tables, length):
    rows = q.shape[0]
    seqs = rows // length
    half = length // 2
    pair = 128

    def body(q_ref, k_ref, v_ref, d_ref, st_ref, c_ref, s_ref, hc_ref, hs_ref, a_ref, dq_ref, dk_ref, dv_ref, db_ref, mask):
        @pl.when(pl.program_id(1) == 0)
        def _():
            key = lax.broadcasted_iota(jnp.int32, (length, length), 0)
            query = lax.broadcasted_iota(jnp.int32, (length, length), 1)
            seen = (key <= query) & (key >= st_ref[0])
            mask[...] = jnp.where(seen, 0.0, masked_fill)

        q_all, k_all, v_all, d_all = q_ref[...], k_ref[...], v_ref[...], d_ref[...]
        vt, kt = v_all.T, k_all.T
        dt = d_all.T.astype(F32)
        lane = lax.broadcasted_iota(jnp.int32, (length, pair), 1)
        zero = jnp.zeros((), BF)
        at, dqt = [], []
        dv = [jnp.zeros((half, pair), F32)] * 2
        dk = [jnp.zeros((half, pair), F32)] * 2
        for h in range(2):
            mine = (lane >= h * HEAD) & (lane < (h + 1) * HEAD)
            qm = jnp.where(mine, q_all, zero)
            dm = jnp.where(mine, d_all, zero)
            vh, kh = vt[h * HEAD : (h + 1) * HEAD], kt[h * HEAD : (h + 1) * HEAD]
            dh = dt[h * HEAD : (h + 1) * HEAD]
            a_parts, q_parts = [], []
            for b in range(2):
                n = half * (b + 1)
                at_q = slice(b * half, (b + 1) * half)
                s = dot_nt(k_all[:n], qm[at_q]) * (HEAD**-0.5 * LOG2E) + mask[:n, at_q]
                e = jnp.exp2(s - jnp.max(s, axis=0, keepdims=True))
                p = e * (1.0 / jnp.sum(e, axis=0, keepdims=True))
                low = p.astype(BF)
                a_t = dot(vh[:, :n], low)
                total = jnp.sum(dh[:, at_q] * a_t, axis=0, keepdims=True)
                ds = (p * (dot_nt(v_all[:n], dm[at_q]) - total)).astype(BF)
                a_parts.append(a_t)
                q_parts.append(dot(kh[:, :n], ds))
                more_v, more_k = dot(low, dm[at_q]), dot(ds, qm[at_q])
                for c in range(b + 1):
                    dv[c] = dv[c] + more_v[c * half : (c + 1) * half]
                    dk[c] = dk[c] + more_k[c * half : (c + 1) * half]
            at.append(jnp.concatenate(a_parts, axis=1))
            dq = jnp.concatenate(q_parts, axis=1) * HEAD**-0.5
            u, w, cos, sin = dq[0:8], dq[8:16], hc_ref[0], hs_ref[0]
            dqt.append(jnp.concatenate([u * cos + w * sin, w * cos - u * sin, dq[16:]], axis=0))
        a_ref[...] = jnp.concatenate(at, axis=0).astype(BF).T
        dq = jnp.concatenate(dqt, axis=0).astype(BF).T
        dq_ref[...] = dq
        sums = [jnp.sum(dq.astype(F32), axis=0, keepdims=True)]
        sum_k = sum_v = jnp.zeros((1, pair), F32)
        for c in range(2):
            at_k = slice(c * half, (c + 1) * half)
            back = turned(dk[c] * HEAD**-0.5, c_ref[at_k], s_ref[0, at_k], -s_ref[1, at_k]).astype(BF)
            dk_ref[at_k] = back
            sum_k = sum_k + jnp.sum(back.astype(F32), axis=0, keepdims=True)
            value = dv[c].astype(BF)
            dv_ref[at_k] = value
            sum_v = sum_v + jnp.sum(value.astype(F32), axis=0, keepdims=True)
        db_ref[0] = jnp.concatenate(sums + [sum_k, sum_v], axis=0)

    spec = pl.BlockSpec((length, pair), lambda s, h: (s, h))
    a, dq, dk, dv, db = pl.pallas_call(
        body,
        grid=(seqs, D // pair),
        in_specs=[
            spec,
            spec,
            spec,
            spec,
            pl.BlockSpec((1, 1, length), lambda s, h: (s, 0, 0)),
            pl.BlockSpec((length, 128), lambda s, h: (s, 0)),
            pl.BlockSpec((2, length, 128), lambda s, h: (0, s, 0)),
            pl.BlockSpec((1, ROT // 2, length), lambda s, h: (s, 0, 0)),
            pl.BlockSpec((1, ROT // 2, length), lambda s, h: (s, 0, 0)),
        ],
        out_specs=[spec, spec, spec, spec, pl.BlockSpec((1, 3, pair), lambda s, h: (s, 0, h))],
        out_shape=[jax.ShapeDtypeStruct((rows, D), BF)] * 4
        + [jax.ShapeDtypeStruct((seqs, 3, D), F32)],
        scratch_shapes=[pltpu.VMEM((length, length), F32)],
        **params(32, 20e9, 20 * rows * D),
    )(q, k, v, da, starts, *tables, *half_tables)
    return a, dq, dk, dv, jnp.sum(db, axis=0)


def attention_grads(me, h_one, a, cot, dqkv, outs, plan):
    rows = h_one.shape[0]
    no, n_out = len(outs), len(plan(0))

    def body(me_ref, h_ref, a_ref, y_ref, dq_ref, dk_ref, dv_ref, *rest):
        o_refs = rest[:no]
        low, sems = rest[no:]
        pending = []
        for i, (left, right) in enumerate(
            ((h_ref, dq_ref), (h_ref, dk_ref), (h_ref, dv_ref), (a_ref, y_ref))
        ):
            low[i] = dot_tn(left[...], right[...]).astype(BF)
            copies = grad_copies(plan, o_refs, i, low.at[i], sems.at[i], me_ref[0])
            for c in copies:
                c.start()
            pending += copies
        for c in pending:
            c.wait()

    whole = pl.BlockSpec(memory_space=pltpu.VMEM)
    return pl.pallas_call(
        body,
        in_specs=[SMEM] + [whole] * 6,
        out_specs=[ANY] * no,
        out_shape=list(outs),
        scratch_shapes=[pltpu.VMEM((4, D, D), BF), pltpu.SemaphoreType.DMA((4, n_out))],
        **params(40, 8 * rows * D * D, 12 * rows * D),
    )(me, h_one, a, cot, *dqkv)


def finish(me, tokens, cot, vectors, a, dqkv, acts, dzs, blocks):
    rows = tokens.shape[0]
    tile = 256
    groups = []
    for group, _ in blocks:
        if not any(group is g for g in groups):
            groups.append(group)
    first = {}
    flat = []
    for group in groups:
        first[id(group)] = len(flat)
        flat += list(group.arrays)
    n_in = max(len(g.plan(0)) for g in groups)
    nw = len(flat)
    count = len(blocks)
    order = (3, 8, 9, 10, 11, 0, 1, 2, 4, 5, 6, 7)

    def body(me_ref, x_ref, y_ref, v_ref, a_ref, dq_ref, dk_ref, dv_ref, *rest):
        act_refs, dz_refs = rest[:SPREAD], rest[SPREAD : 2 * SPREAD]
        w_refs = rest[2 * SPREAD : 2 * SPREAD + nw]
        out_ref, grad_ref, sum_ref = rest[2 * SPREAD + nw : 2 * SPREAD + nw + 3]
        w_all, sems = rest[2 * SPREAD + nw + 3 :]
        step = pl.program_id(0)

        def copies(b):
            group, i = blocks[b]
            refs = w_refs[first[id(group)] :]
            return weight_copies(group, refs, i, w_all.at[b], sems.at[b], me_ref[0])

        @pl.when(step == 0)
        def _():
            for b in order:
                for c in copies(b):
                    c.start()

        def weight(b):
            @pl.when(step == 0)
            def _():
                for c in copies(b):
                    c.wait()

            return w_all[b]

        x = x_ref[...].astype(F32)
        y = y_ref[...].astype(F32)
        out = dot(a_ref[...], weight(3))
        for j in range(SPREAD):
            out = out + dot(act_refs[j][...], weight(8 + j))
        out_ref[...] = (x + out + (v_ref[7:8] + v_ref[8 + SPREAD : 9 + SPREAD])).astype(BF)
        d_one = dot_nt(dq_ref[...], weight(0))
        d_one = d_one + dot_nt(dk_ref[...], weight(1))
        d_one = d_one + dot_nt(dv_ref[...], weight(2))
        d_two = dot_nt(dz_refs[0][...], weight(4))
        for j in range(1, SPREAD):
            d_two = d_two + dot_nt(dz_refs[j][...], weight(4 + j))
        xhat, scale = norms_of(x)
        e = d_one * v_ref[0:1] + d_two * v_ref[2:3]
        inner = jnp.mean(e * xhat, axis=-1, keepdims=True)
        grad_ref[...] = y + (e - jnp.mean(e, axis=-1, keepdims=True) - xhat * inner) * scale
        sums = jnp.concatenate(
            [
                jnp.sum(term, axis=0, keepdims=True)
                for term in (d_one * xhat, d_one, d_two * xhat, d_two, y)
            ],
            axis=0,
        )

        @pl.when(step == 0)
        def _():
            sum_ref[...] = sums

        @pl.when(step > 0)
        def _():
            sum_ref[...] += sums

    spec = pl.BlockSpec((tile, D), lambda t: (t, 0))
    return pl.pallas_call(
        body,
        grid=(rows // tile,),
        in_specs=[SMEM, spec, spec, pl.BlockSpec(vectors.shape, lambda t: (0, 0))]
        + [spec] * (4 + 2 * SPREAD)
        + [ANY] * nw,
        out_specs=[spec, spec, pl.BlockSpec((5, D), lambda t: (0, 0))],
        out_shape=[
            jax.ShapeDtypeStruct((rows, D), BF),
            jax.ShapeDtypeStruct((rows, D), F32),
            jax.ShapeDtypeStruct((5, D), F32),
        ],
        scratch_shapes=[pltpu.VMEM((count, D, D), BF), pltpu.SemaphoreType.DMA((count, n_in))],
        **params(48, 24 * rows * D * D, 40 * rows * D),
    )(me, tokens, cot, vectors, a, *dqkv, *acts, *dzs, *flat)


def adam_update(gradient, weight, moment, square, rate, decay, first_fix, second_fix):
    moment_new = beta_first * moment + (1.0 - beta_first) * gradient
    square_new = beta_second * square + (1.0 - beta_second) * gradient * gradient
    update = moment_new / first_fix / (jnp.sqrt(square_new / second_fix) + adam_epsilon)
    return (weight - rate * (update + decay * weight), moment_new, square_new)


def update_blocks(block_at, owned, scalars, summed, masters, firsts, seconds):
    slots, rows, _ = masters.shape

    def body(at_ref, own_ref, s_ref, g_ref, w_ref, m_ref, v_ref, g_out, w_out, m_out, v_out, c_out):
        slot = pl.program_id(0)
        keep = own_ref[slot] > 0
        clip, one_fix, two_fix = s_ref[0], s_ref[1], s_ref[2]
        gradient = g_ref[0].astype(F32) * clip
        moment = beta_first * m_ref[0] + (1.0 - beta_first) * gradient
        square = beta_second * v_ref[0] + (1.0 - beta_second) * gradient * gradient
        weight = w_ref[0]
        update = (moment * one_fix) / (jnp.sqrt(square * two_fix) + adam_epsilon)
        new = weight - learn_rate * (update + weight_decay * weight)
        new = jnp.where(keep, new, 0.0)
        g_out[0] = jnp.where(keep, gradient, 0.0)
        w_out[0] = new
        m_out[0] = jnp.where(keep, moment, 0.0)
        v_out[0] = jnp.where(keep, square, 0.0)
        c_out[0] = new.astype(BF)

    own = pl.BlockSpec((1, rows, D), lambda s, at, keep, sc: (s, 0, 0))
    return pl.pallas_call(
        body,
        grid_spec=pltpu.PrefetchScalarGridSpec(
            num_scalar_prefetch=3,
            grid=(slots,),
            in_specs=[pl.BlockSpec((1, rows, D), lambda s, at, keep, sc: (at[s], 0, 0)), own, own, own],
            out_specs=[own] * 5,
        ),
        out_shape=[jax.ShapeDtypeStruct((slots, rows, D), F32)] * 4
        + [jax.ShapeDtypeStruct((slots, rows, D), BF)],
        **params(24, 20 * slots * rows * D, 32 * slots * rows * D),
    )(block_at, owned, scalars, summed, masters, firsts, seconds)


def swap(value, axis, bit):
    size = lax.axis_size(axis)
    return lax.ppermute(value, axis, [(i, i ^ bit) for i in range(size)])


def add(a, b):
    return (a.astype(F32) + b.astype(F32)).astype(BF)


def line_total(value):
    size = lax.axis_size("narrow")
    if size != 4:
        return lax.psum(value.astype(F32), "narrow").astype(BF)
    here = lax.axis_index("narrow")
    value = add(value, lax.ppermute(value, "narrow", [(0, 1), (3, 2)]))
    value = add(value, lax.ppermute(value, "narrow", [(1, 2), (2, 1)]))
    outer = lax.ppermute(value, "narrow", [(1, 0), (2, 3)])
    return jnp.where((here == 0) | (here == 3), outer, value)


CORE, SIDE, UP = 1, 2, 4
CHIPS = (0, SIDE, UP, SIDE | UP)


def gather_wide(value):
    size = lax.axis_size("wide")
    count, rows, _ = value.shape
    full = lax.all_gather(value, "wide", axis=0, tiled=False)
    if rows % 16:
        full = jnp.swapaxes(full, 0, 1).reshape(1, count, D, D)
        size, rows = 1, D
    return Group((full,), lambda i: [(0, (p, i), rows, ("at", rows * p)) for p in range(size)])


def gather_wide_steps(value):
    size = lax.axis_size("wide")
    count, rows, _ = value.shape
    if size != 8 or count % 2:
        return gather_wide(value)
    side, up = swap(value, "wide", SIDE), swap(value, "wide", UP)
    part = count // 2
    diag_a = swap(side[:part], "wide", UP)
    diag_b = swap(up[part:], "wide", SIDE)
    mine = jnp.stack([value, side, up, jnp.concatenate([diag_a, diag_b], axis=0)])
    other = swap(mine, "wide", CORE)
    masks = [(m, 0) for m in CHIPS] + [(m ^ CORE, 1) for m in CHIPS]
    return Group(
        (mine, other),
        lambda i: [(a, (n % 4, i), rows, ("xor", m)) for n, (m, a) in enumerate(masks)],
    )


def grad_layout(count, rows, size):
    if size != 8:
        return [jax.ShapeDtypeStruct((count, D, D), BF)], lambda i: [(0, (i,), D, ("at", 0))]
    part = count // 2
    shape = jax.ShapeDtypeStruct((4, part, rows, D), BF)

    def plan(i):
        which = 0 if i < part else 1
        order = (0, UP, SIDE, SIDE | UP) if which == 0 else CHIPS
        at = i % part
        keep = [(which, (n, at), rows, ("xor", m)) for n, m in enumerate(order)]
        give = [(2 + which, (n, at), rows, ("xor", m ^ CORE)) for n, m in enumerate(order)]
        return keep + give

    return [shape] * 4, plan


def scatter_wide(grads):
    if len(grads) == 1:
        return lax.psum_scatter(grads[0], "wide", scatter_dimension=1, tiled=True)
    keep_a, keep_b, give_a, give_b = grads
    sum_a = add(keep_a, swap(give_a, "wide", CORE))
    sum_b = add(keep_b, swap(give_b, "wide", CORE))
    sum_a = add(sum_a[:2], swap(sum_a[2:], "wide", SIDE))
    sum_b = add(sum_b[:2], swap(sum_b[2:], "wide", UP))
    sum_a = add(sum_a[0], swap(sum_a[1], "wide", UP))
    sum_b = add(sum_b[0], swap(sum_b[1], "wide", SIDE))
    return jnp.concatenate([sum_a, sum_b], axis=0)


def total_all(value):
    for axis in ("wide", "narrow"):
        value = total_axis(value, axis)
    return value


def total_axis(value, axis):
    size = lax.axis_size(axis)
    bit = 1
    while bit < size:
        value = value + swap(value, axis, bit)
        bit *= 2
    return value


def slot_table(owners, capacity):
    number = owners.shape[0]
    order = jnp.arange(number, dtype=jnp.int32)
    before = (owners[:, None] == owners[None, :]) & (order[None, :] < order[:, None])
    return owners * capacity + jnp.sum(before.astype(jnp.int32), axis=1)


def rotary_tables(offsets):
    half = ROT // 2
    freqs = jnp.power(rope_base, -2.0 * jnp.arange(half, dtype=F32) / ROT)
    angle = offsets.astype(F32)[:, None, :] * freqs[None, :, None]
    cosine, sine = jnp.cos(angle), jnp.sin(angle)
    cos_t = jnp.swapaxes(cosine, 1, 2).reshape(-1, half)
    sin_t = jnp.swapaxes(sine, 1, 2).reshape(-1, half)
    rows = cos_t.shape[0]
    none = jnp.zeros((rows, half), F32)
    rest = jnp.zeros((rows, HEAD - ROT), F32)
    lanes = jnp.concatenate([cos_t, cos_t, rest + 1.0] * 2, axis=1)
    right = jnp.concatenate([sin_t, none, rest] * 2, axis=1)
    left = jnp.concatenate([none, sin_t, rest] * 2, axis=1)
    return (lanes, jnp.stack([right, left])), (cosine, sine)


FIRST = (4, 8)
SECOND = (0, 1, 2, 3)
THIRD = (5, 9, 6, 10, 7, 11)


def per_device(tokens, doc_lengths, cotangent, owners, step_count, master, moment_one, moment_two, vectors, vector_one, vector_two):
    rows, capacity, _ = master.shape
    seqs = doc_lengths.shape[0]
    length = tokens.shape[0] // seqs
    blocks = owners.shape[0]
    wide = lax.axis_size("wide")
    narrow_index = lax.axis_index("narrow")
    me = lax.axis_index("wide").astype(jnp.int32).reshape(1)
    masters, firsts, seconds = [jnp.swapaxes(m, 0, 1) for m in (master, moment_one, moment_two)]

    local = slot_table(owners, capacity) - owners * capacity
    is_mine = (owners == narrow_index).astype(jnp.int32)
    order = (FIRST, SECOND, THIRD)
    packed = pack_owned(masters, jnp.stack([local, is_mine]), order)
    shards = [line_total(p) for p in packed]
    g_first = gather_wide_steps(shards[0])
    g_second = gather_wide_steps(shards[1])
    g_third = gather_wide(shards[2])
    place = {}
    for group, ids in ((g_first, FIRST), (g_second, SECOND), (g_third, THIRD)):
        for i, b in enumerate(ids):
            place[b] = (group, i)

    h_one, h_two = layer_norms(tokens, vectors)
    ends = jnp.cumsum(doc_lengths, axis=1)
    position = jnp.arange(length, dtype=jnp.int32)
    passed = position[None, None, :] >= ends[:, :, None]
    start = jnp.sum(jnp.where(passed, doc_lengths[:, :, None], 0), axis=1)
    tables, half_tables = rotary_tables(position[None] - start)

    acts, dzs, dbs, sums = [], [], [], {}
    pair_outs, pair_plan = grad_layout(2, rows, wide)
    four_outs, four_plan = grad_layout(4, rows, wide)

    def chunk(j):
        group, i_up = place[4 + j]
        _, i_down = place[8 + j]
        act, dz, db, grads = mlp_chunk(
            me, h_two, cotangent, vectors[8 + j : 9 + j], group, i_up, i_down, pair_outs, pair_plan
        )
        acts.append(act)
        dzs.append(dz)
        dbs.append(db)
        return scatter_wide(grads)

    scattered = [((4, 8), chunk(0))]
    q, k, v, da = project(me, h_one, cotangent, vectors[4:7], tables, g_second)
    a, *dqkv, db_qkv = attention(q, k, v, da, start[:, None, :], tables, half_tables, length)
    scattered.append((SECOND, scatter_wide(attention_grads(me, h_one, a, cotangent, dqkv, four_outs, four_plan))))
    for j in range(1, SPREAD):
        scattered.append(((4 + j, 8 + j), chunk(j)))
    totals = {}
    square = jnp.zeros((), F32)
    for ids, value in scattered:
        value = line_total(value)
        square = square + jnp.sum(jnp.square(value.astype(F32)))
        for i, b in enumerate(ids):
            totals[b] = value[i]
    summed = jnp.stack([totals[b] for b in range(blocks)])

    layer_out, input_grad, sums = finish(
        me, tokens, cotangent, vectors, a, dqkv, acts, dzs, [place[b] for b in range(blocks)]
    )
    vector_term = jnp.concatenate([sums[0:4], db_qkv, sums[4:5], *dbs, sums[4:5]], axis=0)
    vector_total = total_all(vector_term)
    square_total = total_axis(jnp.broadcast_to(square, (8, 128)), "wide")[0, 0]
    grad_norm = jnp.sqrt(square_total + jnp.sum(vector_total * vector_total))
    clip = jnp.minimum(1.0, 1.0 / (grad_norm + 1e-06))
    step_float = step_count[0].astype(F32)
    first_fix = 1.0 - jnp.power(beta_first, step_float)
    second_fix = 1.0 - jnp.power(beta_second, step_float)

    slot = jnp.arange(capacity, dtype=jnp.int32)
    hit = (owners == narrow_index)[None, :] & (local[None, :] == slot[:, None])
    block_at = jnp.sum(jnp.where(hit, jnp.arange(blocks, dtype=jnp.int32)[None], 0), axis=1)
    owned = jnp.sum(hit.astype(jnp.int32), axis=1)
    scalars = jnp.stack([clip, 1.0 / first_fix, 1.0 / second_fix])
    new = update_blocks(block_at, owned, scalars, summed, masters, firsts, seconds)
    block_grads, new_master, new_first, new_second, new_copies = [jnp.swapaxes(m, 0, 1) for m in new]
    vector_grads = vector_total * clip
    new_vectors, vector_first, vector_second = adam_update(
        vector_grads, vectors, vector_one, vector_two, vector_rate, 0.0, first_fix, second_fix
    )
    return (
        layer_out,
        input_grad,
        grad_norm,
        block_grads,
        new_master,
        new_first,
        new_second,
        new_copies,
        vector_grads,
        new_vectors,
        vector_first,
        vector_second,
    )


def solution(mesh):
    tok = P(("wide", "narrow"), None)
    own = P("wide", "narrow", None)
    return jax.shard_map(
        per_device,
        mesh=mesh,
        in_specs=(tok, tok, tok, P(), P(), own, own, own, P(), P(), P()),
        out_specs=(tok, tok, P(), own, own, own, own, own, P(), P(), P(), P()),
        check_vma=False,
    )
```

```python
from functools import partial

import jax
import jax.numpy as jnp
from jax import lax
from jax.experimental import pallas as pl
from jax.experimental.pallas import tpu as pltpu
from jax.sharding import PartitionSpec as P

D = 768
HEADS = 12
HEAD = 64
ROT = 16
FF = 3072
SPREAD = FF // D

norm_epsilon = 1e-05
beta_first = 0.5
beta_second = 0.5
adam_epsilon = 1e-08
learn_rate = 0.02
vector_rate = 0.1
weight_decay = 0.1
masked_fill = -1e30
rope_base = 10000.0
LOG2E = 1.4426950408889634

BF = jnp.bfloat16
F32 = jnp.float32
MB = 1 << 20
ANY = pl.BlockSpec(memory_space=pl.ANY)
SMEM = pl.BlockSpec(memory_space=pltpu.SMEM)


def dot(a, b):
    return lax.dot_general(a, b, (((1,), (0,)), ((), ())), preferred_element_type=F32)


def dot_nt(a, b):
    return lax.dot_general(a, b, (((1,), (1,)), ((), ())), preferred_element_type=F32)


def dot_tn(a, b):
    return lax.dot_general(a, b, (((0,), (0,)), ((), ())), preferred_element_type=F32)


def params(mib, flops=0, moved=0, **more):
    return dict(
        compiler_params=pltpu.CompilerParams(vmem_limit_bytes=int(mib * MB), **more),
        cost_estimate=pl.CostEstimate(
            flops=int(flops), bytes_accessed=int(moved), transcendentals=0
        ),
    )


class Group:
    def __init__(self, arrays, plan):
        self.arrays = tuple(arrays)
        self.plan = plan


def row_of(spec, rows, me):
    if spec[0] == "at":
        return spec[1]
    return pl.multiple_of((me ^ spec[1]) * rows, rows)


def weight_copies(group, refs, i, dst, sems, me):
    copies = []
    for n, (array, lead, rows, spec) in enumerate(group.plan(i)):
        copies.append(
            pltpu.make_async_copy(
                refs[array].at[lead], dst.at[pl.ds(row_of(spec, rows, me), rows)], sems.at[n]
            )
        )
    return copies


def grad_copies(plan, refs, i, src, sems, me):
    copies = []
    for n, (array, lead, rows, spec) in enumerate(plan(i)):
        copies.append(
            pltpu.make_async_copy(
                src.at[pl.ds(row_of(spec, rows, me), rows)], refs[array].at[lead], sems.at[n]
            )
        )
    return copies


def norms_of(x):
    mean = jnp.mean(x, axis=-1, keepdims=True)
    centred = x - mean
    scale = lax.rsqrt(jnp.mean(centred * centred, axis=-1, keepdims=True) + norm_epsilon)
    return centred * scale, scale


def layer_norms(tokens, vectors, deps=()):
    rows = tokens.shape[0]
    tile = 256

    def body(x_ref, v_ref, *rest):
        one_ref, two_ref = rest[len(deps) :]
        xhat, _ = norms_of(x_ref[...].astype(F32))
        one_ref[...] = (xhat * v_ref[0:1] + v_ref[1:2]).astype(BF)
        two_ref[...] = (xhat * v_ref[2:3] + v_ref[3:4]).astype(BF)

    spec = pl.BlockSpec((tile, D), lambda t: (t, 0))
    return pl.pallas_call(
        body,
        grid=(rows // tile,),
        in_specs=[spec, pl.BlockSpec(vectors.shape, lambda t: (0, 0))] + [ANY] * len(deps),
        out_specs=[spec, spec],
        out_shape=[jax.ShapeDtypeStruct((rows, D), BF)] * 2,
        **params(16, 20 * rows * D, 6 * rows * D),
    )(tokens, vectors, *deps)


def pack_owned(masters, table, blocks, deps=()):
    rows = masters.shape[1]
    nb = len(blocks)

    def body(t_ref, m_ref, *rest):
        out, stage, sems = rest[len(deps) :]
        for i, b in enumerate(blocks):
            pltpu.make_async_copy(m_ref.at[t_ref[0, b]], stage.at[i], sems.at[i]).start()
        for i, b in enumerate(blocks):
            pltpu.make_async_copy(m_ref.at[t_ref[0, b]], stage.at[i], sems.at[i]).wait()
            out[i] = jnp.where(t_ref[1, b] > 0, stage[i], 0.0).astype(BF)

    return pl.pallas_call(
        body,
        in_specs=[SMEM, ANY] + [ANY] * len(deps),
        out_specs=pl.BlockSpec(memory_space=pltpu.VMEM),
        out_shape=jax.ShapeDtypeStruct((nb, rows, D), BF),
        scratch_shapes=[pltpu.VMEM((nb, rows, D), F32), pltpu.SemaphoreType.DMA((nb,))],
        **params(8, nb * rows * D, rows * D * 6 * nb),
    )(table, masters, *deps)


def gelu_pair(z):
    size = jnp.abs(z)
    t = pl.reciprocal(1.0 + (0.3275911 * 0.7071067811865476) * size)
    bell = jnp.exp2((-0.5 * LOG2E) * (z * z))
    poly = 0.5 * 1.061405429
    for c in (-1.453152027, 1.421413741, -0.284496736, 0.254829592):
        poly = poly * t + 0.5 * c
    tail = poly * t * bell
    cdf = jnp.where(z >= 0.0, 1.0 - tail, tail)
    return z * cdf, cdf + z * (bell * 0.3989422804014327)


def mlp_chunk(me, h_two, cot, bias, group, i_up, i_down, outs, plan, deps=()):
    rows = h_two.shape[0]
    tile = rows // 2
    na, no = len(group.arrays), len(outs)
    n_in, n_out = len(group.plan(0)), len(plan(0))

    def body(me_ref, h_ref, y_ref, b_ref, *rest):
        w_refs = rest[:na]
        rest = rest[:na] + rest[na + len(deps) :]
        act_ref, dz_ref, db_ref = rest[na : na + 3]
        o_refs = rest[na + 3 : na + 3 + no]
        w_up, w_down, acc_up, acc_down, low, in_sem, out_sem = rest[na + 3 + no :]
        step = pl.program_id(0)
        me_id = me_ref[0]

        @pl.when(step == 0)
        def _():
            ups = weight_copies(group, w_refs, i_up, w_up, in_sem.at[0], me_id)
            downs = weight_copies(group, w_refs, i_down, w_down, in_sem.at[1], me_id)
            for c in ups + downs:
                c.start()
            for c in ups + downs:
                c.wait()

        part = 256
        sums = jnp.zeros((1, D), F32)
        for p in range(tile // part):
            at = pl.ds(p * part, part)
            h = h_ref[at]
            y = y_ref[at]
            z = dot(h, w_up[...]) + b_ref[...]
            u = dot_nt(y, w_down[...])
            act, slope = gelu_pair(z)
            dz = (u * slope).astype(BF)
            act_ref[at] = act.astype(BF)
            dz_ref[at] = dz
            sums = sums + jnp.sum(dz.astype(F32), axis=0, keepdims=True)
        d_up = dot_tn(h_ref[...], dz_ref[...])
        d_down = dot_tn(act_ref[...], y_ref[...])

        @pl.when(step == 0)
        def _():
            acc_up[...] = d_up
            acc_down[...] = d_down
            db_ref[...] = sums

        @pl.when(step == 1)
        def _():
            db_ref[...] += sums
            low[0] = (acc_up[...] + d_up).astype(BF)
            low[1] = (acc_down[...] + d_down).astype(BF)
            ups = grad_copies(plan, o_refs, 0, low.at[0], out_sem.at[0], me_id)
            downs = grad_copies(plan, o_refs, 1, low.at[1], out_sem.at[1], me_id)
            for c in ups + downs:
                c.start()
            for c in ups + downs:
                c.wait()

    spec = pl.BlockSpec((tile, D), lambda t: (t, 0))
    row = pl.BlockSpec((1, D), lambda t: (0, 0))
    act, dz, db, *grads = pl.pallas_call(
        body,
        grid=(2,),
        in_specs=[SMEM, spec, spec, row] + [ANY] * (na + len(deps)),
        out_specs=[spec, spec, row] + [ANY] * no,
        out_shape=[
            jax.ShapeDtypeStruct((rows, D), BF),
            jax.ShapeDtypeStruct((rows, D), BF),
            jax.ShapeDtypeStruct((1, D), F32),
            *outs,
        ],
        scratch_shapes=[
            pltpu.VMEM((D, D), BF),
            pltpu.VMEM((D, D), BF),
            pltpu.VMEM((D, D), F32),
            pltpu.VMEM((D, D), F32),
            pltpu.VMEM((2, D, D), BF),
            pltpu.SemaphoreType.DMA((2, n_in)),
            pltpu.SemaphoreType.DMA((2, n_out)),
        ],
        **params(40, 8 * rows * D * D, 16 * rows * D),
    )(me, h_two, cot, bias, *group.arrays, *deps)
    return act, dz, db, grads


def turned(x, cosine, from_right, from_left):
    return (
        x * cosine
        + pltpu.roll(x, 128 - ROT // 2, 1) * from_right
        + pltpu.roll(x, ROT // 2, 1) * from_left
    )


def project(me, h_one, cot, bias, tables, group, deps=()):
    rows = h_one.shape[0]
    tile = 256
    na, n_in = len(group.arrays), len(group.plan(0))

    def body(me_ref, h_ref, y_ref, b_ref, c_ref, s_ref, *rest):
        w_refs = rest[:na]
        rest = rest[na + len(deps) :]
        outs = rest[:4]
        w_all, sems = rest[4:]
        step = pl.program_id(0)

        def copies(i):
            return weight_copies(group, w_refs, i, w_all.at[i], sems.at[i], me_ref[0])

        @pl.when(step == 0)
        def _():
            for i in range(4):
                for c in copies(i):
                    c.start()

        @pl.when(step == 0)
        def _():
            for i in range(4):
                for c in copies(i):
                    c.wait()

        for i in range(4):
            if i == 3:
                outs[3][...] = dot_nt(y_ref[...], w_all[3]).astype(BF)
                continue
            value = dot(h_ref[...], w_all[i]) + b_ref[i : i + 1]
            if i == 2:
                outs[2][...] = value.astype(BF)
                continue
            cosine, right, left = c_ref[...], s_ref[0], s_ref[1]
            for j in range(D // 128):
                outs[i][:, j * 128 : (j + 1) * 128] = turned(
                    value[:, j * 128 : (j + 1) * 128], cosine, -right, left
                ).astype(BF)

    spec = pl.BlockSpec((tile, D), lambda t: (t, 0))
    return pl.pallas_call(
        body,
        grid=(rows // tile,),
        in_specs=[
            SMEM,
            spec,
            spec,
            pl.BlockSpec((3, D), lambda t: (0, 0)),
            pl.BlockSpec((tile, 128), lambda t: (t, 0)),
            pl.BlockSpec((2, tile, 128), lambda t: (0, t, 0)),
        ]
        + [ANY] * (na + len(deps)),
        out_specs=[spec] * 4,
        out_shape=[jax.ShapeDtypeStruct((rows, D), BF)] * 4,
        scratch_shapes=[pltpu.VMEM((4, D, D), BF), pltpu.SemaphoreType.DMA((4, n_in))],
        **params(32, 8 * rows * D * D, 20 * rows * D),
    )(me, h_one, cot, bias, *tables, *group.arrays, *deps)


def attention(q, k, v, da, starts, tables, half_tables, length, deps=()):
    rows = q.shape[0]
    seqs = rows // length
    half = length // 2
    pair = 128

    def body(q_ref, k_ref, v_ref, d_ref, st_ref, c_ref, s_ref, hc_ref, hs_ref, *rest):
        a_ref, dq_ref, dk_ref, dv_ref, db_ref, mask = rest[len(deps) :]

        @pl.when(pl.program_id(1) == 0)
        def _():
            key = lax.broadcasted_iota(jnp.int32, (length, length), 0)
            query = lax.broadcasted_iota(jnp.int32, (length, length), 1)
            seen = (key <= query) & (key >= st_ref[0])
            mask[...] = jnp.where(seen, 0.0, masked_fill)

        q_all, k_all, v_all, d_all = q_ref[...], k_ref[...], v_ref[...], d_ref[...]
        vt, kt = v_all.T, k_all.T
        dt = d_all.T.astype(F32)
        lane = lax.broadcasted_iota(jnp.int32, (length, pair), 1)
        zero = jnp.zeros((), BF)
        dv = [jnp.zeros((half, pair), F32)] * 2
        dk = [jnp.zeros((half, pair), F32)] * 2
        jobs = []
        for h in range(2):
            mine = (lane >= h * HEAD) & (lane < (h + 1) * HEAD)
            qm = jnp.where(mine, q_all, zero)
            dm = jnp.where(mine, d_all, zero)
            for b in range(2):
                jobs.append((h, b, qm[b * half : (b + 1) * half], dm[b * half : (b + 1) * half]))
        raw, dp, prob, low, at, ds, dqt = {}, {}, {}, {}, {}, {}, {}

        def scores(i):
            h, b, qm, dm = jobs[i]
            n = half * (b + 1)
            raw[i] = dot_nt(k_all[:n], qm)
            dp[i] = dot_nt(v_all[:n], dm)

        def softmax(i):
            h, b, qm, dm = jobs[i]
            n = half * (b + 1)
            s = raw[i] * (HEAD**-0.5 * LOG2E) + mask[:n, b * half : (b + 1) * half]
            e = jnp.exp2(s - jnp.max(s, axis=0, keepdims=True))
            prob[i] = e * (1.0 / jnp.sum(e, axis=0, keepdims=True))
            low[i] = prob[i].astype(BF)
            at[i] = dot(vt[h * HEAD : (h + 1) * HEAD, :n], low[i])

        def slopes(i):
            h, b, qm, dm = jobs[i]
            dh = dt[h * HEAD : (h + 1) * HEAD, b * half : (b + 1) * half]
            total = jnp.sum(dh * at[i], axis=0, keepdims=True)
            ds[i] = (prob[i] * (dp[i] - total)).astype(BF)

        def products(i):
            h, b, qm, dm = jobs[i]
            n = half * (b + 1)
            dqt[i] = dot(kt[h * HEAD : (h + 1) * HEAD, :n], ds[i])
            more_v, more_k = dot(low[i], dm), dot(ds[i], qm)
            for c in range(b + 1):
                dv[c] = dv[c] + more_v[c * half : (c + 1) * half]
                dk[c] = dk[c] + more_k[c * half : (c + 1) * half]

        stages = (scores, softmax, slopes, products)
        for turn in range(len(jobs) + len(stages) - 1):
            for n, stage in reversed(list(enumerate(stages))):
                if 0 <= turn - n < len(jobs):
                    stage(turn - n)
        at_h, dq_h = [], []
        for h in range(2):
            at_h.append(jnp.concatenate([at[2 * h], at[2 * h + 1]], axis=1))
            dq = jnp.concatenate([dqt[2 * h], dqt[2 * h + 1]], axis=1) * HEAD**-0.5
            u, w, cos, sin = dq[0:8], dq[8:16], hc_ref[0], hs_ref[0]
            dq_h.append(jnp.concatenate([u * cos + w * sin, w * cos - u * sin, dq[16:]], axis=0))
        a_ref[...] = jnp.concatenate(at_h, axis=0).astype(BF).T
        dq = jnp.concatenate(dq_h, axis=0).astype(BF).T
        dq_ref[...] = dq
        sums = [jnp.sum(dq.astype(F32), axis=0, keepdims=True)]
        sum_k = sum_v = jnp.zeros((1, pair), F32)
        for c in range(2):
            at_k = slice(c * half, (c + 1) * half)
            back = turned(dk[c] * HEAD**-0.5, c_ref[at_k], s_ref[0, at_k], -s_ref[1, at_k]).astype(BF)
            dk_ref[at_k] = back
            sum_k = sum_k + jnp.sum(back.astype(F32), axis=0, keepdims=True)
            value = dv[c].astype(BF)
            dv_ref[at_k] = value
            sum_v = sum_v + jnp.sum(value.astype(F32), axis=0, keepdims=True)
        db_ref[0] = jnp.concatenate(sums + [sum_k, sum_v], axis=0)

    spec = pl.BlockSpec((length, pair), lambda s, h: (s, h))
    a, dq, dk, dv, db = pl.pallas_call(
        body,
        grid=(seqs, D // pair),
        in_specs=[
            spec,
            spec,
            spec,
            spec,
            pl.BlockSpec((1, 1, length), lambda s, h: (s, 0, 0)),
            pl.BlockSpec((length, 128), lambda s, h: (s, 0)),
            pl.BlockSpec((2, length, 128), lambda s, h: (0, s, 0)),
            pl.BlockSpec((1, ROT // 2, length), lambda s, h: (s, 0, 0)),
            pl.BlockSpec((1, ROT // 2, length), lambda s, h: (s, 0, 0)),
        ]
        + [ANY] * len(deps),
        out_specs=[spec, spec, spec, spec, pl.BlockSpec((1, 3, pair), lambda s, h: (s, 0, h))],
        out_shape=[jax.ShapeDtypeStruct((rows, D), BF)] * 4
        + [jax.ShapeDtypeStruct((seqs, 3, D), F32)],
        scratch_shapes=[pltpu.VMEM((length, length), F32)],
        **params(32, 20e9, 20 * rows * D),
    )(q, k, v, da, starts, *tables, *half_tables, *deps)
    return a, dq, dk, dv, jnp.sum(db, axis=0)


def attention_grads(me, h_one, a, cot, dqkv, outs, plan, deps=()):
    rows = h_one.shape[0]
    no, n_out = len(outs), len(plan(0))

    def body(me_ref, h_ref, a_ref, y_ref, dq_ref, dk_ref, dv_ref, *rest):
        rest = rest[len(deps) :]
        o_refs = rest[:no]
        low, sems = rest[no:]
        pending = []
        for i, (left, right) in enumerate(
            ((h_ref, dq_ref), (h_ref, dk_ref), (h_ref, dv_ref), (a_ref, y_ref))
        ):
            low[i] = dot_tn(left[...], right[...]).astype(BF)
            copies = grad_copies(plan, o_refs, i, low.at[i], sems.at[i], me_ref[0])
            for c in copies:
                c.start()
            pending += copies
        for c in pending:
            c.wait()

    whole = pl.BlockSpec(memory_space=pltpu.VMEM)
    return pl.pallas_call(
        body,
        in_specs=[SMEM] + [whole] * 6 + [ANY] * len(deps),
        out_specs=[ANY] * no,
        out_shape=list(outs),
        scratch_shapes=[pltpu.VMEM((4, D, D), BF), pltpu.SemaphoreType.DMA((4, n_out))],
        **params(40, 8 * rows * D * D, 12 * rows * D),
    )(me, h_one, a, cot, *dqkv, *deps)


def products(me, jobs, deps=(), starts=None, tail=None, extra=(), outs=(), mib=48):
    starts = starts or [None] * len(jobs)
    rows = jobs[0][0][0].shape[0]
    tile = 256
    groups, wanted = [], []
    for job in jobs:
        for _, place, _ in job:
            if not any(place[0] is g for g in groups):
                groups.append(place[0])
            wanted.append(place)
    first, flat = {}, []
    for group in groups:
        first[id(group)] = len(flat)
        flat += list(group.arrays)
    lefts = [left for job in jobs for left, _, _ in job]
    begun = [x for x in starts if x is not None]
    n_in = max(len(g.plan(0)) for g in groups)
    nl, ns, ne, nw, no = len(lefts), len(begun), len(extra), len(flat), len(outs)

    def body(me_ref, *rest):
        l_refs, rest = rest[:nl], rest[nl:]
        s_refs, rest = list(rest[:ns]), rest[ns:]
        e_refs, rest = rest[:ne], rest[ne:]
        w_refs, rest = rest[:nw], rest[nw + len(deps) :]
        o_refs, (w_all, sems) = rest[:no], rest[no:]
        step = pl.program_id(0)

        @pl.when(step == 0)
        def _():
            copies = []
            for n, (group, i) in enumerate(wanted):
                copies += weight_copies(group, w_refs[first[id(group)] :], i, w_all.at[n], sems.at[n], me_ref[0])
            for c in copies:
                c.start()
            for c in copies:
                c.wait()

        results, n = [], 0
        for job, begin in zip(jobs, starts):
            total = s_refs.pop(0)[...] if begin is not None else None
            for _, _, transposed in job:
                term = (dot_nt if transposed else dot)(l_refs[n][...], w_all[n])
                total = term if total is None else total + term
                n += 1
            results.append(total)
        tail(e_refs, results, o_refs, step)

    spec = pl.BlockSpec((tile, D), lambda t: (t, 0))

    def whole(x):
        return pl.BlockSpec(x.shape, lambda t: (0,) * len(x.shape))

    return pl.pallas_call(
        body,
        grid=(rows // tile,),
        in_specs=[SMEM]
        + [spec] * (nl + ns)
        + [spec if per_token else whole(x) for x, per_token in extra]
        + [ANY] * (nw + len(deps)),
        out_specs=[spec if x.shape[0] == rows else whole(x) for x in outs],
        out_shape=list(outs),
        scratch_shapes=[pltpu.VMEM((nl, D, D), BF), pltpu.SemaphoreType.DMA((nl, n_in))],
        **params(mib, 2 * nl * rows * D * D, (2 * nl + 8) * rows * D),
    )(me, *lefts, *begun, *[x for x, _ in extra], *flat, *deps)


def store_all(e_refs, results, o_refs, step):
    for ref, value in zip(o_refs, results):
        ref[...] = value


def out_tail(e_refs, results, o_refs, step):
    x_ref, v_ref = e_refs
    bias = v_ref[7:8] + v_ref[8 + SPREAD : 9 + SPREAD]
    o_refs[0][...] = (x_ref[...].astype(F32) + results[0] + bias).astype(BF)


def grad_tail(e_refs, results, o_refs, step):
    x_ref, y_ref, v_ref = e_refs
    grad_ref, sum_ref = o_refs
    d_one, d_two = results
    y = y_ref[...].astype(F32)
    xhat, scale = norms_of(x_ref[...].astype(F32))
    e = d_one * v_ref[0:1] + d_two * v_ref[2:3]
    inner = jnp.mean(e * xhat, axis=-1, keepdims=True)
    grad_ref[...] = y + (e - jnp.mean(e, axis=-1, keepdims=True) - xhat * inner) * scale
    sums = jnp.concatenate(
        [
            jnp.sum(term, axis=0, keepdims=True)
            for term in (d_one * xhat, d_one, d_two * xhat, d_two, y)
        ],
        axis=0,
    )

    @pl.when(step == 0)
    def _():
        sum_ref[...] = sums

    @pl.when(step > 0)
    def _():
        sum_ref[...] += sums


def adam_update(gradient, weight, moment, square, rate, decay, first_fix, second_fix):
    moment_new = beta_first * moment + (1.0 - beta_first) * gradient
    square_new = beta_second * square + (1.0 - beta_second) * gradient * gradient
    update = moment_new / first_fix / (jnp.sqrt(square_new / second_fix) + adam_epsilon)
    return (weight - rate * (update + decay * weight), moment_new, square_new)


def update_blocks(block_at, owned, scalars, summed, masters, firsts, seconds):
    slots, rows, _ = masters.shape

    def body(at_ref, own_ref, s_ref, g_ref, w_ref, m_ref, v_ref, g_out, w_out, m_out, v_out, c_out):
        slot = pl.program_id(0)
        keep = own_ref[slot] > 0
        clip, one_fix, two_fix = s_ref[0], s_ref[1], s_ref[2]
        gradient = g_ref[0].astype(F32) * clip
        moment = beta_first * m_ref[0] + (1.0 - beta_first) * gradient
        square = beta_second * v_ref[0] + (1.0 - beta_second) * gradient * gradient
        weight = w_ref[0]
        update = (moment * one_fix) / (jnp.sqrt(square * two_fix) + adam_epsilon)
        new = weight - learn_rate * (update + weight_decay * weight)
        new = jnp.where(keep, new, 0.0)
        g_out[0] = jnp.where(keep, gradient, 0.0)
        w_out[0] = new
        m_out[0] = jnp.where(keep, moment, 0.0)
        v_out[0] = jnp.where(keep, square, 0.0)
        c_out[0] = new.astype(BF)

    own = pl.BlockSpec((1, rows, D), lambda s, at, keep, sc: (s, 0, 0))
    return pl.pallas_call(
        body,
        grid_spec=pltpu.PrefetchScalarGridSpec(
            num_scalar_prefetch=3,
            grid=(slots,),
            in_specs=[pl.BlockSpec((1, rows, D), lambda s, at, keep, sc: (at[s], 0, 0)), own, own, own],
            out_specs=[own] * 5,
        ),
        out_shape=[jax.ShapeDtypeStruct((slots, rows, D), F32)] * 4
        + [jax.ShapeDtypeStruct((slots, rows, D), BF)],
        **params(24, 20 * slots * rows * D, 32 * slots * rows * D),
    )(block_at, owned, scalars, summed, masters, firsts, seconds)


def swap(value, axis, bit):
    size = lax.axis_size(axis)
    return lax.ppermute(value, axis, [(i, i ^ bit) for i in range(size)])


def add(a, b):
    return (a.astype(F32) + b.astype(F32)).astype(BF)


def line_one(value):
    if lax.axis_size("narrow") != 4:
        return lax.psum(value.astype(F32), "narrow").astype(BF)
    return add(value, lax.ppermute(value, "narrow", [(0, 1), (3, 2)]))


def line_two(value):
    if lax.axis_size("narrow") != 4:
        return value
    return add(value, lax.ppermute(value, "narrow", [(1, 2), (2, 1)]))


def line_three(value):
    if lax.axis_size("narrow") != 4:
        return value
    here = lax.axis_index("narrow")
    outer = lax.ppermute(value, "narrow", [(1, 0), (2, 3)])
    return jnp.where((here == 0) | (here == 3), outer, value)


CORE, SIDE, UP = 1, 2, 4
CHIPS = (0, SIDE, UP, SIDE | UP)


def gather_wide(value):
    size = lax.axis_size("wide")
    count, rows, _ = value.shape
    full = lax.all_gather(value, "wide", axis=0, tiled=False)
    if rows % 16:
        full = jnp.swapaxes(full, 0, 1).reshape(1, count, D, D)
        size, rows = 1, D
    return Group((full,), lambda i: [(0, (p, i), rows, ("at", rows * p)) for p in range(size)])


def gather_wide_steps(value):
    size = lax.axis_size("wide")
    count, rows, _ = value.shape
    if size != 8 or count % 2:
        return gather_wide(value)
    side, up = swap(value, "wide", SIDE), swap(value, "wide", UP)
    part = count // 2
    diag_a = swap(side[:part], "wide", UP)
    diag_b = swap(up[part:], "wide", SIDE)
    mine = jnp.stack([value, side, up, jnp.concatenate([diag_a, diag_b], axis=0)])
    other = swap(mine, "wide", CORE)
    masks = [(m, 0) for m in CHIPS] + [(m ^ CORE, 1) for m in CHIPS]
    return Group(
        (mine, other),
        lambda i: [(a, (n % 4, i), rows, ("xor", m)) for n, (m, a) in enumerate(masks)],
    )


def grad_layout(count, rows, size):
    if size != 8:
        return [jax.ShapeDtypeStruct((count, D, D), BF)], lambda i: [(0, (i,), D, ("at", 0))]
    part = count // 2
    shape = jax.ShapeDtypeStruct((2, 4, part, rows, D), BF)

    def plan(i):
        which, at = i // part, i % part
        order = (CHIPS, (0, UP, SIDE, SIDE | UP))[1 - which]
        keep = [(0, (which, n, at), rows, ("xor", m)) for n, m in enumerate(order)]
        give = [(1, (which, n, at), rows, ("xor", m ^ CORE)) for n, m in enumerate(order)]
        return keep + give

    return [shape] * 2, plan


class Scatter:
    def __init__(self, grads):
        self.grads = grads

    def cores(self):
        if len(self.grads) == 1:
            self.total = lax.psum_scatter(self.grads[0], "wide", scatter_dimension=1, tiled=True)
            return self.total
        keep, give = self.grads
        got = swap(give, "wide", CORE)
        self.keep = [add(keep[w, :2], got[w, :2]) for w in range(2)]
        self.give = [add(keep[w, 2:], got[w, 2:]) for w in range(2)]
        return self.give

    def first(self):
        if len(self.grads) == 1:
            return self.total
        got = [swap(self.give[0], "wide", SIDE), swap(self.give[1], "wide", UP)]
        keep = [add(self.keep[w][0], got[w][0]) for w in range(2)]
        self.give = [add(self.keep[w][1], got[w][1]) for w in range(2)]
        self.keep = keep
        return self.give

    def second(self):
        if len(self.grads) == 1:
            return self.total
        got = [swap(self.give[0], "wide", UP), swap(self.give[1], "wide", SIDE)]
        self.total = jnp.concatenate([add(self.keep[w], got[w]) for w in range(2)], axis=0)
        return self.total


def total_all(value):
    for axis in ("wide", "narrow"):
        value = total_axis(value, axis)
    return value


def total_axis(value, axis):
    size = lax.axis_size(axis)
    bit = 1
    while bit < size:
        value = value + swap(value, axis, bit)
        bit *= 2
    return value


def slot_table(owners, capacity):
    number = owners.shape[0]
    order = jnp.arange(number, dtype=jnp.int32)
    before = (owners[:, None] == owners[None, :]) & (order[None, :] < order[:, None])
    return owners * capacity + jnp.sum(before.astype(jnp.int32), axis=1)


def rotary_tables(offsets):
    half = ROT // 2
    freqs = jnp.power(rope_base, -2.0 * jnp.arange(half, dtype=F32) / ROT)
    angle = offsets.astype(F32)[:, None, :] * freqs[None, :, None]
    cosine, sine = jnp.cos(angle), jnp.sin(angle)
    cos_t = jnp.swapaxes(cosine, 1, 2).reshape(-1, half)
    sin_t = jnp.swapaxes(sine, 1, 2).reshape(-1, half)
    rows = cos_t.shape[0]
    none = jnp.zeros((rows, half), F32)
    rest = jnp.zeros((rows, HEAD - ROT), F32)
    lanes = jnp.concatenate([cos_t, cos_t, rest + 1.0] * 2, axis=1)
    right = jnp.concatenate([sin_t, none, rest] * 2, axis=1)
    left = jnp.concatenate([none, sin_t, rest] * 2, axis=1)
    return (lanes, jnp.stack([right, left])), (cosine, sine)


def per_device(tokens, doc_lengths, cotangent, owners, step_count, master, moment_one, moment_two, vectors, vector_one, vector_two):
    rows, capacity, _ = master.shape
    seqs = doc_lengths.shape[0]
    length = tokens.shape[0] // seqs
    blocks = owners.shape[0]
    wide = lax.axis_size("wide")
    narrow_index = lax.axis_index("narrow")
    me = lax.axis_index("wide").astype(jnp.int32).reshape(1)
    masters, firsts, seconds = [jnp.swapaxes(m, 0, 1) for m in (master, moment_one, moment_two)]

    local = slot_table(owners, capacity) - owners * capacity
    is_mine = (owners == narrow_index).astype(jnp.int32)
    table = jnp.stack([local, is_mine])
    ids_0, ids_1, ids_s, ids_t = (4, 8), (5, 9), (0, 1, 2, 3), (6, 10, 7, 11)
    one_0 = line_one(pack_owned(masters, table, ids_0))
    one_1 = line_one(pack_owned(masters, table, ids_1, deps=[one_0]))
    two_0 = line_two(one_0)
    one_s = line_one(pack_owned(masters, table, ids_s, deps=[one_1]))
    shard_0 = line_three(two_0)
    two_1 = line_two(one_1)
    pack_t = pack_owned(masters, table, ids_t, deps=[one_s])
    shard_1 = line_three(two_1)
    group_0 = gather_wide_steps(shard_0)
    group_1 = gather_wide_steps(shard_1)
    two_s = line_two(one_s)
    one_t = line_one(pack_t)
    shard_s = line_three(two_s)
    group_s = gather_wide_steps(shard_s)
    two_t = line_two(one_t)
    shard_t = line_three(two_t)
    group_t = gather_wide(shard_t)
    place = {}
    for group, ids in ((group_0, ids_0), (group_1, ids_1), (group_s, ids_s), (group_t, ids_t)):
        for i, b in enumerate(ids):
            place[b] = (group, i)

    ends = jnp.cumsum(doc_lengths, axis=1)
    position = jnp.arange(length, dtype=jnp.int32)
    passed = position[None, None, :] >= ends[:, :, None]
    start = jnp.sum(jnp.where(passed, doc_lengths[:, :, None], 0), axis=1)
    tables, half_tables = rotary_tables(position[None] - start)
    h_one, h_two = layer_norms(tokens, vectors, deps=[*tables, *half_tables])

    acts, dzs, dbs = [], [], []
    pair_outs, pair_plan = grad_layout(2, rows, wide)
    four_outs, four_plan = grad_layout(4, rows, wide)

    def chunk(j, deps):
        group, i_up = place[4 + j]
        _, i_down = place[8 + j]
        act, dz, db, grads = mlp_chunk(
            me, h_two, cotangent, vectors[8 + j : 9 + j], group, i_up, i_down, pair_outs, pair_plan, deps
        )
        acts.append(act)
        dzs.append(dz)
        dbs.append(db)
        return Scatter(grads)

    full = jax.ShapeDtypeStruct(tokens.shape, F32)

    rs_0 = chunk(0, [shard_1, one_s, pack_t])
    rs_1 = chunk(1, [two_s, one_t, *rs_0.cores()])
    early = products(
        me,
        [[(acts[j], place[8 + j], False) for j in range(2)], [(dzs[j], place[4 + j], True) for j in range(2)]],
        deps=[shard_s, *rs_0.first(), *rs_1.cores()],
        tail=store_all,
        outs=[full, full],
    )
    q, k, v, da = project(
        me, h_one, cotangent, vectors[4:7], tables, group_s, deps=[two_t, rs_0.second(), *rs_1.first(), early[0]]
    )
    front = jnp.concatenate([rs_0.total, rs_1.second()], axis=0)
    a, *dqkv, db_qkv = attention(
        q, k, v, da, start[:, None, :], tables, half_tables, length, deps=[shard_t, front]
    )
    front = line_one(front)
    rs_s = Scatter(attention_grads(me, h_one, a, cotangent, dqkv, four_outs, four_plan, deps=[front]))
    front = line_two(front)
    rs_2 = chunk(2, [front, *rs_s.cores()])
    front = line_three(front)
    rs_3 = chunk(3, [front, *rs_s.first(), *rs_2.cores()])
    mid = rs_s.second()
    (layer_out,) = products(
        me,
        [[(a, place[3], False)] + [(acts[j], place[8 + j], False) for j in range(2, SPREAD)]],
        deps=[mid, *rs_2.first(), *rs_3.cores()],
        starts=[early[0]],
        tail=out_tail,
        extra=[(tokens, True), (vectors, False)],
        outs=[jax.ShapeDtypeStruct(tokens.shape, BF)],
    )
    mid = line_one(mid)
    input_grad, sums = products(
        me,
        [
            [(dqkv[n], place[n], True) for n in range(3)],
            [(dzs[j], place[4 + j], True) for j in range(2, SPREAD)],
        ],
        deps=[mid, rs_2.second(), *rs_3.first(), layer_out],
        starts=[None, early[1]],
        tail=grad_tail,
        extra=[(tokens, True), (cotangent, True), (vectors, False)],
        outs=[full, jax.ShapeDtypeStruct((5, D), F32)],
    )
    mid = line_three(line_two(mid))
    last = jnp.concatenate([rs_2.total, rs_3.second()], axis=0)
    last = line_three(line_two(line_one(last)))
    square = jnp.zeros((), F32)
    totals = {}
    for ids, value in (((4, 8, 5, 9), front), (ids_s, mid), (ids_t, last)):
        square = square + jnp.sum(jnp.square(value.astype(F32)))
        for i, b in enumerate(ids):
            totals[b] = value[i]
    summed = jnp.stack([totals[b] for b in range(blocks)])

    vector_term = jnp.concatenate([sums[0:4], db_qkv, sums[4:5], *dbs, sums[4:5]], axis=0)
    vector_total = total_all(vector_term)
    square_total = total_axis(jnp.broadcast_to(square, (8, 128)), "wide")[0, 0]
    grad_norm = jnp.sqrt(square_total + jnp.sum(vector_total * vector_total))
    clip = jnp.minimum(1.0, 1.0 / (grad_norm + 1e-06))
    step_float = step_count[0].astype(F32)
    first_fix = 1.0 - jnp.power(beta_first, step_float)
    second_fix = 1.0 - jnp.power(beta_second, step_float)

    slot = jnp.arange(capacity, dtype=jnp.int32)
    hit = (owners == narrow_index)[None, :] & (local[None, :] == slot[:, None])
    block_at = jnp.sum(jnp.where(hit, jnp.arange(blocks, dtype=jnp.int32)[None], 0), axis=1)
    owned = jnp.sum(hit.astype(jnp.int32), axis=1)
    scalars = jnp.stack([clip, 1.0 / first_fix, 1.0 / second_fix])
    new = update_blocks(block_at, owned, scalars, summed, masters, firsts, seconds)
    block_grads, new_master, new_first, new_second, new_copies = [jnp.swapaxes(m, 0, 1) for m in new]
    vector_grads = vector_total * clip
    new_vectors, vector_first, vector_second = adam_update(
        vector_grads, vectors, vector_one, vector_two, vector_rate, 0.0, first_fix, second_fix
    )
    return (
        layer_out,
        input_grad,
        grad_norm,
        block_grads,
        new_master,
        new_first,
        new_second,
        new_copies,
        vector_grads,
        new_vectors,
        vector_first,
        vector_second,
    )


def solution(mesh):
    tok = P(("wide", "narrow"), None)
    own = P("wide", "narrow", None)
    return jax.shard_map(
        per_device,
        mesh=mesh,
        in_specs=(tok, tok, tok, P(), P(), own, own, own, P(), P(), P()),
        out_specs=(tok, tok, P(), own, own, own, own, own, P(), P(), P(), P()),
        check_vma=False,
    )
```

```python
from functools import partial

import jax
import jax.numpy as jnp
from jax import lax
from jax.experimental import pallas as pl
from jax.experimental.pallas import tpu as pltpu
from jax.sharding import PartitionSpec as P

D = 768
HEADS = 12
HEAD = 64
ROT = 16
FF = 3072
SPREAD = FF // D

norm_epsilon = 1e-05
beta_first = 0.5
beta_second = 0.5
adam_epsilon = 1e-08
learn_rate = 0.02
vector_rate = 0.1
weight_decay = 0.1
masked_fill = -1e30
rope_base = 10000.0
LOG2E = 1.4426950408889634

BF = jnp.bfloat16
F32 = jnp.float32
MB = 1 << 20
ANY = pl.BlockSpec(memory_space=pl.ANY)
HBM = pl.BlockSpec(memory_space=pltpu.HBM)
SMEM = pl.BlockSpec(memory_space=pltpu.SMEM)
VMEM = pl.BlockSpec(memory_space=pltpu.VMEM)


def dot(a, b):
    return lax.dot_general(a, b, (((1,), (0,)), ((), ())), preferred_element_type=F32)


def dot_nt(a, b):
    return lax.dot_general(a, b, (((1,), (1,)), ((), ())), preferred_element_type=F32)


def dot_tn(a, b):
    return lax.dot_general(a, b, (((0,), (0,)), ((), ())), preferred_element_type=F32)


def params(mib, flops=0, moved=0, **more):
    return dict(
        compiler_params=pltpu.CompilerParams(vmem_limit_bytes=int(mib * MB), **more),
        cost_estimate=pl.CostEstimate(
            flops=int(flops), bytes_accessed=int(moved), transcendentals=0
        ),
    )


class Order:
    deps = ()


def ordered(body, *, in_specs, out_specs, out_shape, scratch_shapes=(), **more):
    single = not isinstance(out_shape, (list, tuple))
    specs, shapes = ([out_specs], [out_shape]) if single else (list(out_specs), list(out_shape))
    deps, n_in, n_out = Order.deps, len(in_specs), len(shapes)

    def wrapped(*refs):
        rest = refs[n_in + len(deps) :]
        body(*refs[:n_in], *rest[:n_out], *rest[n_out + 1 :])
        rest[n_out][...] = jnp.zeros((8, 128), F32)

    mark = VMEM if more.get("grid") is None else pl.BlockSpec((8, 128), lambda *at: (0, 0))
    call = pl.pallas_call(
        wrapped,
        in_specs=[*in_specs, *[ANY] * len(deps)],
        out_specs=[*specs, mark],
        out_shape=[*shapes, jax.ShapeDtypeStruct((8, 128), F32)],
        scratch_shapes=list(scratch_shapes),
        **more,
    )

    def run(*args):
        *out, token = call(*args, *deps)
        Order.deps = (token,)
        return out[0] if single else out

    return run


class Group:
    def __init__(self, arrays, pieces):
        self.arrays = tuple(arrays)
        self.pieces = tuple(pieces)


def row_of(spec, rows, me):
    if spec[0] == "at":
        return spec[1]
    return pl.multiple_of((me ^ spec[1]) * rows, rows)


def weight_copies(group, refs, first, count, dst, sems, me):
    copies = []
    for n, (array, lead, rows, spec) in enumerate(group.pieces):
        src = refs[array].at[lead + (pl.ds(first, count),)]
        copies.append(
            pltpu.make_async_copy(src, dst.at[:, pl.ds(row_of(spec, rows, me), rows)], sems.at[n])
        )
    return copies


def grad_copies(plan, refs, first, count, src, sems, me):
    blocks = pl.ds(first, count)
    return [
        pltpu.make_async_copy(
            src.at[blocks, pl.ds(row_of(spec, rows, me), rows)], refs[array].at[lead + (blocks,)], sems.at[n]
        )
        for n, (array, lead, rows, spec) in enumerate(plan)
    ]


def norms_of(x):
    mean = jnp.mean(x, axis=-1, keepdims=True)
    centred = x - mean
    scale = lax.rsqrt(jnp.mean(centred * centred, axis=-1, keepdims=True) + norm_epsilon)
    return centred * scale, scale


def layer_norms(tokens, vectors, deps=()):
    rows = tokens.shape[0]
    tile = 256

    def body(x_ref, v_ref, *rest):
        one_ref, two_ref = rest[len(deps) :]
        xhat, _ = norms_of(x_ref[...].astype(F32))
        one_ref[...] = (xhat * v_ref[0:1] + v_ref[1:2]).astype(BF)
        two_ref[...] = (xhat * v_ref[2:3] + v_ref[3:4]).astype(BF)

    spec = pl.BlockSpec((tile, D), lambda t: (t, 0))
    return ordered(
        body,
        grid=(rows // tile,),
        in_specs=[spec, pl.BlockSpec(vectors.shape, lambda t: (0, 0))] + [ANY] * len(deps),
        out_specs=[spec, spec],
        out_shape=[jax.ShapeDtypeStruct((rows, D), BF)] * 2,
        **params(16, 20 * rows * D, 6 * rows * D),
    )(tokens, vectors, *deps)


def pack_owned(masters, table, blocks, deps=()):
    rows = masters.shape[1]
    nb = len(blocks)

    def body(t_ref, m_ref, *rest):
        out, stage, sems = rest[len(deps) :]
        for i, b in enumerate(blocks):
            pltpu.make_async_copy(m_ref.at[t_ref[0, b]], stage.at[i], sems.at[i]).start()
        for i, b in enumerate(blocks):
            pltpu.make_async_copy(m_ref.at[t_ref[0, b]], stage.at[i], sems.at[i]).wait()
            out[i] = jnp.where(t_ref[1, b] > 0, stage[i], 0.0).astype(BF)

    return ordered(
        body,
        in_specs=[SMEM, ANY] + [ANY] * len(deps),
        out_specs=pl.BlockSpec(memory_space=pltpu.VMEM),
        out_shape=jax.ShapeDtypeStruct((nb, rows, D), BF),
        scratch_shapes=[pltpu.VMEM((nb, rows, D), F32), pltpu.SemaphoreType.DMA((nb,))],
        **params(16, 1, 1),
    )(table, masters, *deps)


def gelu_pair(z):
    size = jnp.abs(z)
    t = pl.reciprocal(1.0 + (0.3275911 * 0.7071067811865476) * size)
    bell = jnp.exp2((-0.5 * LOG2E) * (z * z))
    poly = 0.5 * 1.061405429
    for c in (-1.453152027, 1.421413741, -0.284496736, 0.254829592):
        poly = poly * t + 0.5 * c
    tail = poly * t * bell
    cdf = jnp.where(z >= 0.0, 1.0 - tail, tail)
    return z * cdf, cdf + z * (bell * 0.3989422804014327)


def mlp_chunk(me, h_two, cot, bias, group, first, outs, plan, deps=()):
    rows = h_two.shape[0]
    part = 256
    parts = rows // part
    na, no, nd = len(group.arrays), len(outs), len(deps)
    n_in, n_out = len(group.pieces), len(plan)

    def body(me_ref, h_ref, y_ref, b_ref, *rest):
        w_refs, rest = rest[:na], rest[na + nd :]
        act_ref, dz_ref, db_ref = rest[:3]
        o_refs = rest[3 : 3 + no]
        h, y, w, act, dz, low, in_sem, t_sem, out_sem = rest[3 + no :]
        me_id = me_ref[0]
        at = [pl.ds(p * part, part) for p in range(parts)]
        loads = weight_copies(group, w_refs, first, 2, w, in_sem, me_id)
        tokens = [
            [
                pltpu.make_async_copy(src.at[at[p]], dst.at[at[p]], t_sem.at[n, p])
                for n, (src, dst) in enumerate(((h_ref, h), (y_ref, y)))
            ]
            for p in range(parts)
        ]
        for c in loads:
            c.start()
        for pair in tokens:
            for c in pair:
                c.start()
        for c in loads:
            c.wait()
        for pair in tokens:
            for c in pair:
                c.wait()
        stores, z, u, sums = [], {}, {}, []

        def into(p):
            z[p] = dot(h[at[p]], w[0]) + b_ref[...]
            u[p] = dot_nt(y[at[p]], w[1])

        def slopes(p):
            value, slope = gelu_pair(z[p])
            act[at[p]] = value.astype(BF)
            low_dz = (u[p] * slope).astype(BF)
            dz[at[p]] = low_dz
            sums.append(jnp.sum(low_dz.astype(F32), axis=0, keepdims=True))
            for n, (src, dst) in enumerate(((act, act_ref), (dz, dz_ref))):
                stores.append(pltpu.make_async_copy(src.at[at[p]], dst.at[at[p]], t_sem.at[2 + n, p]))
                stores[-1].start()

        for turn in range(parts + 1):
            if turn < parts:
                into(turn)
            if turn:
                slopes(turn - 1)
        for i, (left, right) in enumerate(((h, dz), (act, y))):
            low[i] = dot_tn(left[...], right[...]).astype(BF)
        for c in grad_copies(plan, o_refs, 0, 2, low, out_sem, me_id):
            c.start()
            stores.append(c)
        db_ref[...] = sum(sums[1:], sums[0])
        for c in stores:
            c.wait()

    act, dz, db, *grads = ordered(
        body,
        in_specs=[SMEM, HBM, HBM, VMEM] + [HBM] * na + [ANY] * nd,
        out_specs=[HBM, HBM, VMEM] + [HBM] * no,
        out_shape=[
            jax.ShapeDtypeStruct((rows, D), BF),
            jax.ShapeDtypeStruct((rows, D), BF),
            jax.ShapeDtypeStruct((1, D), F32),
            *outs,
        ],
        scratch_shapes=[
            pltpu.VMEM((rows, D), BF),
            pltpu.VMEM((rows, D), BF),
            pltpu.VMEM((2, D, D), BF),
            pltpu.VMEM((rows, D), BF),
            pltpu.VMEM((rows, D), BF),
            pltpu.VMEM((2, D, D), BF),
            pltpu.SemaphoreType.DMA((n_in,)),
            pltpu.SemaphoreType.DMA((4, parts)),
            pltpu.SemaphoreType.DMA((n_out,)),
        ],
        **params(60, 8 * rows * D * D, 16 * rows * D),
    )(me, h_two, cot, bias, *group.arrays, *deps)
    return act, dz, db, grads


def turned(x, cosine, from_right, from_left):
    return (
        x * cosine
        + pltpu.roll(x, 128 - ROT // 2, 1) * from_right
        + pltpu.roll(x, ROT // 2, 1) * from_left
    )


def lanes_of(cosine, sine):
    half = ROT // 2
    lane = lax.broadcasted_iota(jnp.int32, (half, 128), 1) % HEAD
    row = lax.broadcasted_iota(jnp.int32, (half, 128), 0)
    one, two = (lane == row).astype(F32), (lane == row + half).astype(F32)

    def spread(values, mask):
        return lax.dot_general(
            values, mask, (((0,), (0,)), ((), ())), precision=lax.Precision.HIGHEST, preferred_element_type=F32
        )

    still = (lax.broadcasted_iota(jnp.int32, (1, 128), 1) % HEAD >= ROT).astype(F32)
    return spread(cosine, one + two) + still, spread(sine, one), spread(sine, two)


def project(me, h_one, cot, bias, cosine, sine, group, deps=()):
    rows = h_one.shape[0]
    tile = 256
    per = cosine.shape[2] // tile
    na, n_in = len(group.arrays), len(group.pieces)

    def body(me_ref, h_ref, y_ref, b_ref, c_ref, s_ref, *rest):
        w_refs, rest = rest[:na], rest[na + len(deps) :]
        outs = rest[:4]
        w_all, sems = rest[4:]
        step = pl.program_id(0)

        @pl.when(step == 0)
        def _():
            copies = weight_copies(group, w_refs, 0, 4, w_all, sems, me_ref[0])
            for c in copies:
                c.start()
            for c in copies:
                c.wait()

        cos_l, right, left = lanes_of(c_ref[0], s_ref[0])
        outs[3][...] = dot_nt(y_ref[...], w_all[3]).astype(BF)
        for i in range(3):
            value = dot(h_ref[...], w_all[i]) + b_ref[i : i + 1]
            if i == 2:
                outs[2][...] = value.astype(BF)
                continue
            for j in range(D // 128):
                outs[i][:, j * 128 : (j + 1) * 128] = turned(
                    value[:, j * 128 : (j + 1) * 128], cos_l, -right, left
                ).astype(BF)

    spec = pl.BlockSpec((tile, D), lambda t: (t, 0))
    table = pl.BlockSpec((1, ROT // 2, tile), lambda t: (t // per, 0, t % per))
    return ordered(
        body,
        grid=(rows // tile,),
        in_specs=[SMEM, spec, spec, pl.BlockSpec((3, D), lambda t: (0, 0)), table, table]
        + [HBM] * na
        + [ANY] * len(deps),
        out_specs=[spec] * 4,
        out_shape=[jax.ShapeDtypeStruct((rows, D), BF)] * 4,
        scratch_shapes=[pltpu.VMEM((4, D, D), BF), pltpu.SemaphoreType.DMA((n_in,))],
        **params(60, 8 * rows * D * D, 20 * rows * D),
    )(me, h_one, cot, bias, cosine, sine, *group.arrays, *deps)


def attention(q, k, v, da, starts, cosine, sine, length, which, into=(), deps=()):
    rows = q.shape[0]
    seqs = len(which)
    half = length // 2
    pair = 128

    def body(q_ref, k_ref, v_ref, d_ref, st_ref, hc_ref, hs_ref, *rest):
        a_ref, dq_ref, dk_ref, dv_ref, db_ref, mask, wheel = rest[len(into) + len(deps) :]

        @pl.when(pl.program_id(1) == 0)
        def _():
            key = lax.broadcasted_iota(jnp.int32, (length, length), 0)
            query = lax.broadcasted_iota(jnp.int32, (length, length), 1)
            seen = (key <= query) & (key >= st_ref[0])
            mask[...] = jnp.where(seen, 0.0, masked_fill)
            wheel[0], wheel[1], wheel[2] = lanes_of(hc_ref[0], hs_ref[0])

        q_all, k_all, v_all, d_all = q_ref[...], k_ref[...], v_ref[...], d_ref[...]
        vt, kt = v_all.T, k_all.T
        dt = d_all.T.astype(F32)
        lane = lax.broadcasted_iota(jnp.int32, (length, pair), 1)
        zero = jnp.zeros((), BF)
        dv = [jnp.zeros((half, pair), F32)] * 2
        dk = [jnp.zeros((half, pair), F32)] * 2
        jobs = []
        for h in range(2):
            mine = (lane >= h * HEAD) & (lane < (h + 1) * HEAD)
            qm = jnp.where(mine, q_all, zero)
            dm = jnp.where(mine, d_all, zero)
            for b in range(2):
                jobs.append((h, b, qm[b * half : (b + 1) * half], dm[b * half : (b + 1) * half]))
        raw, dp, prob, low, at, ds, dqt = {}, {}, {}, {}, {}, {}, {}

        def scores(i):
            h, b, qm, dm = jobs[i]
            n = half * (b + 1)
            raw[i] = dot_nt(k_all[:n], qm)
            dp[i] = dot_nt(v_all[:n], dm)

        def softmax(i):
            h, b, qm, dm = jobs[i]
            n = half * (b + 1)
            s = raw[i] * (HEAD**-0.5 * LOG2E) + mask[:n, b * half : (b + 1) * half]
            e = jnp.exp2(s - jnp.max(s, axis=0, keepdims=True))
            prob[i] = e * (1.0 / jnp.sum(e, axis=0, keepdims=True))
            low[i] = prob[i].astype(BF)
            at[i] = dot(vt[h * HEAD : (h + 1) * HEAD, :n], low[i])

        def slopes(i):
            h, b, qm, dm = jobs[i]
            dh = dt[h * HEAD : (h + 1) * HEAD, b * half : (b + 1) * half]
            total = jnp.sum(dh * at[i], axis=0, keepdims=True)
            ds[i] = (prob[i] * (dp[i] - total)).astype(BF)

        def grads(i):
            h, b, qm, dm = jobs[i]
            n = half * (b + 1)
            dqt[i] = dot(kt[h * HEAD : (h + 1) * HEAD, :n], ds[i])
            more_v, more_k = dot(low[i], dm), dot(ds[i], qm)
            for c in range(b + 1):
                dv[c] = dv[c] + more_v[c * half : (c + 1) * half]
                dk[c] = dk[c] + more_k[c * half : (c + 1) * half]

        stages = (scores, softmax, slopes, grads)
        for turn in range(len(jobs) + len(stages) - 1):
            for n, stage in reversed(list(enumerate(stages))):
                if 0 <= turn - n < len(jobs):
                    stage(turn - n)
        at_h, dq_h = [], []
        for h in range(2):
            at_h.append(jnp.concatenate([at[2 * h], at[2 * h + 1]], axis=1))
            dq = jnp.concatenate([dqt[2 * h], dqt[2 * h + 1]], axis=1) * HEAD**-0.5
            u, w, cos, sin = dq[0:8], dq[8:16], hc_ref[0], hs_ref[0]
            dq_h.append(jnp.concatenate([u * cos + w * sin, w * cos - u * sin, dq[16:]], axis=0))
        a_ref[...] = jnp.concatenate(at_h, axis=0).astype(BF).T
        dq = jnp.concatenate(dq_h, axis=0).astype(BF).T
        dq_ref[...] = dq
        sums = [jnp.sum(dq.astype(F32), axis=0, keepdims=True)]
        sum_k = sum_v = jnp.zeros((1, pair), F32)
        for c in range(2):
            at_k = slice(c * half, (c + 1) * half)
            back = turned(dk[c] * HEAD**-0.5, wheel[0, at_k], wheel[1, at_k], -wheel[2, at_k]).astype(BF)
            dk_ref[at_k] = back
            sum_k = sum_k + jnp.sum(back.astype(F32), axis=0, keepdims=True)
            value = dv[c].astype(BF)
            dv_ref[at_k] = value
            sum_v = sum_v + jnp.sum(value.astype(F32), axis=0, keepdims=True)
        db_ref[0] = jnp.concatenate(sums + [sum_k, sum_v], axis=0)

    base = which[0]
    spec = pl.BlockSpec((length, pair), lambda s, h: (s + base, h))
    table = pl.BlockSpec((1, ROT // 2, length), lambda s, h: (s + base, 0, 0))
    a, dq, dk, dv, db = ordered(
        body,
        grid=(seqs, D // pair),
        in_specs=[spec] * 4
        + [pl.BlockSpec((1, 1, length), lambda s, h: (s + base, 0, 0)), table, table]
        + [ANY] * (len(into) + len(deps)),
        out_specs=[spec, spec, spec, spec, pl.BlockSpec((1, 3, pair), lambda s, h: (s, 0, h))],
        out_shape=[jax.ShapeDtypeStruct((rows, D), BF)] * 4
        + [jax.ShapeDtypeStruct((seqs, 3, D), F32)],
        scratch_shapes=[pltpu.VMEM((length, length), F32), pltpu.VMEM((3, length, 128), F32)],
        input_output_aliases={7 + n: n for n in range(len(into))},
        **params(60, 10e9 * seqs, 20 * rows * D),
    )(q, k, v, da, starts, cosine, sine, *into, *deps)
    return a, dq, dk, dv, jnp.sum(db, axis=0)


def attention_grads(me, h_one, a, cot, dqkv, outs, plan, deps=()):
    rows = h_one.shape[0]
    no, n_out = len(outs), len(plan)

    def body(me_ref, h_ref, a_ref, y_ref, dq_ref, dk_ref, dv_ref, *rest):
        rest = rest[len(deps) :]
        o_refs = rest[:no]
        low, sems = rest[no:]
        pending = []
        for i, (left, right) in enumerate(
            ((h_ref, dq_ref), (h_ref, dk_ref), (h_ref, dv_ref), (a_ref, y_ref))
        ):
            low[i] = dot_tn(left[...], right[...]).astype(BF)
            if i % 2:
                copies = grad_copies(plan, o_refs, i - 1, 2, low, sems.at[i // 2], me_ref[0])
                for c in copies:
                    c.start()
                pending += copies
        for c in pending:
            c.wait()

    whole = pl.BlockSpec(memory_space=pltpu.VMEM)
    return ordered(
        body,
        in_specs=[SMEM] + [whole] * 6 + [ANY] * len(deps),
        out_specs=[HBM] * no,
        out_shape=list(outs),
        scratch_shapes=[pltpu.VMEM((4, D, D), BF), pltpu.SemaphoreType.DMA((2, n_out))],
        **params(60, 8 * rows * D * D, 12 * rows * D),
    )(me, h_one, a, cot, *dqkv, *deps)


def products(me, jobs, tail, outs, starts=None, extra=(), deps=(), mib=60):
    starts = starts or [None] * len(jobs)
    rows = jobs[0][0][0].shape[0]
    tile = 256
    groups, used = [], {}
    for job in jobs:
        for _, (group, i), _ in job:
            if id(group) not in used:
                groups.append(group)
                used[id(group)] = []
            used[id(group)].append(i)
    first, flat, runs, slot, at = {}, [], [], {}, 0
    for group in groups:
        first[id(group)] = len(flat)
        flat += list(group.arrays)
        low, high = min(used[id(group)]), max(used[id(group)])
        runs.append((group, low, high - low + 1, at))
        for i in range(low, high + 1):
            slot[id(group), i] = at
            at += 1
    lefts = [left for job in jobs for left, _, _ in job]
    begun = [x for x in starts if x is not None]
    n_in = max(len(g.pieces) for g in groups)
    nl, ns, ne, nw, no = len(lefts), len(begun), len(extra), len(flat), len(outs)

    def body(me_ref, *rest):
        l_refs, rest = rest[:nl], rest[nl:]
        s_refs, rest = list(rest[:ns]), rest[ns:]
        e_refs, rest = rest[:ne], rest[ne:]
        w_refs, rest = rest[:nw], rest[nw + len(deps) :]
        o_refs, (w_all, sems) = rest[:no], rest[no:]
        step = pl.program_id(0)

        @pl.when(step == 0)
        def _():
            copies = []
            for n, (group, low, count, to) in enumerate(runs):
                refs = w_refs[first[id(group)] :]
                copies += weight_copies(
                    group, refs, low, count, w_all.at[pl.ds(to, count)], sems.at[n], me_ref[0]
                )
            for c in copies:
                c.start()
            for c in copies:
                c.wait()

        results, n = [], 0
        for job, begin in zip(jobs, starts):
            total = s_refs.pop(0)[...] if begin is not None else None
            for _, (group, i), transposed in job:
                term = (dot_nt if transposed else dot)(l_refs[n][...], w_all[slot[id(group), i]])
                total = term if total is None else total + term
                n += 1
            results.append(total)
        tail(e_refs, results, o_refs, step)

    spec = pl.BlockSpec((tile, D), lambda t: (t, 0))

    def whole(x):
        return pl.BlockSpec(x.shape, lambda t: (0,) * len(x.shape))

    return ordered(
        body,
        grid=(rows // tile,),
        in_specs=[SMEM]
        + [spec] * (nl + ns)
        + [spec if per_token else whole(x) for x, per_token in extra]
        + [HBM] * nw
        + [ANY] * len(deps),
        out_specs=[spec if x.shape[0] == rows else whole(x) for x in outs],
        out_shape=list(outs),
        scratch_shapes=[pltpu.VMEM((at, D, D), BF), pltpu.SemaphoreType.DMA((len(runs), n_in))],
        **params(mib, 2 * nl * rows * D * D, (2 * nl + 8) * rows * D),
    )(me, *lefts, *begun, *[x for x, _ in extra], *flat, *deps)


def store_all(e_refs, results, o_refs, step):
    for ref, value in zip(o_refs, results):
        ref[...] = value


def add_rows(ref, terms, step):
    sums = jnp.concatenate([jnp.sum(term, axis=0, keepdims=True) for term in terms], axis=0)

    @pl.when(step == 0)
    def _():
        ref[...] = sums

    @pl.when(step > 0)
    def _():
        ref[...] += sums


def middle_tail(e_refs, results, o_refs, step):
    x_ref, y_ref, v_ref = e_refs
    out_ref, e_ref, sum_ref = o_refs
    out, d_one, d_two = results
    x = x_ref[...].astype(F32)
    out_ref[...] = out + x + (v_ref[7:8] + v_ref[8 + SPREAD : 9 + SPREAD])
    xhat, _ = norms_of(x)
    e_ref[...] = d_one * v_ref[0:1] + d_two * v_ref[2:3]
    add_rows(sum_ref, (d_one * xhat, d_one, d_two * xhat, d_two, y_ref[...].astype(F32)), step)


def last_tail(e_refs, results, o_refs, step):
    x_ref, y_ref, v_ref, e_ref = e_refs
    out_ref, grad_ref, sum_ref = o_refs
    out, d_two = results
    out_ref[...] = out.astype(BF)
    xhat, scale = norms_of(x_ref[...].astype(F32))
    e = e_ref[...] + d_two * v_ref[2:3]
    inner = jnp.mean(e * xhat, axis=-1, keepdims=True)
    y = y_ref[...].astype(F32)
    grad_ref[...] = y + (e - jnp.mean(e, axis=-1, keepdims=True) - xhat * inner) * scale
    add_rows(sum_ref, (d_two * xhat, d_two), step)


def adam(gradient, weight, moment, square, rate, decay, one_fix, two_fix):
    moment_new = beta_first * moment + (1.0 - beta_first) * gradient
    square_new = beta_second * square + (1.0 - beta_second) * gradient * gradient
    update = (moment_new * one_fix) / (jnp.sqrt(square_new * two_fix) + adam_epsilon)
    return weight - rate * (update + decay * weight), moment_new, square_new


def update_all(source, fixes, squares, vector_total, vector_state, summed, masters, firsts, seconds):
    slots, rows, _ = masters.shape
    ng = len(summed)

    def body(src_ref, fix_ref, q_ref, t_ref, vw_ref, vm_ref, vv_ref, *rest):
        g_refs, (w_ref, m_ref, v_ref) = rest[:ng], rest[ng : ng + 3]
        norm_out, tg_out, tw_out, tm_out, tv_out, g_out, w_out, m_out, v_out, c_out, clip_ref = rest[ng + 3 :]
        slot = pl.program_id(0)
        one_fix, two_fix = fix_ref[0], fix_ref[1]

        @pl.when(slot == 0)
        def _():
            t = t_ref[...]
            norm = jnp.sqrt(jnp.sum(q_ref[...], keepdims=True) + jnp.sum(t * t, keepdims=True))
            clip = jnp.minimum(1.0, 1.0 / (norm + 1e-06))
            norm_out[...] = norm
            clip_ref[...] = jnp.broadcast_to(clip, clip_ref.shape)
            gradient = t * clip
            new, moment, square = adam(
                gradient, vw_ref[...], vm_ref[...], vv_ref[...], vector_rate, 0.0, one_fix, two_fix
            )
            tg_out[...], tw_out[...], tm_out[...], tv_out[...] = gradient, new, moment, square

        keep = src_ref[2, slot] > 0
        low = g_refs[0][0]
        for n in range(1, ng):
            low = jnp.where(src_ref[0, slot] == n, g_refs[n][0], low)
        gradient = low.astype(F32) * clip_ref[0:1, 0:1]
        new, moment, square = adam(
            gradient, w_ref[0], m_ref[0], v_ref[0], learn_rate, weight_decay, one_fix, two_fix
        )
        new = jnp.where(keep, new, 0.0)
        g_out[0] = jnp.where(keep, gradient, 0.0)
        w_out[0] = new
        m_out[0] = jnp.where(keep, moment, 0.0)
        v_out[0] = jnp.where(keep, square, 0.0)
        c_out[0] = new.astype(BF)

    def whole(shape):
        return pl.BlockSpec(shape, lambda s, src, fix: (0,) * len(shape))

    def picked(n):
        return pl.BlockSpec(
            (1, rows, D), lambda s, src, fix: (jnp.where(src[0, s] == n, src[1, s], 0), 0, 0)
        )

    own = pl.BlockSpec((1, rows, D), lambda s, src, fix: (s, 0, 0))
    vec = vector_total.shape
    return pl.pallas_call(
        body,
        grid_spec=pltpu.PrefetchScalarGridSpec(
            num_scalar_prefetch=2,
            grid=(slots,),
            in_specs=[whole((8, 128))] + [whole(vec)] * 4 + [picked(n) for n in range(ng)] + [own] * 3,
            out_specs=[whole((1, 1))] + [whole(vec)] * 4 + [own] * 5,
            scratch_shapes=[pltpu.VMEM((8, 128), F32)],
        ),
        out_shape=[jax.ShapeDtypeStruct((1, 1), F32)]
        + [jax.ShapeDtypeStruct(vec, F32)] * 4
        + [jax.ShapeDtypeStruct((slots, rows, D), F32)] * 4
        + [jax.ShapeDtypeStruct((slots, rows, D), BF)],
        **params(24, 20 * slots * rows * D, 32 * slots * rows * D),
    )(source, fixes, squares, vector_total, *vector_state, *summed, masters, firsts, seconds)


def stacked(pieces, deps=()):
    count = len(pieces)

    def body(*refs):
        out, sems = refs[count + len(deps) :]
        copies = [pltpu.make_async_copy(refs[n], out.at[n], sems.at[n]) for n in range(count)]
        for c in copies:
            c.start()
        for c in copies:
            c.wait()

    return ordered(
        body,
        in_specs=[ANY] * (count + len(deps)),
        out_specs=VMEM,
        out_shape=jax.ShapeDtypeStruct((count, *pieces[0].shape), pieces[0].dtype),
        scratch_shapes=[pltpu.SemaphoreType.DMA((count,))],
        **params(16, 1, 1),
    )(*pieces, *deps)


def pair_sums(pairs, deps=()):
    chips, each, rows, _ = pairs[0][0].shape
    count = len(pairs)

    def body(*refs):
        outs = refs[2 * count + len(deps) :]
        for n in range(chips):

            @pl.when(pl.program_id(0) == n)
            def _(n=n):
                for i in range(count):
                    keep, got = refs[2 * i], refs[2 * i + 1]
                    outs[n][i * each : (i + 1) * each] = (keep[0].astype(F32) + got[0].astype(F32)).astype(BF)

    spec = pl.BlockSpec((1, each, rows, D), lambda n: (n, 0, 0, 0))
    one = (count * each, rows, D)
    return ordered(
        body,
        grid=(chips,),
        in_specs=[spec] * (2 * count) + [ANY] * len(deps),
        out_specs=[pl.BlockSpec(one, lambda n: (0, 0, 0))] * chips,
        out_shape=[jax.ShapeDtypeStruct(one, BF)] * chips,
        **params(16, 1, 1),
    )(*[x for pair in pairs for x in pair], *deps)


def total_of(*groups):
    flat = [x for group in groups for x in group]
    _, rows, _ = flat[0].shape
    blocks = sum(group[0].shape[0] for group in groups)

    def body(*refs):
        out, n, at = refs[len(flat)], 0, 0
        for group in groups:
            total = refs[n][...].astype(F32)
            for ref in refs[n + 1 : n + len(group)]:
                total = total + ref[...].astype(F32)
            out[at : at + total.shape[0]] = total.astype(BF)
            n, at = n + len(group), at + total.shape[0]

    return ordered(
        body,
        in_specs=[VMEM] * len(flat),
        out_specs=VMEM,
        out_shape=jax.ShapeDtypeStruct((blocks, rows, D), BF),
        **params(16, 1, 1),
    )(*flat)


def plus(a, b):
    def body(a_ref, b_ref, out):
        out[...] = a_ref[...] + b_ref[...]

    return ordered(
        body,
        in_specs=[VMEM] * 2,
        out_specs=VMEM,
        out_shape=jax.ShapeDtypeStruct(a.shape, F32),
        **params(16, 1, 1),
    )(a, b)


def picked_end(here, value, outer):
    def body(h_ref, v_ref, o_ref, out):
        ends = (h_ref[0] == 0) | (h_ref[0] == 3)
        out[...] = jnp.where(ends, o_ref[...], v_ref[...])

    return ordered(
        body,
        in_specs=[SMEM, VMEM, VMEM],
        out_specs=VMEM,
        out_shape=jax.ShapeDtypeStruct(value.shape, BF),
        **params(16, 1, 1),
    )(here, value, outer)


def settled(here, value, outer):
    count, rows, _ = value.shape

    def body(h_ref, v_ref, o_ref, out_ref, q_ref):
        ends = (h_ref[0] == 0) | (h_ref[0] == 3)
        total = jnp.zeros((8, 128), F32)
        for n in range(count):
            kept = jnp.where(ends, o_ref[n], v_ref[n])
            out_ref[n] = kept
            x = kept.astype(F32)
            x = x * x
            for c in range(D // 128):
                part = x[:, c * 128 : (c + 1) * 128]
                for r in range(rows // 8):
                    total = total + part[r * 8 : (r + 1) * 8]
        q_ref[...] = total

    return ordered(
        body,
        in_specs=[SMEM, VMEM, VMEM],
        out_specs=[VMEM, VMEM],
        out_shape=[jax.ShapeDtypeStruct(value.shape, BF), jax.ShapeDtypeStruct((8, 128), F32)],
        **params(16, 1, 1),
    )(here, value, outer)


def swap(value, axis, bit):
    size = lax.axis_size(axis)
    return lax.ppermute(value, axis, [(i, i ^ bit) for i in range(size)])


CORE, SIDE, UP = 1, 2, 4
CHIPS = (0, SIDE, UP, SIDE | UP)


INWARD, ACROSS, OUTWARD = [(0, 1), (3, 2)], [(1, 2), (2, 1)], [(1, 0), (2, 3)]


def hop(value, pairs):
    if lax.axis_size("narrow") == 4:
        return lax.ppermute(value, "narrow", pairs)
    if pairs is INWARD:
        return (lax.psum(value.astype(F32), "narrow") - value.astype(F32)).astype(BF)
    return jnp.zeros_like(value) if pairs is ACROSS else value


def spread_wide(value):
    if lax.axis_size("wide") == 8:
        return [swap(value, "wide", m) for m in CHIPS[1:]]
    return None


def gather_wide(value):
    size = lax.axis_size("wide")
    count, rows, _ = value.shape
    full = lax.all_gather(value, "wide", axis=0, tiled=False)
    if rows % 16:
        full = jnp.swapaxes(full, 0, 1).reshape(1, count, D, D)
        size, rows = 1, D
    return Group((full,), [(0, (p,), rows, ("at", rows * p)) for p in range(size)])


def grad_layout(count, rows, size):
    if size != 8:
        return [jax.ShapeDtypeStruct((count, D, D), BF)], [(0, (), D, ("at", 0))]
    shape = jax.ShapeDtypeStruct((4, count, rows, D), BF)
    keep = [(0, (n,), rows, ("xor", m)) for n, m in enumerate(CHIPS)]
    give = [(1, (n,), rows, ("xor", m ^ CORE)) for n, m in enumerate(CHIPS)]
    return [shape] * 2, keep + give


def gathered(shard, parts):
    if parts is None:
        return gather_wide(shard)
    mine = stacked([shard, *parts])
    other = swap(mine, "wide", CORE)
    rows = shard.shape[1]
    masks = [(m, 0) for m in CHIPS] + [(m ^ CORE, 1) for m in CHIPS]
    return Group((mine, other), [(a, (n % 4,), rows, ("xor", m)) for n, (m, a) in enumerate(masks)])


def give(grads):
    if len(grads) == 1:
        return lax.psum_scatter(grads[0], "wide", scatter_dimension=1, tiled=True)
    return grads[0], swap(grads[1], "wide", CORE)


def exchange(*given):
    if not isinstance(given[0], tuple):
        return [given[0] if len(given) == 1 else jnp.concatenate(given, axis=0)]
    parts = pair_sums(list(given))
    return [parts[0]] + [swap(p, "wide", m) for p, m in zip(parts[1:], CHIPS[1:])]


def total_axis(value, axis):
    size = lax.axis_size(axis)
    bit = 1
    while bit < size:
        value = value + swap(value, axis, bit)
        bit *= 2
    return value


def slot_table(owners, capacity):
    number = owners.shape[0]
    order = jnp.arange(number, dtype=jnp.int32)
    before = (owners[:, None] == owners[None, :]) & (order[None, :] < order[:, None])
    return owners * capacity + jnp.sum(before.astype(jnp.int32), axis=1)


def per_device(tokens, doc_lengths, cotangent, owners, step_count, master, moment_one, moment_two, vectors, vector_one, vector_two):
    rows, capacity, _ = master.shape
    seqs = doc_lengths.shape[0]
    length = tokens.shape[0] // seqs
    blocks = owners.shape[0]
    wide = lax.axis_size("wide")
    narrow_index = lax.axis_index("narrow")
    me = lax.axis_index("wide").astype(jnp.int32).reshape(1)
    masters, firsts, seconds = [jnp.swapaxes(m, 0, 1) for m in (master, moment_one, moment_two)]

    here = narrow_index.astype(jnp.int32).reshape(1)
    local = slot_table(owners, capacity) - owners * capacity
    is_mine = (owners == narrow_index).astype(jnp.int32)
    table = jnp.stack([local, is_mine])
    ends = jnp.cumsum(doc_lengths, axis=1)
    position = jnp.arange(length, dtype=jnp.int32)
    passed = position[None, None, :] >= ends[:, :, None]
    start = jnp.sum(jnp.where(passed, doc_lengths[:, :, None], 0), axis=1)
    freqs = jnp.power(rope_base, -2.0 * jnp.arange(ROT // 2, dtype=F32) / ROT)
    angle = (position[None] - start).astype(F32)[:, None, :] * freqs[None, :, None]
    cosine, sine = jnp.cos(angle), jnp.sin(angle)
    start = start[:, None, :]

    ids_0, ids_1, ids_s, ids_t = (4, 8), (5, 9), (0, 1, 2, 3), (6, 10, 7, 11)
    pair_outs, pair_plan = grad_layout(2, rows, wide)
    four_outs, four_plan = grad_layout(4, rows, wide)
    full = jax.ShapeDtypeStruct(tokens.shape, F32)
    low = jax.ShapeDtypeStruct(tokens.shape, BF)
    acts, dzs, dbs, place = [], [], [], {}
    Order.deps = ()

    def arrived(group, ids):
        for i, b in enumerate(ids):
            place[b] = (group, i)

    def chunk(j):
        group, first = place[4 + j]
        act, dz, db, grads = mlp_chunk(
            me, h_two, cotangent, vectors[8 + j : 9 + j], group, first, pair_outs, pair_plan
        )
        acts.append(act)
        dzs.append(dz)
        dbs.append(db)
        return give(grads)

    def forth(j):
        return (acts[j], place[8 + j], False)

    def back(j):
        return (dzs[j], place[4 + j], True)

    w_0 = pack_owned(masters, table, ids_0)
    r_0 = hop(w_0, INWARD)
    h_one, h_two = layer_norms(tokens, vectors)
    w_0 = total_of([w_0, r_0])
    r_0 = hop(w_0, ACROSS)
    w_1 = pack_owned(masters, table, ids_1)
    r_1 = hop(w_1, INWARD)
    w_0 = total_of([w_0, r_0])
    r_0 = hop(w_0, OUTWARD)
    w_1 = total_of([w_1, r_1])
    r_1 = hop(w_1, ACROSS)
    w_s = pack_owned(masters, table, ids_s)
    r_s = hop(w_s, INWARD)
    w_0 = picked_end(here, w_0, r_0)
    arrived(gather_wide(w_0), ids_0)
    w_1 = total_of([w_1, r_1])
    r_1 = hop(w_1, OUTWARD)
    w_s = total_of([w_s, r_s])
    r_s = hop(w_s, ACROSS)
    w_1 = picked_end(here, w_1, r_1)
    arrived(gather_wide(w_1), ids_1)
    w_s = total_of([w_s, r_s])
    r_s = hop(w_s, OUTWARD)
    w_t = pack_owned(masters, table, ids_t)
    r_t = hop(w_t, INWARD)
    s_0 = chunk(0)
    w_s = picked_end(here, w_s, r_s)
    arrived(gather_wide(w_s), ids_s)
    w_t = total_of([w_t, r_t])
    r_t = hop(w_t, ACROSS)
    s_1 = chunk(1)
    w_t = total_of([w_t, r_t])
    r_t = hop(w_t, OUTWARD)
    early = products(me, [[forth(0), forth(1)], [back(0), back(1)]], store_all, [full, full])
    w_t = picked_end(here, w_t, r_t)
    arrived(gather_wide(w_t), ids_t)
    front = exchange(s_0, s_1)
    q, k, v, da = project(me, h_one, cotangent, vectors[4:7], cosine, sine, place[0][0])
    half = seqs // 2
    *inner, db_a = attention(q, k, v, da, start, cosine, sine, length, tuple(range(half)))
    front = total_of(front)
    r_f = hop(front, INWARD)
    a, *dqkv, db_b = attention(
        q, k, v, da, start, cosine, sine, length, tuple(range(half, seqs)), into=inner
    )
    db_qkv = db_a + db_b
    front = total_of([front, r_f])
    r_f = hop(front, ACROSS)
    s_s = give(attention_grads(me, h_one, a, cotangent, dqkv, four_outs, four_plan))
    front = total_of([front, r_f])
    r_f = hop(front, OUTWARD)
    s_2 = chunk(2)
    front, front_square = settled(here, front, r_f)
    mid = exchange(s_s)
    s_3 = chunk(3)
    middle, e_part, sums = products(
        me,
        [
            [(a, place[3], False), forth(2)],
            [(dqkv[n], place[n], True) for n in range(3)],
            [back(2)],
        ],
        middle_tail,
        [full, full, jax.ShapeDtypeStruct((5, D), F32)],
        starts=[early[0], None, early[1]],
        extra=[(tokens, True), (cotangent, True), (vectors, False)],
    )
    third = exchange(s_2)
    mid = total_of(mid)
    r_m = hop(mid, INWARD)
    layer_out, input_grad, last_sums = products(
        me,
        [[forth(3)], [back(3)]],
        last_tail,
        [low, full, jax.ShapeDtypeStruct((2, D), F32)],
        starts=[middle, None],
        extra=[(tokens, True), (cotangent, True), (vectors, False), (e_part, True)],
    )
    vector_total = jnp.concatenate(
        [sums[0:2], sums[2:4] + last_sums, db_qkv, sums[4:5], *dbs, sums[4:5]], axis=0
    )
    masks = [(axis, 1 << n) for axis in ("wide", "narrow") for n in range(lax.axis_size(axis).bit_length() - 1)]

    def vector_step(value):
        return plus(value, swap(value, *masks.pop(0)))

    last = exchange(s_3)
    third = total_of(third)
    r_h = hop(third, INWARD)
    mid = total_of([mid, r_m])
    r_m = hop(mid, ACROSS)
    vector_total = vector_step(vector_total)
    third = total_of([third, r_h])
    r_h = hop(third, ACROSS)
    last = total_of(last)
    r_l = hop(last, INWARD)
    vector_total = vector_step(vector_total)
    mid = total_of([mid, r_m])
    r_m = hop(mid, OUTWARD)
    last = total_of([last, r_l])
    r_l = hop(last, ACROSS)
    third = total_of([third, r_h])
    r_h = hop(third, OUTWARD)
    vector_total = vector_step(vector_total)
    last = total_of([last, r_l])
    r_l = hop(last, OUTWARD)
    while masks:
        vector_total = vector_step(vector_total)
    mid, mid_square = settled(here, mid, r_m)
    third, third_square = settled(here, third, r_h)
    last, last_square = settled(here, last, r_l)
    squares = total_axis(front_square + mid_square + third_square + last_square, "wide")
    summed = (front, mid, third, last)
    held = ((4, 8, 5, 9), ids_s, (6, 10), (7, 11))
    step_float = step_count[0].astype(F32)
    fixes = jnp.stack(
        [1.0 / (1.0 - jnp.power(beta_first, step_float)), 1.0 / (1.0 - jnp.power(beta_second, step_float))]
    )
    slot = jnp.arange(capacity, dtype=jnp.int32)
    hit = ((owners == narrow_index)[None, :] & (local[None, :] == slot[:, None])).astype(jnp.int32)
    which, inner = [0] * blocks, [0] * blocks
    for n, ids in enumerate(held):
        for i, b in enumerate(ids):
            which[b], inner[b] = n, i
    source = jnp.stack(
        [
            jnp.sum(hit * jnp.array(which, jnp.int32)[None], axis=1),
            jnp.sum(hit * jnp.array(inner, jnp.int32)[None], axis=1),
            jnp.sum(hit, axis=1),
        ]
    )
    norm, vector_grads, new_vectors, vector_first, vector_second, *new = update_all(
        source, fixes, squares, vector_total, (vectors, vector_one, vector_two), summed, masters, firsts, seconds
    )
    block_grads, new_master, new_first, new_second, new_copies = [jnp.swapaxes(m, 0, 1) for m in new]
    return (
        layer_out,
        input_grad,
        norm[0, 0],
        block_grads,
        new_master,
        new_first,
        new_second,
        new_copies,
        vector_grads,
        new_vectors,
        vector_first,
        vector_second,
    )


def solution(mesh):
    tok = P(("wide", "narrow"), None)
    own = P("wide", "narrow", None)
    return jax.shard_map(
        per_device,
        mesh=mesh,
        in_specs=(tok, tok, tok, P(), P(), own, own, own, P(), P(), P()),
        out_specs=(tok, tok, P(), own, own, own, own, own, P(), P(), P(), P()),
        check_vma=False,
    )
```

```python
from functools import partial

import jax
import jax.numpy as jnp
from jax import lax
from jax.experimental import pallas as pl
from jax.experimental.pallas import tpu as pltpu
from jax.sharding import PartitionSpec as P

D = 768
HEADS = 12
HEAD = 64
ROT = 16
FF = 3072
SPREAD = FF // D

norm_epsilon = 1e-05
beta_first = 0.5
beta_second = 0.5
adam_epsilon = 1e-08
learn_rate = 0.02
vector_rate = 0.1
weight_decay = 0.1
masked_fill = -1e30
rope_base = 10000.0
LOG2E = 1.4426950408889634

BF = jnp.bfloat16
F32 = jnp.float32
MB = 1 << 20
ANY = pl.BlockSpec(memory_space=pl.ANY)
HBM = pl.BlockSpec(memory_space=pltpu.HBM)
SMEM = pl.BlockSpec(memory_space=pltpu.SMEM)
VMEM = pl.BlockSpec(memory_space=pltpu.VMEM)


def dot(a, b):
    return lax.dot_general(a, b, (((1,), (0,)), ((), ())), preferred_element_type=F32)


def dot_nt(a, b):
    return lax.dot_general(a, b, (((1,), (1,)), ((), ())), preferred_element_type=F32)


def dot_tn(a, b):
    return lax.dot_general(a, b, (((0,), (0,)), ((), ())), preferred_element_type=F32)


def params(mib, flops=0, moved=0, **more):
    return dict(
        compiler_params=pltpu.CompilerParams(vmem_limit_bytes=int(mib * MB), **more),
        cost_estimate=pl.CostEstimate(
            flops=int(flops), bytes_accessed=int(moved), transcendentals=0
        ),
    )


class Order:
    deps = ()


def ordered(body, *, in_specs, out_specs, out_shape, scratch_shapes=(), **more):
    single = not isinstance(out_shape, (list, tuple))
    specs, shapes = ([out_specs], [out_shape]) if single else (list(out_specs), list(out_shape))
    deps, n_in, n_out = Order.deps, len(in_specs), len(shapes)

    def wrapped(*refs):
        rest = refs[n_in + len(deps) :]
        body(*refs[:n_in], *rest[:n_out], *rest[n_out + 1 :])
        rest[n_out][...] = jnp.zeros((8, 128), F32)

    mark = VMEM if more.get("grid") is None else pl.BlockSpec((8, 128), lambda *at: (0, 0))
    call = pl.pallas_call(
        wrapped,
        in_specs=[*in_specs, *[ANY] * len(deps)],
        out_specs=[*specs, mark],
        out_shape=[*shapes, jax.ShapeDtypeStruct((8, 128), F32)],
        scratch_shapes=list(scratch_shapes),
        **more,
    )

    def run(*args):
        *out, token = call(*args, *deps)
        Order.deps = (token,)
        return out[0] if single else out

    return run


class Group:
    def __init__(self, arrays, pieces):
        self.arrays = tuple(arrays)
        self.pieces = tuple(pieces)


def row_of(spec, rows, me):
    if spec[0] == "at":
        return spec[1]
    return pl.multiple_of((me ^ spec[1]) * rows, rows)


def weight_copies(group, refs, first, count, dst, sems, me):
    copies = []
    for n, (array, lead, rows, spec) in enumerate(group.pieces):
        src = refs[array].at[lead + (pl.ds(first, count),)]
        copies.append(
            pltpu.make_async_copy(src, dst.at[:, pl.ds(row_of(spec, rows, me), rows)], sems.at[n])
        )
    return copies


def grad_copies(plan, refs, first, count, src, sems, me):
    blocks = pl.ds(first, count)
    return [
        pltpu.make_async_copy(
            src.at[blocks, pl.ds(row_of(spec, rows, me), rows)], refs[array].at[lead + (blocks,)], sems.at[n]
        )
        for n, (array, lead, rows, spec) in enumerate(plan)
    ]


def norms_of(x):
    mean = jnp.mean(x, axis=-1, keepdims=True)
    centred = x - mean
    scale = lax.rsqrt(jnp.mean(centred * centred, axis=-1, keepdims=True) + norm_epsilon)
    return centred * scale, scale


def layer_norms(tokens, vectors, deps=()):
    rows = tokens.shape[0]
    tile = 256

    def body(x_ref, v_ref, *rest):
        one_ref, two_ref = rest[len(deps) :]
        xhat, _ = norms_of(x_ref[...].astype(F32))
        one_ref[...] = (xhat * v_ref[0:1] + v_ref[1:2]).astype(BF)
        two_ref[...] = (xhat * v_ref[2:3] + v_ref[3:4]).astype(BF)

    spec = pl.BlockSpec((tile, D), lambda t: (t, 0))
    return ordered(
        body,
        grid=(rows // tile,),
        in_specs=[spec, pl.BlockSpec(vectors.shape, lambda t: (0, 0))] + [ANY] * len(deps),
        out_specs=[spec, spec],
        out_shape=[jax.ShapeDtypeStruct((rows, D), BF)] * 2,
        **params(16, 20 * rows * D, 6 * rows * D),
    )(tokens, vectors, *deps)


def pack_owned(here, owners, masters, blocks):
    rows = masters.shape[1]
    nb = len(blocks)

    def body(h_ref, o_ref, m_ref, out, stage, sems):
        copies, mine = [], []
        for i, b in enumerate(blocks):
            owner = o_ref[b]
            slot = jnp.int32(0)
            for before in range(b):
                slot = slot + (o_ref[before] == owner).astype(jnp.int32)
            mine.append(owner == h_ref[0])
            copies.append(pltpu.make_async_copy(m_ref.at[slot], stage.at[i], sems.at[i]))
            copies[-1].start()
        for i in range(nb):
            copies[i].wait()
            out[i] = jnp.where(mine[i], stage[i], 0.0).astype(BF)

    return ordered(
        body,
        in_specs=[SMEM, SMEM, ANY],
        out_specs=VMEM,
        out_shape=jax.ShapeDtypeStruct((nb, rows, D), BF),
        scratch_shapes=[pltpu.VMEM((nb, rows, D), F32), pltpu.SemaphoreType.DMA((nb,))],
        **params(16, 1, 1),
    )(here, owners, masters)


def gelu_pair(z):
    size = jnp.abs(z)
    t = pl.reciprocal(1.0 + (0.3275911 * 0.7071067811865476) * size)
    bell = jnp.exp2((-0.5 * LOG2E) * (z * z))
    poly = 0.5 * 1.061405429
    for c in (-1.453152027, 1.421413741, -0.284496736, 0.254829592):
        poly = poly * t + 0.5 * c
    tail = poly * t * bell
    cdf = jnp.where(z >= 0.0, 1.0 - tail, tail)
    return z * cdf, cdf + z * (bell * 0.3989422804014327)


def mlp_chunk(me, h_two, cot, bias, group, first, outs, plan, deps=()):
    rows = h_two.shape[0]
    part = 256
    parts = rows // part
    na, no, nd = len(group.arrays), len(outs), len(deps)
    n_in, n_out = len(group.pieces), len(plan)

    def body(me_ref, h_ref, y_ref, b_ref, *rest):
        w_refs, rest = rest[:na], rest[na + nd :]
        act_ref, dz_ref, db_ref = rest[:3]
        o_refs = rest[3 : 3 + no]
        h, y, w, act, dz, low, in_sem, t_sem, out_sem = rest[3 + no :]
        me_id = me_ref[0]
        at = [pl.ds(p * part, part) for p in range(parts)]
        loads = weight_copies(group, w_refs, first, 2, w, in_sem, me_id)
        tokens = [
            [
                pltpu.make_async_copy(src.at[at[p]], dst.at[at[p]], t_sem.at[n, p])
                for n, (src, dst) in enumerate(((h_ref, h), (y_ref, y)))
            ]
            for p in range(parts)
        ]
        for c in loads:
            c.start()
        for pair in tokens:
            for c in pair:
                c.start()
        for c in loads:
            c.wait()
        for pair in tokens:
            for c in pair:
                c.wait()
        stores, z, u, sums = [], {}, {}, []

        def into(p):
            z[p] = dot(h[at[p]], w[0]) + b_ref[...]
            u[p] = dot_nt(y[at[p]], w[1])

        def slopes(p):
            value, slope = gelu_pair(z[p])
            act[at[p]] = value.astype(BF)
            low_dz = (u[p] * slope).astype(BF)
            dz[at[p]] = low_dz
            sums.append(jnp.sum(low_dz.astype(F32), axis=0, keepdims=True))
            for n, (src, dst) in enumerate(((act, act_ref), (dz, dz_ref))):
                stores.append(pltpu.make_async_copy(src.at[at[p]], dst.at[at[p]], t_sem.at[2 + n, p]))
                stores[-1].start()

        for turn in range(parts + 1):
            if turn < parts:
                into(turn)
            if turn:
                slopes(turn - 1)
        for i, (left, right) in enumerate(((h, dz), (act, y))):
            low[i] = dot_tn(left[...], right[...]).astype(BF)
        for c in grad_copies(plan, o_refs, 0, 2, low, out_sem, me_id):
            c.start()
            stores.append(c)
        db_ref[...] = sum(sums[1:], sums[0])
        for c in stores:
            c.wait()

    act, dz, db, *grads = ordered(
        body,
        in_specs=[SMEM, HBM, HBM, VMEM] + [HBM] * na + [ANY] * nd,
        out_specs=[HBM, HBM, VMEM] + [HBM] * no,
        out_shape=[
            jax.ShapeDtypeStruct((rows, D), BF),
            jax.ShapeDtypeStruct((rows, D), BF),
            jax.ShapeDtypeStruct((1, D), F32),
            *outs,
        ],
        scratch_shapes=[
            pltpu.VMEM((rows, D), BF),
            pltpu.VMEM((rows, D), BF),
            pltpu.VMEM((2, D, D), BF),
            pltpu.VMEM((rows, D), BF),
            pltpu.VMEM((rows, D), BF),
            pltpu.VMEM((2, D, D), BF),
            pltpu.SemaphoreType.DMA((n_in,)),
            pltpu.SemaphoreType.DMA((4, parts)),
            pltpu.SemaphoreType.DMA((n_out,)),
        ],
        **params(60, 8 * rows * D * D, 16 * rows * D),
    )(me, h_two, cot, bias, *group.arrays, *deps)
    return act, dz, db, grads


def turned(x, cosine, from_right, from_left):
    return (
        x * cosine
        + pltpu.roll(x, 128 - ROT // 2, 1) * from_right
        + pltpu.roll(x, ROT // 2, 1) * from_left
    )


def lanes_of(cosine, sine):
    half = ROT // 2
    lane = lax.broadcasted_iota(jnp.int32, (half, 128), 1) % HEAD
    row = lax.broadcasted_iota(jnp.int32, (half, 128), 0)
    one, two = (lane == row).astype(F32), (lane == row + half).astype(F32)

    def spread(values, mask):
        return lax.dot_general(
            values, mask, (((0,), (0,)), ((), ())), precision=lax.Precision.HIGHEST, preferred_element_type=F32
        )

    still = (lax.broadcasted_iota(jnp.int32, (1, 128), 1) % HEAD >= ROT).astype(F32)
    return spread(cosine, one + two) + still, spread(sine, one), spread(sine, two)


def project(me, h_one, cot, bias, cosine, sine, group, deps=()):
    rows = h_one.shape[0]
    tile = 256
    per = cosine.shape[2] // tile
    na, n_in = len(group.arrays), len(group.pieces)

    def body(me_ref, h_ref, y_ref, b_ref, c_ref, s_ref, *rest):
        w_refs, rest = rest[:na], rest[na + len(deps) :]
        outs = rest[:4]
        w_all, sems = rest[4:]
        step = pl.program_id(0)

        @pl.when(step == 0)
        def _():
            copies = weight_copies(group, w_refs, 0, 4, w_all, sems, me_ref[0])
            for c in copies:
                c.start()
            for c in copies:
                c.wait()

        cos_l, right, left = lanes_of(c_ref[0], s_ref[0])
        outs[3][...] = dot_nt(y_ref[...], w_all[3]).astype(BF)
        for i in range(3):
            value = dot(h_ref[...], w_all[i]) + b_ref[i : i + 1]
            if i == 2:
                outs[2][...] = value.astype(BF)
                continue
            for j in range(D // 128):
                outs[i][:, j * 128 : (j + 1) * 128] = turned(
                    value[:, j * 128 : (j + 1) * 128], cos_l, -right, left
                ).astype(BF)

    spec = pl.BlockSpec((tile, D), lambda t: (t, 0))
    table = pl.BlockSpec((1, ROT // 2, tile), lambda t: (t // per, 0, t % per))
    return ordered(
        body,
        grid=(rows // tile,),
        in_specs=[SMEM, spec, spec, pl.BlockSpec((3, D), lambda t: (0, 0)), table, table]
        + [HBM] * na
        + [ANY] * len(deps),
        out_specs=[spec] * 4,
        out_shape=[jax.ShapeDtypeStruct((rows, D), BF)] * 4,
        scratch_shapes=[pltpu.VMEM((4, D, D), BF), pltpu.SemaphoreType.DMA((n_in,))],
        **params(60, 8 * rows * D * D, 20 * rows * D),
    )(me, h_one, cot, bias, cosine, sine, *group.arrays, *deps)


def attention(q, k, v, da, starts, cosine, sine, length, which, into=(), deps=()):
    rows = q.shape[0]
    seqs = len(which)
    half = length // 2
    pair = 128

    def body(q_ref, k_ref, v_ref, d_ref, st_ref, hc_ref, hs_ref, *rest):
        a_ref, dq_ref, dk_ref, dv_ref, db_ref, mask, wheel = rest[len(into) + len(deps) :]

        @pl.when(pl.program_id(1) == 0)
        def _():
            key = lax.broadcasted_iota(jnp.int32, (length, length), 0)
            query = lax.broadcasted_iota(jnp.int32, (length, length), 1)
            seen = (key <= query) & (key >= st_ref[0])
            mask[...] = jnp.where(seen, 0.0, masked_fill)
            wheel[0], wheel[1], wheel[2] = lanes_of(hc_ref[0], hs_ref[0])

        q_all, k_all, v_all, d_all = q_ref[...], k_ref[...], v_ref[...], d_ref[...]
        vt, kt = v_all.T, k_all.T
        dt = d_all.T.astype(F32)
        lane = lax.broadcasted_iota(jnp.int32, (length, pair), 1)
        zero = jnp.zeros((), BF)
        dv = [jnp.zeros((half, pair), F32)] * 2
        dk = [jnp.zeros((half, pair), F32)] * 2
        jobs = []
        for h in range(2):
            mine = (lane >= h * HEAD) & (lane < (h + 1) * HEAD)
            qm = jnp.where(mine, q_all, zero)
            dm = jnp.where(mine, d_all, zero)
            for b in range(2):
                jobs.append((h, b, qm[b * half : (b + 1) * half], dm[b * half : (b + 1) * half]))
        raw, dp, prob, low, at, ds, dqt = {}, {}, {}, {}, {}, {}, {}

        def scores(i):
            h, b, qm, dm = jobs[i]
            n = half * (b + 1)
            raw[i] = dot_nt(k_all[:n], qm)
            dp[i] = dot_nt(v_all[:n], dm)

        def softmax(i):
            h, b, qm, dm = jobs[i]
            n = half * (b + 1)
            s = raw[i] * (HEAD**-0.5 * LOG2E) + mask[:n, b * half : (b + 1) * half]
            e = jnp.exp2(s - jnp.max(s, axis=0, keepdims=True))
            prob[i] = e * (1.0 / jnp.sum(e, axis=0, keepdims=True))
            low[i] = prob[i].astype(BF)
            at[i] = dot(vt[h * HEAD : (h + 1) * HEAD, :n], low[i])

        def slopes(i):
            h, b, qm, dm = jobs[i]
            dh = dt[h * HEAD : (h + 1) * HEAD, b * half : (b + 1) * half]
            total = jnp.sum(dh * at[i], axis=0, keepdims=True)
            ds[i] = (prob[i] * (dp[i] - total)).astype(BF)

        def grads(i):
            h, b, qm, dm = jobs[i]
            n = half * (b + 1)
            dqt[i] = dot(kt[h * HEAD : (h + 1) * HEAD, :n], ds[i])
            more_v, more_k = dot(low[i], dm), dot(ds[i], qm)
            for c in range(b + 1):
                dv[c] = dv[c] + more_v[c * half : (c + 1) * half]
                dk[c] = dk[c] + more_k[c * half : (c + 1) * half]

        stages = (scores, softmax, slopes, grads)
        for turn in range(len(jobs) + len(stages) - 1):
            for n, stage in reversed(list(enumerate(stages))):
                if 0 <= turn - n < len(jobs):
                    stage(turn - n)
        at_h, dq_h = [], []
        for h in range(2):
            at_h.append(jnp.concatenate([at[2 * h], at[2 * h + 1]], axis=1))
            dq = jnp.concatenate([dqt[2 * h], dqt[2 * h + 1]], axis=1) * HEAD**-0.5
            u, w, cos, sin = dq[0:8], dq[8:16], hc_ref[0], hs_ref[0]
            dq_h.append(jnp.concatenate([u * cos + w * sin, w * cos - u * sin, dq[16:]], axis=0))
        a_ref[...] = jnp.concatenate(at_h, axis=0).astype(BF).T
        dq = jnp.concatenate(dq_h, axis=0).astype(BF).T
        dq_ref[...] = dq
        sums = [jnp.sum(dq.astype(F32), axis=0, keepdims=True)]
        sum_k = sum_v = jnp.zeros((1, pair), F32)
        for c in range(2):
            at_k = slice(c * half, (c + 1) * half)
            back = turned(dk[c] * HEAD**-0.5, wheel[0, at_k], wheel[1, at_k], -wheel[2, at_k]).astype(BF)
            dk_ref[at_k] = back
            sum_k = sum_k + jnp.sum(back.astype(F32), axis=0, keepdims=True)
            value = dv[c].astype(BF)
            dv_ref[at_k] = value
            sum_v = sum_v + jnp.sum(value.astype(F32), axis=0, keepdims=True)
        db_ref[0] = jnp.concatenate(sums + [sum_k, sum_v], axis=0)

    base = which[0]
    spec = pl.BlockSpec((length, pair), lambda s, h: (s + base, h))
    table = pl.BlockSpec((1, ROT // 2, length), lambda s, h: (s + base, 0, 0))
    a, dq, dk, dv, db = ordered(
        body,
        grid=(seqs, D // pair),
        in_specs=[spec] * 4
        + [pl.BlockSpec((1, 1, length), lambda s, h: (s + base, 0, 0)), table, table]
        + [ANY] * (len(into) + len(deps)),
        out_specs=[spec, spec, spec, spec, pl.BlockSpec((1, 3, pair), lambda s, h: (s, 0, h))],
        out_shape=[jax.ShapeDtypeStruct((rows, D), BF)] * 4
        + [jax.ShapeDtypeStruct((seqs, 3, D), F32)],
        scratch_shapes=[pltpu.VMEM((length, length), F32), pltpu.VMEM((3, length, 128), F32)],
        input_output_aliases={7 + n: n for n in range(len(into))},
        **params(60, 10e9 * seqs, 20 * rows * D),
    )(q, k, v, da, starts, cosine, sine, *into, *deps)
    return a, dq, dk, dv, db


def attention_grads(me, h_one, a, cot, dqkv, outs, plan, deps=()):
    rows = h_one.shape[0]
    no, n_out = len(outs), len(plan)

    def body(me_ref, h_ref, a_ref, y_ref, dq_ref, dk_ref, dv_ref, *rest):
        rest = rest[len(deps) :]
        o_refs = rest[:no]
        low, sems = rest[no:]
        pending = []
        for i, (left, right) in enumerate(
            ((h_ref, dq_ref), (h_ref, dk_ref), (h_ref, dv_ref), (a_ref, y_ref))
        ):
            low[i] = dot_tn(left[...], right[...]).astype(BF)
            if i % 2:
                copies = grad_copies(plan, o_refs, i - 1, 2, low, sems.at[i // 2], me_ref[0])
                for c in copies:
                    c.start()
                pending += copies
        for c in pending:
            c.wait()

    whole = pl.BlockSpec(memory_space=pltpu.VMEM)
    return ordered(
        body,
        in_specs=[SMEM] + [whole] * 6 + [ANY] * len(deps),
        out_specs=[HBM] * no,
        out_shape=list(outs),
        scratch_shapes=[pltpu.VMEM((4, D, D), BF), pltpu.SemaphoreType.DMA((2, n_out))],
        **params(60, 8 * rows * D * D, 12 * rows * D),
    )(me, h_one, a, cot, *dqkv, *deps)


def products(me, jobs, tail, outs, starts=None, extra=(), deps=(), mib=60):
    starts = starts or [()] * len(jobs)
    rows = jobs[0][0][0].shape[0]
    tile = 256
    groups, used = [], {}
    for job in jobs:
        for _, (group, i), _ in job:
            if id(group) not in used:
                groups.append(group)
                used[id(group)] = []
            used[id(group)].append(i)
    first, flat, runs, slot, at = {}, [], [], {}, 0
    for group in groups:
        first[id(group)] = len(flat)
        flat += list(group.arrays)
        low, high = min(used[id(group)]), max(used[id(group)])
        runs.append((group, low, high - low + 1, at))
        for i in range(low, high + 1):
            slot[id(group), i] = at
            at += 1
    lefts = [left for job in jobs for left, _, _ in job]
    begun = [x for group in starts for x in group]
    n_in = max(len(g.pieces) for g in groups)
    nl, ns, ne, nw, no = len(lefts), len(begun), len(extra), len(flat), len(outs)

    def body(me_ref, *rest):
        l_refs, rest = rest[:nl], rest[nl:]
        s_refs, rest = list(rest[:ns]), rest[ns:]
        e_refs, rest = rest[:ne], rest[ne:]
        w_refs, rest = rest[:nw], rest[nw + len(deps) :]
        o_refs, (w_all, sems) = rest[:no], rest[no:]
        step = pl.program_id(0)

        @pl.when(step == 0)
        def _():
            copies = []
            for n, (group, low, count, to) in enumerate(runs):
                refs = w_refs[first[id(group)] :]
                copies += weight_copies(
                    group, refs, low, count, w_all.at[pl.ds(to, count)], sems.at[n], me_ref[0]
                )
            for c in copies:
                c.start()
            for c in copies:
                c.wait()

        results, n = [], 0
        for job, begin in zip(jobs, starts):
            total = None
            for _ in begin:
                more = s_refs.pop(0)[...]
                total = more if total is None else total + more
            for _, (group, i), transposed in job:
                term = (dot_nt if transposed else dot)(l_refs[n][...], w_all[slot[id(group), i]])
                total = term if total is None else total + term
                n += 1
            results.append(total)
        tail(e_refs, results, o_refs, step)

    spec = pl.BlockSpec((tile, D), lambda t: (t, 0))

    def whole(x):
        return pl.BlockSpec(x.shape, lambda t: (0,) * len(x.shape))

    return ordered(
        body,
        grid=(rows // tile,),
        in_specs=[SMEM]
        + [spec] * (nl + ns)
        + [spec if per_token else whole(x) for x, per_token in extra]
        + [HBM] * nw
        + [ANY] * len(deps),
        out_specs=[spec if x.shape[0] == rows else whole(x) for x in outs],
        out_shape=list(outs),
        scratch_shapes=[pltpu.VMEM((at, D, D), BF), pltpu.SemaphoreType.DMA((len(runs), n_in))],
        **params(mib, 2 * nl * rows * D * D, (2 * nl + 8) * rows * D),
    )(me, *lefts, *begun, *[x for x, _ in extra], *flat, *deps)


def store_all(e_refs, results, o_refs, step):
    for ref, value in zip(o_refs, results):
        ref[...] = value


def add_rows(ref, terms, step):
    sums = jnp.concatenate([jnp.sum(term, axis=0, keepdims=True) for term in terms], axis=0)

    @pl.when(step == 0)
    def _():
        ref[...] = sums

    @pl.when(step > 0)
    def _():
        ref[...] += sums


def middle_tail(e_refs, results, o_refs, step):
    x_ref, y_ref, v_ref = e_refs
    out_ref, e_ref, sum_ref = o_refs
    out, d_one, d_two = results
    x = x_ref[...].astype(F32)
    out_ref[...] = out + x + (v_ref[7:8] + v_ref[8 + SPREAD : 9 + SPREAD])
    xhat, _ = norms_of(x)
    e_ref[...] = d_one * v_ref[0:1] + d_two * v_ref[2:3]
    add_rows(sum_ref, (d_one * xhat, d_one, d_two * xhat, d_two, y_ref[...].astype(F32)), step)


def last_tail(e_refs, results, o_refs, step):
    x_ref, y_ref, v_ref, e_ref = e_refs
    out_ref, grad_ref, sum_ref = o_refs
    out, d_two = results
    out_ref[...] = out.astype(BF)
    xhat, scale = norms_of(x_ref[...].astype(F32))
    e = e_ref[...] + d_two * v_ref[2:3]
    inner = jnp.mean(e * xhat, axis=-1, keepdims=True)
    y = y_ref[...].astype(F32)
    grad_ref[...] = y + (e - jnp.mean(e, axis=-1, keepdims=True) - xhat * inner) * scale
    add_rows(sum_ref, (d_two * xhat, d_two), step)


def adam(gradient, weight, moment, square, rate, decay, one_fix, two_fix):
    moment_new = beta_first * moment + (1.0 - beta_first) * gradient
    square_new = beta_second * square + (1.0 - beta_second) * gradient * gradient
    update = (moment_new * one_fix) / (jnp.sqrt(square_new * two_fix) + adam_epsilon)
    return weight - rate * (update + decay * weight), moment_new, square_new


def update_all(source, fixes, squares, vector_total, vector_state, summed, masters, firsts, seconds):
    slots, rows, _ = masters.shape
    ng = len(summed)

    def body(src_ref, fix_ref, q_ref, t_ref, vw_ref, vm_ref, vv_ref, *rest):
        g_refs, (w_ref, m_ref, v_ref) = rest[:ng], rest[ng : ng + 3]
        norm_out, tg_out, tw_out, tm_out, tv_out, g_out, w_out, m_out, v_out, c_out, clip_ref = rest[ng + 3 :]
        slot = pl.program_id(0)
        one_fix, two_fix = fix_ref[0], fix_ref[1]

        @pl.when(slot == 0)
        def _():
            t = t_ref[...]
            norm = jnp.sqrt(jnp.sum(q_ref[...], keepdims=True) + jnp.sum(t * t, keepdims=True))
            clip = jnp.minimum(1.0, 1.0 / (norm + 1e-06))
            norm_out[...] = norm
            clip_ref[...] = jnp.broadcast_to(clip, clip_ref.shape)
            gradient = t * clip
            new, moment, square = adam(
                gradient, vw_ref[...], vm_ref[...], vv_ref[...], vector_rate, 0.0, one_fix, two_fix
            )
            tg_out[...], tw_out[...], tm_out[...], tv_out[...] = gradient, new, moment, square

        keep = src_ref[2, slot] > 0
        low = g_refs[0][0]
        for n in range(1, ng):
            low = jnp.where(src_ref[0, slot] == n, g_refs[n][0], low)
        gradient = low.astype(F32) * clip_ref[0:1, 0:1]
        new, moment, square = adam(
            gradient, w_ref[0], m_ref[0], v_ref[0], learn_rate, weight_decay, one_fix, two_fix
        )
        new = jnp.where(keep, new, 0.0)
        g_out[0] = jnp.where(keep, gradient, 0.0)
        w_out[0] = new
        m_out[0] = jnp.where(keep, moment, 0.0)
        v_out[0] = jnp.where(keep, square, 0.0)
        c_out[0] = new.astype(BF)

    def whole(shape):
        return pl.BlockSpec(shape, lambda s, src, fix: (0,) * len(shape))

    def picked(n):
        return pl.BlockSpec(
            (1, rows, D), lambda s, src, fix: (jnp.where(src[0, s] == n, src[1, s], 0), 0, 0)
        )

    own = pl.BlockSpec((1, rows, D), lambda s, src, fix: (s, 0, 0))
    vec = vector_total.shape
    return pl.pallas_call(
        body,
        grid_spec=pltpu.PrefetchScalarGridSpec(
            num_scalar_prefetch=2,
            grid=(slots,),
            in_specs=[whole((8, 128))] + [whole(vec)] * 4 + [picked(n) for n in range(ng)] + [own] * 3,
            out_specs=[whole((1, 1))] + [whole(vec)] * 4 + [own] * 5,
            scratch_shapes=[pltpu.VMEM((8, 128), F32)],
        ),
        out_shape=[jax.ShapeDtypeStruct((1, 1), F32)]
        + [jax.ShapeDtypeStruct(vec, F32)] * 4
        + [jax.ShapeDtypeStruct((slots, rows, D), F32)] * 4
        + [jax.ShapeDtypeStruct((slots, rows, D), BF)],
        **params(24, 20 * slots * rows * D, 32 * slots * rows * D),
    )(source, fixes, squares, vector_total, *vector_state, *summed, masters, firsts, seconds)


def stacked(pieces, deps=()):
    count = len(pieces)

    def body(*refs):
        out, sems = refs[count + len(deps) :]
        copies = [pltpu.make_async_copy(refs[n], out.at[n], sems.at[n]) for n in range(count)]
        for c in copies:
            c.start()
        for c in copies:
            c.wait()

    return ordered(
        body,
        in_specs=[ANY] * (count + len(deps)),
        out_specs=VMEM,
        out_shape=jax.ShapeDtypeStruct((count, *pieces[0].shape), pieces[0].dtype),
        scratch_shapes=[pltpu.SemaphoreType.DMA((count,))],
        **params(16, 1, 1),
    )(*pieces, *deps)


def pair_sums(pairs, deps=()):
    chips, each, rows, _ = pairs[0][0].shape
    count = len(pairs)

    def body(*refs):
        outs = refs[2 * count + len(deps) :]
        for n in range(chips):

            @pl.when(pl.program_id(0) == n)
            def _(n=n):
                for i in range(count):
                    keep, got = refs[2 * i], refs[2 * i + 1]
                    outs[n][i * each : (i + 1) * each] = (keep[0].astype(F32) + got[0].astype(F32)).astype(BF)

    spec = pl.BlockSpec((1, each, rows, D), lambda n: (n, 0, 0, 0))
    one = (count * each, rows, D)
    return ordered(
        body,
        grid=(chips,),
        in_specs=[spec] * (2 * count) + [ANY] * len(deps),
        out_specs=[pl.BlockSpec(one, lambda n: (0, 0, 0))] * chips,
        out_shape=[jax.ShapeDtypeStruct(one, BF)] * chips,
        **params(16, 1, 1),
    )(*[x for pair in pairs for x in pair], *deps)


def total_of(*groups):
    flat = [x for group in groups for x in group]
    _, rows, _ = flat[0].shape
    blocks = sum(group[0].shape[0] for group in groups)

    def body(*refs):
        out, n, at = refs[len(flat)], 0, 0
        for group in groups:
            total = refs[n][...].astype(F32)
            for ref in refs[n + 1 : n + len(group)]:
                total = total + ref[...].astype(F32)
            out[at : at + total.shape[0]] = total.astype(BF)
            n, at = n + len(group), at + total.shape[0]

    return ordered(
        body,
        in_specs=[VMEM] * len(flat),
        out_specs=VMEM,
        out_shape=jax.ShapeDtypeStruct((blocks, rows, D), BF),
        **params(16, 1, 1),
    )(*flat)


def handed_on(value):
    def body(value_ref, out):
        pass

    return ordered(
        body,
        in_specs=[ANY],
        out_specs=ANY,
        out_shape=jax.ShapeDtypeStruct(value.shape, value.dtype),
        input_output_aliases={0: 0},
        **params(1, 1, 1),
    )(value)


def vector_terms(sums, last_sums, db_a, db_b, dbs):
    def body(s_ref, l_ref, a_ref, b_ref, *rest):
        out = rest[SPREAD]
        out[0:2] = s_ref[0:2]
        out[2:4] = s_ref[2:4] + l_ref[...]
        qkv = a_ref[0] + b_ref[0]
        for n in range(1, a_ref.shape[0]):
            qkv = qkv + (a_ref[n] + b_ref[n])
        out[4:7] = qkv
        out[7:8] = s_ref[4:5]
        for n in range(SPREAD):
            out[8 + n : 9 + n] = rest[n][...]
        out[8 + SPREAD : 9 + SPREAD] = s_ref[4:5]

    return ordered(
        body,
        in_specs=[VMEM] * (4 + SPREAD),
        out_specs=VMEM,
        out_shape=jax.ShapeDtypeStruct((9 + SPREAD, D), F32),
        **params(16, 1, 1),
    )(sums, last_sums, db_a, db_b, *dbs)


def plus(a, b):
    def body(a_ref, b_ref, out):
        out[...] = a_ref[...] + b_ref[...]

    return ordered(
        body,
        in_specs=[VMEM] * 2,
        out_specs=VMEM,
        out_shape=jax.ShapeDtypeStruct(a.shape, F32),
        **params(16, 1, 1),
    )(a, b)


def picked_end(here, value, outer):
    def body(h_ref, v_ref, o_ref, out):
        ends = (h_ref[0] == 0) | (h_ref[0] == 3)
        out[...] = jnp.where(ends, o_ref[...], v_ref[...])

    return ordered(
        body,
        in_specs=[SMEM, VMEM, VMEM],
        out_specs=VMEM,
        out_shape=jax.ShapeDtypeStruct(value.shape, BF),
        **params(16, 1, 1),
    )(here, value, outer)


def settled(here, value, outer):
    count, rows, _ = value.shape

    def body(h_ref, v_ref, o_ref, out_ref, q_ref):
        ends = (h_ref[0] == 0) | (h_ref[0] == 3)
        total = jnp.zeros((8, 128), F32)
        for n in range(count):
            kept = jnp.where(ends, o_ref[n], v_ref[n])
            out_ref[n] = kept
            x = kept.astype(F32)
            x = x * x
            for c in range(D // 128):
                part = x[:, c * 128 : (c + 1) * 128]
                for r in range(rows // 8):
                    total = total + part[r * 8 : (r + 1) * 8]
        q_ref[...] = total

    return ordered(
        body,
        in_specs=[SMEM, VMEM, VMEM],
        out_specs=[VMEM, VMEM],
        out_shape=[jax.ShapeDtypeStruct(value.shape, BF), jax.ShapeDtypeStruct((8, 128), F32)],
        **params(16, 1, 1),
    )(here, value, outer)


def swap(value, axis, bit):
    size = lax.axis_size(axis)
    return lax.ppermute(value, axis, [(i, i ^ bit) for i in range(size)])


CORE, SIDE, UP = 1, 2, 4
CHIPS = (0, SIDE, UP, SIDE | UP)


INWARD, ACROSS, OUTWARD = [(0, 1), (3, 2)], [(1, 2), (2, 1)], [(1, 0), (2, 3)]


def hop(value, pairs):
    if lax.axis_size("narrow") == 4:
        return lax.ppermute(value, "narrow", pairs)
    if pairs is INWARD:
        return (lax.psum(value.astype(F32), "narrow") - value.astype(F32)).astype(BF)
    return jnp.zeros_like(value) if pairs is ACROSS else value


def spread_wide(value):
    if lax.axis_size("wide") == 8:
        return [swap(value, "wide", m) for m in CHIPS[1:]]
    return None


def gather_wide(value):
    size = lax.axis_size("wide")
    count, rows, _ = value.shape
    full = lax.all_gather(value, "wide", axis=0, tiled=False)
    if rows % 16:
        full = jnp.swapaxes(full, 0, 1).reshape(1, count, D, D)
        size, rows = 1, D
    return Group((full,), [(0, (p,), rows, ("at", rows * p)) for p in range(size)])


def grad_layout(count, rows, size):
    if size != 8:
        return [jax.ShapeDtypeStruct((count, D, D), BF)], [(0, (), D, ("at", 0))]
    shape = jax.ShapeDtypeStruct((4, count, rows, D), BF)
    keep = [(0, (n,), rows, ("xor", m)) for n, m in enumerate(CHIPS)]
    give = [(1, (n,), rows, ("xor", m ^ CORE)) for n, m in enumerate(CHIPS)]
    return [shape] * 2, keep + give


def gathered(shard, parts):
    if parts is None:
        return gather_wide(shard)
    mine = stacked([shard, *parts])
    other = swap(mine, "wide", CORE)
    rows = shard.shape[1]
    masks = [(m, 0) for m in CHIPS] + [(m ^ CORE, 1) for m in CHIPS]
    return Group((mine, other), [(a, (n % 4,), rows, ("xor", m)) for n, (m, a) in enumerate(masks)])


def give(grads):
    if len(grads) == 1:
        return lax.psum_scatter(grads[0], "wide", scatter_dimension=1, tiled=True)
    return grads[0], swap(grads[1], "wide", CORE)


def exchange(*given):
    if not isinstance(given[0], tuple):
        return [given[0] if len(given) == 1 else jnp.concatenate(given, axis=0)]
    parts = pair_sums(list(given))
    return [parts[0]] + [swap(p, "wide", m) for p, m in zip(parts[1:], CHIPS[1:])]


def total_axis(value, axis):
    size = lax.axis_size(axis)
    bit = 1
    while bit < size:
        value = value + swap(value, axis, bit)
        bit *= 2
    return value


def slot_table(owners, capacity):
    number = owners.shape[0]
    order = jnp.arange(number, dtype=jnp.int32)
    before = (owners[:, None] == owners[None, :]) & (order[None, :] < order[:, None])
    return owners * capacity + jnp.sum(before.astype(jnp.int32), axis=1)


def per_device(tokens, doc_lengths, cotangent, owners, step_count, master, moment_one, moment_two, vectors, vector_one, vector_two):
    rows, capacity, _ = master.shape
    seqs = doc_lengths.shape[0]
    length = tokens.shape[0] // seqs
    blocks = owners.shape[0]
    wide = lax.axis_size("wide")
    narrow_index = lax.axis_index("narrow")
    me = lax.axis_index("wide").astype(jnp.int32).reshape(1)
    masters, firsts, seconds = [jnp.swapaxes(m, 0, 1) for m in (master, moment_one, moment_two)]

    here = narrow_index.astype(jnp.int32).reshape(1)
    local = slot_table(owners, capacity) - owners * capacity
    ends = jnp.cumsum(doc_lengths, axis=1)
    position = jnp.arange(length, dtype=jnp.int32)
    passed = position[None, None, :] >= ends[:, :, None]
    start = jnp.sum(jnp.where(passed, doc_lengths[:, :, None], 0), axis=1)
    freqs = jnp.power(rope_base, -2.0 * jnp.arange(ROT // 2, dtype=F32) / ROT)
    angle = (position[None] - start).astype(F32)[:, None, :] * freqs[None, :, None]
    cosine, sine = jnp.cos(angle), jnp.sin(angle)
    start = start[:, None, :]

    ids_0, ids_s, ids_t = (4, 8, 5, 9), (0, 1, 2, 3), (6, 10, 7, 11)
    pair_outs, pair_plan = grad_layout(2, rows, wide)
    four_outs, four_plan = grad_layout(4, rows, wide)
    full = jax.ShapeDtypeStruct(tokens.shape, F32)
    low = jax.ShapeDtypeStruct(tokens.shape, BF)
    acts, dzs, dbs, place = [], [], [], {}
    Order.deps = ()

    def arrived(group, ids):
        for i, b in enumerate(ids):
            place[b] = (group, i)

    def chunk(j):
        group, first = place[4 + j]
        act, dz, db, grads = mlp_chunk(
            me, h_two, cotangent, vectors[8 + j : 9 + j], group, first, pair_outs, pair_plan
        )
        acts.append(act)
        dzs.append(dz)
        dbs.append(db)
        return grads

    def forth(j):
        return (acts[j], place[8 + j], False)

    def back(j):
        return (dzs[j], place[4 + j], True)

    w_0 = pack_owned(here, owners, masters, ids_0)
    r_0 = hop(w_0, INWARD)
    h_one, h_two = layer_norms(tokens, vectors)
    w_0 = total_of([w_0, r_0])
    r_0 = hop(w_0, ACROSS)
    w_s = pack_owned(here, owners, masters, ids_s)
    r_s = hop(w_s, INWARD)
    w_0 = total_of([w_0, r_0])
    r_0 = hop(w_0, OUTWARD)
    w_s = total_of([w_s, r_s])
    r_s = hop(w_s, ACROSS)
    w_0 = picked_end(here, w_0, r_0)
    arrived(gather_wide(w_0), ids_0)
    w_t = pack_owned(here, owners, masters, ids_t)
    r_t = hop(w_t, INWARD)
    w_s = total_of([w_s, r_s])
    r_s = hop(w_s, OUTWARD)
    w_t = total_of([w_t, r_t])
    r_t = hop(w_t, ACROSS)
    w_s = picked_end(here, w_s, r_s)
    arrived(gather_wide(w_s), ids_s)
    w_t = total_of([w_t, r_t])
    r_t = hop(w_t, OUTWARD)
    s_0 = give(chunk(0))
    s_1 = give(chunk(1))
    w_t = picked_end(here, w_t, r_t)
    arrived(gather_wide(w_t), ids_t)
    front = exchange(s_0, s_1)
    q, k, v, da = project(me, h_one, cotangent, vectors[4:7], cosine, sine, place[0][0])
    half = seqs // 2
    *inner, db_a = attention(q, k, v, da, start, cosine, sine, length, tuple(range(half)))
    a, *dqkv, db_b = attention(
        q, k, v, da, start, cosine, sine, length, tuple(range(half, seqs)), into=inner
    )
    front = total_of(front)
    r_f = hop(front, INWARD)
    s_s = give(attention_grads(me, h_one, a, cotangent, dqkv, four_outs, four_plan))
    s_2 = give(chunk(2))
    front = total_of([front, r_f])
    r_f = hop(front, ACROSS)
    mid = exchange(s_s)
    middle, e_part, sums = products(
        me,
        [
            [(a, place[3], False), forth(2)],
            [(dqkv[n], place[n], True) for n in range(3)],
            [back(2)],
        ],
        middle_tail,
        [full, full, jax.ShapeDtypeStruct((5, D), F32)],
        extra=[(tokens, True), (cotangent, True), (vectors, False)],
    )
    front = total_of([front, r_f])
    r_f = hop(front, OUTWARD)
    third = exchange(s_2)
    mid = total_of(mid)
    r_m = hop(mid, INWARD)
    s_3 = chunk(3)
    mid = total_of([mid, r_m])
    r_m = hop(mid, ACROSS)
    third = total_of(third)
    r_h = hop(third, INWARD)
    last = exchange(give([*s_3[:-1], handed_on(s_3[-1])]))
    early = products(me, [[forth(0), forth(1)], [back(0), back(1)]], store_all, [full, full])
    last = total_of(last)
    r_l = hop(last, INWARD)
    mid = total_of([mid, r_m])
    r_m = hop(mid, OUTWARD)
    third = total_of([third, r_h])
    r_h = hop(third, ACROSS)
    layer_out, input_grad, last_sums = products(
        me,
        [[forth(3)], [back(3)]],
        last_tail,
        [low, full, jax.ShapeDtypeStruct((2, D), F32)],
        starts=[(middle, early[0]), (early[1],)],
        extra=[(tokens, True), (cotangent, True), (vectors, False), (e_part, True)],
    )
    vector_total = vector_terms(sums, last_sums, db_a, db_b, dbs)
    masks = [(axis, 1 << n) for axis in ("wide", "narrow") for n in range(lax.axis_size(axis).bit_length() - 1)]

    def vector_step(value):
        return plus(value, swap(value, *masks.pop(0)))

    last = total_of([last, r_l])
    r_l = hop(last, ACROSS)
    third = total_of([third, r_h])
    r_h = hop(third, OUTWARD)
    vector_total = vector_step(vector_total)
    vector_total = vector_step(vector_total)
    last = total_of([last, r_l])
    r_l = hop(last, OUTWARD)
    vector_total = vector_step(vector_total)
    front, front_square = settled(here, front, r_f)
    mid, mid_square = settled(here, mid, r_m)
    third, third_square = settled(here, third, r_h)
    while masks:
        vector_total = vector_step(vector_total)
    last, last_square = settled(here, last, r_l)
    squares = total_axis(front_square + mid_square + third_square + last_square, "wide")
    summed = (front, mid, third, last)
    held = ((4, 8, 5, 9), ids_s, (6, 10), (7, 11))
    step_float = step_count[0].astype(F32)
    fixes = jnp.stack(
        [1.0 / (1.0 - jnp.power(beta_first, step_float)), 1.0 / (1.0 - jnp.power(beta_second, step_float))]
    )
    slot = jnp.arange(capacity, dtype=jnp.int32)
    hit = ((owners == narrow_index)[None, :] & (local[None, :] == slot[:, None])).astype(jnp.int32)
    which, inner = [0] * blocks, [0] * blocks
    for n, ids in enumerate(held):
        for i, b in enumerate(ids):
            which[b], inner[b] = n, i
    source = jnp.stack(
        [
            jnp.sum(hit * jnp.array(which, jnp.int32)[None], axis=1),
            jnp.sum(hit * jnp.array(inner, jnp.int32)[None], axis=1),
            jnp.sum(hit, axis=1),
        ]
    )
    norm, vector_grads, new_vectors, vector_first, vector_second, *new = update_all(
        source, fixes, squares, vector_total, (vectors, vector_one, vector_two), summed, masters, firsts, seconds
    )
    block_grads, new_master, new_first, new_second, new_copies = [jnp.swapaxes(m, 0, 1) for m in new]
    return (
        layer_out,
        input_grad,
        norm[0, 0],
        block_grads,
        new_master,
        new_first,
        new_second,
        new_copies,
        vector_grads,
        new_vectors,
        vector_first,
        vector_second,
    )


def solution(mesh):
    tok = P(("wide", "narrow"), None)
    own = P("wide", "narrow", None)
    return jax.shard_map(
        per_device,
        mesh=mesh,
        in_specs=(tok, tok, tok, P(), P(), own, own, own, P(), P(), P()),
        out_specs=(tok, tok, P(), own, own, own, own, own, P(), P(), P(), P()),
        check_vma=False,
    )
```

```python
from functools import partial

import jax
import jax.numpy as jnp
from jax import lax
from jax.experimental import pallas as pl
from jax.experimental.pallas import tpu as pltpu
from jax.sharding import PartitionSpec as P

D = 768
HEADS = 12
HEAD = 64
ROT = 16
FF = 3072
SPREAD = FF // D

norm_epsilon = 1e-05
beta_first = 0.5
beta_second = 0.5
adam_epsilon = 1e-08
learn_rate = 0.02
vector_rate = 0.1
weight_decay = 0.1
masked_fill = -1e30
rope_base = 10000.0
LOG2E = 1.4426950408889634

BF = jnp.bfloat16
F32 = jnp.float32
MB = 1 << 20
ANY = pl.BlockSpec(memory_space=pl.ANY)
HBM = pl.BlockSpec(memory_space=pltpu.HBM)
SMEM = pl.BlockSpec(memory_space=pltpu.SMEM)
VMEM = pl.BlockSpec(memory_space=pltpu.VMEM)


def dot(a, b):
    return lax.dot_general(a, b, (((1,), (0,)), ((), ())), preferred_element_type=F32)


def dot_nt(a, b):
    return lax.dot_general(a, b, (((1,), (1,)), ((), ())), preferred_element_type=F32)


def dot_tn(a, b):
    return lax.dot_general(a, b, (((0,), (0,)), ((), ())), preferred_element_type=F32)


def params(mib, flops=0, moved=0, **more):
    return dict(
        compiler_params=pltpu.CompilerParams(vmem_limit_bytes=int(mib * MB), **more),
        cost_estimate=pl.CostEstimate(
            flops=int(flops), bytes_accessed=int(moved), transcendentals=0
        ),
    )


class Order:
    deps = ()


def ordered(body, *, in_specs, out_specs, out_shape, scratch_shapes=(), **more):
    single = not isinstance(out_shape, (list, tuple))
    specs, shapes = ([out_specs], [out_shape]) if single else (list(out_specs), list(out_shape))
    deps, n_in, n_out = Order.deps, len(in_specs), len(shapes)

    def wrapped(*refs):
        rest = refs[n_in + len(deps) :]
        body(*refs[:n_in], *rest[:n_out], *rest[n_out + 1 :])
        rest[n_out][...] = jnp.zeros((8, 128), F32)

    mark = VMEM if more.get("grid") is None else pl.BlockSpec((8, 128), lambda *at: (0, 0))
    call = pl.pallas_call(
        wrapped,
        in_specs=[*in_specs, *[ANY] * len(deps)],
        out_specs=[*specs, mark],
        out_shape=[*shapes, jax.ShapeDtypeStruct((8, 128), F32)],
        scratch_shapes=list(scratch_shapes),
        **more,
    )

    def run(*args):
        *out, token = call(*args, *deps)
        Order.deps = (token,)
        return out[0] if single else out

    return run


class Group:
    def __init__(self, arrays, pieces):
        self.arrays = tuple(arrays)
        self.pieces = tuple(pieces)


def row_of(spec, rows, me):
    if spec[0] == "at":
        return spec[1]
    return pl.multiple_of((me ^ spec[1]) * rows, rows)


def weight_copies(group, refs, first, count, dst, sems, me):
    copies = []
    for n, (array, lead, rows, spec) in enumerate(group.pieces):
        src = refs[array].at[lead + (pl.ds(first, count),)]
        copies.append(
            pltpu.make_async_copy(src, dst.at[:, pl.ds(row_of(spec, rows, me), rows)], sems.at[n])
        )
    return copies


def grad_copies(plan, refs, first, count, src, sems, me):
    blocks = pl.ds(first, count)
    return [
        pltpu.make_async_copy(
            src.at[blocks, pl.ds(row_of(spec, rows, me), rows)], refs[array].at[lead + (blocks,)], sems.at[n]
        )
        for n, (array, lead, rows, spec) in enumerate(plan)
    ]


def norms_of(x):
    mean = jnp.mean(x, axis=-1, keepdims=True)
    centred = x - mean
    scale = lax.rsqrt(jnp.mean(centred * centred, axis=-1, keepdims=True) + norm_epsilon)
    return centred * scale, scale


def layer_norms(tokens, vectors, deps=()):
    rows = tokens.shape[0]
    tile = 256

    def body(x_ref, v_ref, *rest):
        one_ref, two_ref = rest[len(deps) :]
        xhat, _ = norms_of(x_ref[...].astype(F32))
        one_ref[...] = (xhat * v_ref[0:1] + v_ref[1:2]).astype(BF)
        two_ref[...] = (xhat * v_ref[2:3] + v_ref[3:4]).astype(BF)

    spec = pl.BlockSpec((tile, D), lambda t: (t, 0))
    return ordered(
        body,
        grid=(rows // tile,),
        in_specs=[spec, pl.BlockSpec(vectors.shape, lambda t: (0, 0))] + [ANY] * len(deps),
        out_specs=[spec, spec],
        out_shape=[jax.ShapeDtypeStruct((rows, D), BF)] * 2,
        **params(16, 20 * rows * D, 6 * rows * D),
    )(tokens, vectors, *deps)


def pack_owned(here, owners, masters, blocks):
    rows = masters.shape[1]
    nb = len(blocks)

    def body(h_ref, o_ref, m_ref, out, stage, sems):
        copies, mine = [], []
        for i, b in enumerate(blocks):
            owner = o_ref[b]
            slot = jnp.int32(0)
            for before in range(b):
                slot = slot + (o_ref[before] == owner).astype(jnp.int32)
            mine.append(owner == h_ref[0])
            copies.append(pltpu.make_async_copy(m_ref.at[slot], stage.at[i], sems.at[i]))
            copies[-1].start()
        for i in range(nb):
            copies[i].wait()
            out[i] = jnp.where(mine[i], stage[i], 0.0).astype(BF)

    return ordered(
        body,
        in_specs=[SMEM, SMEM, ANY],
        out_specs=VMEM,
        out_shape=jax.ShapeDtypeStruct((nb, rows, D), BF),
        scratch_shapes=[pltpu.VMEM((nb, rows, D), F32), pltpu.SemaphoreType.DMA((nb,))],
        **params(16, 1, 1),
    )(here, owners, masters)


def gelu_pair(z):
    size = jnp.abs(z)
    t = pl.reciprocal(1.0 + (0.3275911 * 0.7071067811865476) * size)
    bell = jnp.exp2((-0.5 * LOG2E) * (z * z))
    poly = 0.5 * 1.061405429
    for c in (-1.453152027, 1.421413741, -0.284496736, 0.254829592):
        poly = poly * t + 0.5 * c
    tail = poly * t * bell
    cdf = jnp.where(z >= 0.0, 1.0 - tail, tail)
    return z * cdf, cdf + z * (bell * 0.3989422804014327)


def mlp_chunk(me, h_two, cot, bias, group, first, outs, plan, deps=()):
    rows = h_two.shape[0]
    part = 256
    parts = rows // part
    na, no, nd = len(group.arrays), len(outs), len(deps)
    n_in, n_out = len(group.pieces), len(plan)

    def body(me_ref, h_ref, y_ref, b_ref, *rest):
        w_refs, rest = rest[:na], rest[na + nd :]
        act_ref, dz_ref, db_ref = rest[:3]
        o_refs = rest[3 : 3 + no]
        h, y, w, act, dz, low, in_sem, t_sem, out_sem = rest[3 + no :]
        me_id = me_ref[0]
        at = [pl.ds(p * part, part) for p in range(parts)]
        loads = weight_copies(group, w_refs, first, 2, w, in_sem, me_id)
        tokens = [
            [
                pltpu.make_async_copy(src.at[at[p]], dst.at[at[p]], t_sem.at[n, p])
                for n, (src, dst) in enumerate(((h_ref, h), (y_ref, y)))
            ]
            for p in range(parts)
        ]
        for c in loads:
            c.start()
        for pair in tokens:
            for c in pair:
                c.start()
        for c in loads:
            c.wait()
        for pair in tokens:
            for c in pair:
                c.wait()
        stores, z, u, sums = [], {}, {}, []

        def into(p):
            z[p] = dot(h[at[p]], w[0]) + b_ref[...]
            u[p] = dot_nt(y[at[p]], w[1])

        def slopes(p):
            value, slope = gelu_pair(z[p])
            act[at[p]] = value.astype(BF)
            low_dz = (u[p] * slope).astype(BF)
            dz[at[p]] = low_dz
            sums.append(jnp.sum(low_dz.astype(F32), axis=0, keepdims=True))
            for n, (src, dst) in enumerate(((act, act_ref), (dz, dz_ref))):
                stores.append(pltpu.make_async_copy(src.at[at[p]], dst.at[at[p]], t_sem.at[2 + n, p]))
                stores[-1].start()

        for turn in range(parts + 1):
            if turn < parts:
                into(turn)
            if turn:
                slopes(turn - 1)
        for i, (left, right) in enumerate(((h, dz), (act, y))):
            low[i] = dot_tn(left[...], right[...]).astype(BF)
        for c in grad_copies(plan, o_refs, 0, 2, low, out_sem, me_id):
            c.start()
            stores.append(c)
        db_ref[...] = sum(sums[1:], sums[0])
        for c in stores:
            c.wait()

    act, dz, db, *grads = ordered(
        body,
        in_specs=[SMEM, HBM, HBM, VMEM] + [HBM] * na + [ANY] * nd,
        out_specs=[HBM, HBM, VMEM] + [HBM] * no,
        out_shape=[
            jax.ShapeDtypeStruct((rows, D), BF),
            jax.ShapeDtypeStruct((rows, D), BF),
            jax.ShapeDtypeStruct((1, D), F32),
            *outs,
        ],
        scratch_shapes=[
            pltpu.VMEM((rows, D), BF),
            pltpu.VMEM((rows, D), BF),
            pltpu.VMEM((2, D, D), BF),
            pltpu.VMEM((rows, D), BF),
            pltpu.VMEM((rows, D), BF),
            pltpu.VMEM((2, D, D), BF),
            pltpu.SemaphoreType.DMA((n_in,)),
            pltpu.SemaphoreType.DMA((4, parts)),
            pltpu.SemaphoreType.DMA((n_out,)),
        ],
        **params(60, 8 * rows * D * D, 16 * rows * D),
    )(me, h_two, cot, bias, *group.arrays, *deps)
    return act, dz, db, grads


def turned(x, cosine, from_right, from_left):
    return (
        x * cosine
        + pltpu.roll(x, 128 - ROT // 2, 1) * from_right
        + pltpu.roll(x, ROT // 2, 1) * from_left
    )


def lanes_of(cosine, sine):
    half = ROT // 2
    lane = lax.broadcasted_iota(jnp.int32, (half, 128), 1) % HEAD
    row = lax.broadcasted_iota(jnp.int32, (half, 128), 0)
    one, two = (lane == row).astype(F32), (lane == row + half).astype(F32)

    def spread(values, mask):
        return lax.dot_general(
            values, mask, (((0,), (0,)), ((), ())), precision=lax.Precision.HIGHEST, preferred_element_type=F32
        )

    still = (lax.broadcasted_iota(jnp.int32, (1, 128), 1) % HEAD >= ROT).astype(F32)
    return spread(cosine, one + two) + still, spread(sine, one), spread(sine, two)


def project(me, h_one, cot, bias, cosine, sine, group, deps=()):
    rows = h_one.shape[0]
    tile = 256
    per = cosine.shape[2] // tile
    na, n_in = len(group.arrays), len(group.pieces)

    def body(me_ref, h_ref, y_ref, b_ref, c_ref, s_ref, *rest):
        w_refs, rest = rest[:na], rest[na + len(deps) :]
        outs = rest[:4]
        w_all, sems = rest[4:]
        step = pl.program_id(0)

        @pl.when(step == 0)
        def _():
            copies = weight_copies(group, w_refs, 0, 4, w_all, sems, me_ref[0])
            for c in copies:
                c.start()
            for c in copies:
                c.wait()

        cos_l, right, left = lanes_of(c_ref[0], s_ref[0])
        outs[3][...] = dot_nt(y_ref[...], w_all[3]).astype(BF)
        for i in range(3):
            value = dot(h_ref[...], w_all[i]) + b_ref[i : i + 1]
            if i == 2:
                outs[2][...] = value.astype(BF)
                continue
            for j in range(D // 128):
                outs[i][:, j * 128 : (j + 1) * 128] = turned(
                    value[:, j * 128 : (j + 1) * 128], cos_l, -right, left
                ).astype(BF)

    spec = pl.BlockSpec((tile, D), lambda t: (t, 0))
    table = pl.BlockSpec((1, ROT // 2, tile), lambda t: (t // per, 0, t % per))
    return ordered(
        body,
        grid=(rows // tile,),
        in_specs=[SMEM, spec, spec, pl.BlockSpec((3, D), lambda t: (0, 0)), table, table]
        + [HBM] * na
        + [ANY] * len(deps),
        out_specs=[spec] * 4,
        out_shape=[jax.ShapeDtypeStruct((rows, D), BF)] * 4,
        scratch_shapes=[pltpu.VMEM((4, D, D), BF), pltpu.SemaphoreType.DMA((n_in,))],
        **params(60, 8 * rows * D * D, 20 * rows * D),
    )(me, h_one, cot, bias, cosine, sine, *group.arrays, *deps)


def attention(q, k, v, da, starts, cosine, sine, length, which, into=(), deps=()):
    rows = q.shape[0]
    seqs = len(which)
    half = length // 2
    pair = 128

    def body(q_ref, k_ref, v_ref, d_ref, st_ref, hc_ref, hs_ref, *rest):
        a_ref, dq_ref, dk_ref, dv_ref, db_ref, mask, wheel = rest[len(into) + len(deps) :]

        @pl.when(pl.program_id(1) == 0)
        def _():
            key = lax.broadcasted_iota(jnp.int32, (length, length), 0)
            query = lax.broadcasted_iota(jnp.int32, (length, length), 1)
            seen = (key <= query) & (key >= st_ref[0])
            mask[...] = jnp.where(seen, 0.0, masked_fill)
            wheel[0], wheel[1], wheel[2] = lanes_of(hc_ref[0], hs_ref[0])

        q_all, k_all, v_all, d_all = q_ref[...], k_ref[...], v_ref[...], d_ref[...]
        vt, kt = v_all.T, k_all.T
        dt = d_all.T.astype(F32)
        lane = lax.broadcasted_iota(jnp.int32, (length, pair), 1)
        zero = jnp.zeros((), BF)
        dv = [jnp.zeros((half, pair), F32)] * 2
        dk = [jnp.zeros((half, pair), F32)] * 2
        jobs = []
        for h in range(2):
            mine = (lane >= h * HEAD) & (lane < (h + 1) * HEAD)
            qm = jnp.where(mine, q_all, zero)
            dm = jnp.where(mine, d_all, zero)
            for b in range(2):
                jobs.append((h, b, qm[b * half : (b + 1) * half], dm[b * half : (b + 1) * half]))
        raw, dp, prob, low, at, ds, dqt = {}, {}, {}, {}, {}, {}, {}

        def scores(i):
            h, b, qm, dm = jobs[i]
            n = half * (b + 1)
            raw[i] = dot_nt(k_all[:n], qm)
            dp[i] = dot_nt(v_all[:n], dm)

        def softmax(i):
            h, b, qm, dm = jobs[i]
            n = half * (b + 1)
            s = raw[i] * (HEAD**-0.5 * LOG2E) + mask[:n, b * half : (b + 1) * half]
            e = jnp.exp2(s - jnp.max(s, axis=0, keepdims=True))
            prob[i] = e * (1.0 / jnp.sum(e, axis=0, keepdims=True))
            low[i] = prob[i].astype(BF)
            at[i] = dot(vt[h * HEAD : (h + 1) * HEAD, :n], low[i])

        def slopes(i):
            h, b, qm, dm = jobs[i]
            dh = dt[h * HEAD : (h + 1) * HEAD, b * half : (b + 1) * half]
            total = jnp.sum(dh * at[i], axis=0, keepdims=True)
            ds[i] = (prob[i] * (dp[i] - total)).astype(BF)

        def grads(i):
            h, b, qm, dm = jobs[i]
            n = half * (b + 1)
            dqt[i] = dot(kt[h * HEAD : (h + 1) * HEAD, :n], ds[i])
            more_v, more_k = dot(low[i], dm), dot(ds[i], qm)
            for c in range(b + 1):
                dv[c] = dv[c] + more_v[c * half : (c + 1) * half]
                dk[c] = dk[c] + more_k[c * half : (c + 1) * half]

        stages = (scores, softmax, slopes, grads)
        for turn in range(len(jobs) + len(stages) - 1):
            for n, stage in reversed(list(enumerate(stages))):
                if 0 <= turn - n < len(jobs):
                    stage(turn - n)
        at_h, dq_h = [], []
        for h in range(2):
            at_h.append(jnp.concatenate([at[2 * h], at[2 * h + 1]], axis=1))
            dq = jnp.concatenate([dqt[2 * h], dqt[2 * h + 1]], axis=1) * HEAD**-0.5
            u, w, cos, sin = dq[0:8], dq[8:16], hc_ref[0], hs_ref[0]
            dq_h.append(jnp.concatenate([u * cos + w * sin, w * cos - u * sin, dq[16:]], axis=0))
        a_ref[...] = jnp.concatenate(at_h, axis=0).astype(BF).T
        dq = jnp.concatenate(dq_h, axis=0).astype(BF).T
        dq_ref[...] = dq
        sums = [jnp.sum(dq.astype(F32), axis=0, keepdims=True)]
        sum_k = sum_v = jnp.zeros((1, pair), F32)
        for c in range(2):
            at_k = slice(c * half, (c + 1) * half)
            back = turned(dk[c] * HEAD**-0.5, wheel[0, at_k], wheel[1, at_k], -wheel[2, at_k]).astype(BF)
            dk_ref[at_k] = back
            sum_k = sum_k + jnp.sum(back.astype(F32), axis=0, keepdims=True)
            value = dv[c].astype(BF)
            dv_ref[at_k] = value
            sum_v = sum_v + jnp.sum(value.astype(F32), axis=0, keepdims=True)
        db_ref[0] = jnp.concatenate(sums + [sum_k, sum_v], axis=0)

    base = which[0]
    spec = pl.BlockSpec((length, pair), lambda s, h: (s + base, h))
    table = pl.BlockSpec((1, ROT // 2, length), lambda s, h: (s + base, 0, 0))
    a, dq, dk, dv, db = ordered(
        body,
        grid=(seqs, D // pair),
        in_specs=[spec] * 4
        + [pl.BlockSpec((1, 1, length), lambda s, h: (s + base, 0, 0)), table, table]
        + [ANY] * (len(into) + len(deps)),
        out_specs=[spec, spec, spec, spec, pl.BlockSpec((1, 3, pair), lambda s, h: (s, 0, h))],
        out_shape=[jax.ShapeDtypeStruct((rows, D), BF)] * 4
        + [jax.ShapeDtypeStruct((seqs, 3, D), F32)],
        scratch_shapes=[pltpu.VMEM((length, length), F32), pltpu.VMEM((3, length, 128), F32)],
        input_output_aliases={7 + n: n for n in range(len(into))},
        **params(60, 10e9 * seqs, 20 * rows * D),
    )(q, k, v, da, starts, cosine, sine, *into, *deps)
    return a, dq, dk, dv, db


def attention_grads(me, h_one, a, cot, dqkv, outs, plan, deps=()):
    rows = h_one.shape[0]
    no, n_out = len(outs), len(plan)

    def body(me_ref, h_ref, a_ref, y_ref, dq_ref, dk_ref, dv_ref, *rest):
        rest = rest[len(deps) :]
        o_refs = rest[:no]
        low, sems = rest[no:]
        pending = []
        for i, (left, right) in enumerate(
            ((h_ref, dq_ref), (h_ref, dk_ref), (h_ref, dv_ref), (a_ref, y_ref))
        ):
            low[i] = dot_tn(left[...], right[...]).astype(BF)
            if i % 2:
                copies = grad_copies(plan, o_refs, i - 1, 2, low, sems.at[i // 2], me_ref[0])
                for c in copies:
                    c.start()
                pending += copies
        for c in pending:
            c.wait()

    whole = pl.BlockSpec(memory_space=pltpu.VMEM)
    return ordered(
        body,
        in_specs=[SMEM] + [whole] * 6 + [ANY] * len(deps),
        out_specs=[HBM] * no,
        out_shape=list(outs),
        scratch_shapes=[pltpu.VMEM((4, D, D), BF), pltpu.SemaphoreType.DMA((2, n_out))],
        **params(60, 8 * rows * D * D, 12 * rows * D),
    )(me, h_one, a, cot, *dqkv, *deps)


def products(me, jobs, tail, outs, starts=None, extra=(), deps=(), mib=60):
    starts = starts or [()] * len(jobs)
    rows = jobs[0][0][0].shape[0]
    tile = 256
    groups, used = [], {}
    for job in jobs:
        for _, (group, i), _ in job:
            if id(group) not in used:
                groups.append(group)
                used[id(group)] = []
            used[id(group)].append(i)
    first, flat, runs, slot, at = {}, [], [], {}, 0
    for group in groups:
        first[id(group)] = len(flat)
        flat += list(group.arrays)
        low, high = min(used[id(group)]), max(used[id(group)])
        runs.append((group, low, high - low + 1, at))
        for i in range(low, high + 1):
            slot[id(group), i] = at
            at += 1
    lefts = [left for job in jobs for left, _, _ in job]
    begun = [x for group in starts for x in group]
    n_in = max(len(g.pieces) for g in groups)
    nl, ns, ne, nw, no = len(lefts), len(begun), len(extra), len(flat), len(outs)

    def body(me_ref, *rest):
        l_refs, rest = rest[:nl], rest[nl:]
        s_refs, rest = list(rest[:ns]), rest[ns:]
        e_refs, rest = rest[:ne], rest[ne:]
        w_refs, rest = rest[:nw], rest[nw + len(deps) :]
        o_refs, (w_all, sems) = rest[:no], rest[no:]
        step = pl.program_id(0)

        @pl.when(step == 0)
        def _():
            copies = []
            for n, (group, low, count, to) in enumerate(runs):
                refs = w_refs[first[id(group)] :]
                copies += weight_copies(
                    group, refs, low, count, w_all.at[pl.ds(to, count)], sems.at[n], me_ref[0]
                )
            for c in copies:
                c.start()
            for c in copies:
                c.wait()

        results, n = [], 0
        for job, begin in zip(jobs, starts):
            total = None
            for _ in begin:
                more = s_refs.pop(0)[...]
                total = more if total is None else total + more
            for _, (group, i), transposed in job:
                term = (dot_nt if transposed else dot)(l_refs[n][...], w_all[slot[id(group), i]])
                total = term if total is None else total + term
                n += 1
            results.append(total)
        tail(e_refs, results, o_refs, step)

    spec = pl.BlockSpec((tile, D), lambda t: (t, 0))

    def whole(x):
        return pl.BlockSpec(x.shape, lambda t: (0,) * len(x.shape))

    return ordered(
        body,
        grid=(rows // tile,),
        in_specs=[SMEM]
        + [spec] * (nl + ns)
        + [spec if per_token else whole(x) for x, per_token in extra]
        + [HBM] * nw
        + [ANY] * len(deps),
        out_specs=[spec if x.shape[0] == rows else whole(x) for x in outs],
        out_shape=list(outs),
        scratch_shapes=[pltpu.VMEM((at, D, D), BF), pltpu.SemaphoreType.DMA((len(runs), n_in))],
        **params(mib, 2 * nl * rows * D * D, (2 * nl + 8) * rows * D),
    )(me, *lefts, *begun, *[x for x, _ in extra], *flat, *deps)


def store_all(e_refs, results, o_refs, step):
    for ref, value in zip(o_refs, results):
        ref[...] = value


def add_rows(ref, terms, step):
    sums = jnp.concatenate([jnp.sum(term, axis=0, keepdims=True) for term in terms], axis=0)

    @pl.when(step == 0)
    def _():
        ref[...] = sums

    @pl.when(step > 0)
    def _():
        ref[...] += sums


def middle_tail(e_refs, results, o_refs, step):
    x_ref, y_ref, v_ref = e_refs
    out_ref, e_ref, sum_ref = o_refs
    out, d_one, d_two = results
    x = x_ref[...].astype(F32)
    out_ref[...] = out + x + (v_ref[7:8] + v_ref[8 + SPREAD : 9 + SPREAD])
    xhat, _ = norms_of(x)
    e_ref[...] = d_one * v_ref[0:1] + d_two * v_ref[2:3]
    add_rows(sum_ref, (d_one * xhat, d_one, d_two * xhat, d_two, y_ref[...].astype(F32)), step)


def last_tail(e_refs, results, o_refs, step):
    x_ref, y_ref, v_ref, e_ref = e_refs
    out_ref, grad_ref, sum_ref = o_refs
    out, d_two = results
    out_ref[...] = out.astype(BF)
    xhat, scale = norms_of(x_ref[...].astype(F32))
    e = e_ref[...] + d_two * v_ref[2:3]
    inner = jnp.mean(e * xhat, axis=-1, keepdims=True)
    y = y_ref[...].astype(F32)
    grad_ref[...] = y + (e - jnp.mean(e, axis=-1, keepdims=True) - xhat * inner) * scale
    add_rows(sum_ref, (d_two * xhat, d_two), step)


def adam(gradient, weight, moment, square, rate, decay, one_fix, two_fix):
    moment_new = beta_first * moment + (1.0 - beta_first) * gradient
    square_new = beta_second * square + (1.0 - beta_second) * gradient * gradient
    update = (moment_new * one_fix) / (jnp.sqrt(square_new * two_fix) + adam_epsilon)
    return weight - rate * (update + decay * weight), moment_new, square_new


def update_all(source, fixes, squares, vector_total, vector_state, summed, masters, firsts, seconds):
    slots, rows, _ = masters.shape
    ng = len(summed)

    def body(src_ref, fix_ref, q_ref, t_ref, vw_ref, vm_ref, vv_ref, *rest):
        g_refs, (w_ref, m_ref, v_ref) = rest[:ng], rest[ng : ng + 3]
        norm_out, tg_out, tw_out, tm_out, tv_out, g_out, w_out, m_out, v_out, c_out, clip_ref = rest[ng + 3 :]
        slot = pl.program_id(0)
        one_fix, two_fix = fix_ref[0], fix_ref[1]

        @pl.when(slot == 0)
        def _():
            t = t_ref[...]
            norm = jnp.sqrt(jnp.sum(q_ref[...], keepdims=True) + jnp.sum(t * t, keepdims=True))
            clip = jnp.minimum(1.0, 1.0 / (norm + 1e-06))
            norm_out[...] = norm
            clip_ref[...] = jnp.broadcast_to(clip, clip_ref.shape)
            gradient = t * clip
            new, moment, square = adam(
                gradient, vw_ref[...], vm_ref[...], vv_ref[...], vector_rate, 0.0, one_fix, two_fix
            )
            tg_out[...], tw_out[...], tm_out[...], tv_out[...] = gradient, new, moment, square

        keep = src_ref[2, slot] > 0
        low = g_refs[0][0]
        for n in range(1, ng):
            low = jnp.where(src_ref[0, slot] == n, g_refs[n][0], low)
        gradient = low.astype(F32) * clip_ref[0:1, 0:1]
        new, moment, square = adam(
            gradient, w_ref[0], m_ref[0], v_ref[0], learn_rate, weight_decay, one_fix, two_fix
        )
        new = jnp.where(keep, new, 0.0)
        g_out[0] = jnp.where(keep, gradient, 0.0)
        w_out[0] = new
        m_out[0] = jnp.where(keep, moment, 0.0)
        v_out[0] = jnp.where(keep, square, 0.0)
        c_out[0] = new.astype(BF)

    def whole(shape):
        return pl.BlockSpec(shape, lambda s, src, fix: (0,) * len(shape))

    def picked(n):
        return pl.BlockSpec(
            (1, rows, D), lambda s, src, fix: (jnp.where(src[0, s] == n, src[1, s], 0), 0, 0)
        )

    own = pl.BlockSpec((1, rows, D), lambda s, src, fix: (s, 0, 0))
    vec = vector_total.shape
    return pl.pallas_call(
        body,
        grid_spec=pltpu.PrefetchScalarGridSpec(
            num_scalar_prefetch=2,
            grid=(slots,),
            in_specs=[whole((8, 128))] + [whole(vec)] * 4 + [picked(n) for n in range(ng)] + [own] * 3,
            out_specs=[whole((1, 1))] + [whole(vec)] * 4 + [own] * 5,
            scratch_shapes=[pltpu.VMEM((8, 128), F32)],
        ),
        out_shape=[jax.ShapeDtypeStruct((1, 1), F32)]
        + [jax.ShapeDtypeStruct(vec, F32)] * 4
        + [jax.ShapeDtypeStruct((slots, rows, D), F32)] * 4
        + [jax.ShapeDtypeStruct((slots, rows, D), BF)],
        **params(24, 20 * slots * rows * D, 32 * slots * rows * D),
    )(source, fixes, squares, vector_total, *vector_state, *summed, masters, firsts, seconds)


def stacked(pieces, deps=()):
    count = len(pieces)

    def body(*refs):
        out, sems = refs[count + len(deps) :]
        copies = [pltpu.make_async_copy(refs[n], out.at[n], sems.at[n]) for n in range(count)]
        for c in copies:
            c.start()
        for c in copies:
            c.wait()

    return ordered(
        body,
        in_specs=[ANY] * (count + len(deps)),
        out_specs=VMEM,
        out_shape=jax.ShapeDtypeStruct((count, *pieces[0].shape), pieces[0].dtype),
        scratch_shapes=[pltpu.SemaphoreType.DMA((count,))],
        **params(16, 1, 1),
    )(*pieces, *deps)


def pair_sums(pairs, deps=()):
    chips, each, rows, _ = pairs[0][0].shape
    count = len(pairs)

    def body(*refs):
        outs = refs[2 * count + len(deps) :]
        for n in range(chips):

            @pl.when(pl.program_id(0) == n)
            def _(n=n):
                for i in range(count):
                    keep, got = refs[2 * i], refs[2 * i + 1]
                    outs[n][i * each : (i + 1) * each] = (keep[0].astype(F32) + got[0].astype(F32)).astype(BF)

    spec = pl.BlockSpec((1, each, rows, D), lambda n: (n, 0, 0, 0))
    one = (count * each, rows, D)
    return ordered(
        body,
        grid=(chips,),
        in_specs=[spec] * (2 * count) + [ANY] * len(deps),
        out_specs=[pl.BlockSpec(one, lambda n: (0, 0, 0))] * chips,
        out_shape=[jax.ShapeDtypeStruct(one, BF)] * chips,
        **params(16, 1, 1),
    )(*[x for pair in pairs for x in pair], *deps)


def total_of(*groups):
    flat = [x for group in groups for x in group]
    _, rows, _ = flat[0].shape
    blocks = sum(group[0].shape[0] for group in groups)

    def body(*refs):
        out, n, at = refs[len(flat)], 0, 0
        for group in groups:
            total = refs[n][...].astype(F32)
            for ref in refs[n + 1 : n + len(group)]:
                total = total + ref[...].astype(F32)
            out[at : at + total.shape[0]] = total.astype(BF)
            n, at = n + len(group), at + total.shape[0]

    return ordered(
        body,
        in_specs=[VMEM] * len(flat),
        out_specs=VMEM,
        out_shape=jax.ShapeDtypeStruct((blocks, rows, D), BF),
        **params(16, 1, 1),
    )(*flat)


def handed_on(value):
    def body(value_ref, out):
        pass

    return ordered(
        body,
        in_specs=[ANY],
        out_specs=ANY,
        out_shape=jax.ShapeDtypeStruct(value.shape, value.dtype),
        input_output_aliases={0: 0},
        **params(1, 1, 1),
    )(value)


def vector_terms(sums, last_sums, db_a, db_b, dbs):
    def body(s_ref, l_ref, a_ref, b_ref, *rest):
        out = rest[SPREAD]
        out[0:2] = s_ref[0:2]
        out[2:4] = s_ref[2:4] + l_ref[...]
        qkv = a_ref[0] + b_ref[0]
        for n in range(1, a_ref.shape[0]):
            qkv = qkv + (a_ref[n] + b_ref[n])
        out[4:7] = qkv
        out[7:8] = s_ref[4:5]
        for n in range(SPREAD):
            out[8 + n : 9 + n] = rest[n][...]
        out[8 + SPREAD : 9 + SPREAD] = s_ref[4:5]

    return ordered(
        body,
        in_specs=[VMEM] * (4 + SPREAD),
        out_specs=VMEM,
        out_shape=jax.ShapeDtypeStruct((9 + SPREAD, D), F32),
        **params(16, 1, 1),
    )(sums, last_sums, db_a, db_b, *dbs)


def plus(a, b):
    def body(a_ref, b_ref, out):
        out[...] = a_ref[...] + b_ref[...]

    return ordered(
        body,
        in_specs=[VMEM] * 2,
        out_specs=VMEM,
        out_shape=jax.ShapeDtypeStruct(a.shape, F32),
        **params(16, 1, 1),
    )(a, b)


def picked_end(here, value, outer):
    def body(h_ref, v_ref, o_ref, out):
        ends = (h_ref[0] == 0) | (h_ref[0] == 3)
        out[...] = jnp.where(ends, o_ref[...], v_ref[...])

    return ordered(
        body,
        in_specs=[SMEM, VMEM, VMEM],
        out_specs=VMEM,
        out_shape=jax.ShapeDtypeStruct(value.shape, BF),
        **params(16, 1, 1),
    )(here, value, outer)


def settled(value, other):
    count, rows, _ = value.shape

    def body(v_ref, o_ref, out_ref, q_ref):
        total = jnp.zeros((8, 128), F32)
        for n in range(count):
            low = (v_ref[n].astype(F32) + o_ref[n].astype(F32)).astype(BF)
            out_ref[n] = low
            x = low.astype(F32)
            x = x * x
            for c in range(D // 128):
                part = x[:, c * 128 : (c + 1) * 128]
                for r in range(rows // 8):
                    total = total + part[r * 8 : (r + 1) * 8]
        q_ref[...] = total

    return ordered(
        body,
        in_specs=[VMEM, VMEM],
        out_specs=[VMEM, VMEM],
        out_shape=[jax.ShapeDtypeStruct(value.shape, BF), jax.ShapeDtypeStruct((8, 128), F32)],
        **params(16, 1, 1),
    )(value, other)


def swap(value, axis, bit):
    size = lax.axis_size(axis)
    return lax.ppermute(value, axis, [(i, i ^ bit) for i in range(size)])


CORE, SIDE, UP = 1, 2, 4
CHIPS = (0, SIDE, UP, SIDE | UP)


INWARD, ACROSS, OUTWARD = [(0, 1), (3, 2)], [(1, 2), (2, 1)], [(1, 0), (2, 3)]


def hop(value, pairs):
    if lax.axis_size("narrow") == 4:
        return lax.ppermute(value, "narrow", pairs)
    if pairs is INWARD:
        return (lax.psum(value.astype(F32), "narrow") - value.astype(F32)).astype(BF)
    return jnp.zeros_like(value) if pairs is ACROSS else value


def near(value):
    if lax.axis_size("narrow") == 4:
        return swap(value, "narrow", 1)
    return (lax.psum(value.astype(F32), "narrow") - value.astype(F32)).astype(BF)


def far(value):
    return swap(value, "narrow", 2) if lax.axis_size("narrow") == 4 else jnp.zeros_like(value)


def spread_wide(value):
    if lax.axis_size("wide") == 8:
        return [swap(value, "wide", m) for m in CHIPS[1:]]
    return None


def gather_wide(value):
    size = lax.axis_size("wide")
    count, rows, _ = value.shape
    full = lax.all_gather(value, "wide", axis=0, tiled=False)
    if rows % 16:
        full = jnp.swapaxes(full, 0, 1).reshape(1, count, D, D)
        size, rows = 1, D
    return Group((full,), [(0, (p,), rows, ("at", rows * p)) for p in range(size)])


def grad_layout(count, rows, size):
    if size != 8:
        return [jax.ShapeDtypeStruct((count, D, D), BF)], [(0, (), D, ("at", 0))]
    shape = jax.ShapeDtypeStruct((4, count, rows, D), BF)
    keep = [(0, (n,), rows, ("xor", m)) for n, m in enumerate(CHIPS)]
    give = [(1, (n,), rows, ("xor", m ^ CORE)) for n, m in enumerate(CHIPS)]
    return [shape] * 2, keep + give


def gathered(shard, parts):
    if parts is None:
        return gather_wide(shard)
    mine = stacked([shard, *parts])
    other = swap(mine, "wide", CORE)
    rows = shard.shape[1]
    masks = [(m, 0) for m in CHIPS] + [(m ^ CORE, 1) for m in CHIPS]
    return Group((mine, other), [(a, (n % 4,), rows, ("xor", m)) for n, (m, a) in enumerate(masks)])


def give(grads):
    if len(grads) == 1:
        return lax.psum_scatter(grads[0], "wide", scatter_dimension=1, tiled=True)
    return grads[0], swap(grads[1], "wide", CORE)


def exchange(*given):
    if not isinstance(given[0], tuple):
        return [given[0] if len(given) == 1 else jnp.concatenate(given, axis=0)]
    parts = pair_sums(list(given))
    return [parts[0]] + [swap(p, "wide", m) for p, m in zip(parts[1:], CHIPS[1:])]


def total_axis(value, axis):
    size = lax.axis_size(axis)
    bit = 1
    while bit < size:
        value = value + swap(value, axis, bit)
        bit *= 2
    return value


def slot_table(owners, capacity):
    number = owners.shape[0]
    order = jnp.arange(number, dtype=jnp.int32)
    before = (owners[:, None] == owners[None, :]) & (order[None, :] < order[:, None])
    return owners * capacity + jnp.sum(before.astype(jnp.int32), axis=1)


def per_device(tokens, doc_lengths, cotangent, owners, step_count, master, moment_one, moment_two, vectors, vector_one, vector_two):
    rows, capacity, _ = master.shape
    seqs = doc_lengths.shape[0]
    length = tokens.shape[0] // seqs
    blocks = owners.shape[0]
    wide = lax.axis_size("wide")
    narrow_index = lax.axis_index("narrow")
    me = lax.axis_index("wide").astype(jnp.int32).reshape(1)
    masters, firsts, seconds = [jnp.swapaxes(m, 0, 1) for m in (master, moment_one, moment_two)]

    here = narrow_index.astype(jnp.int32).reshape(1)
    local = slot_table(owners, capacity) - owners * capacity
    ends = jnp.cumsum(doc_lengths, axis=1)
    position = jnp.arange(length, dtype=jnp.int32)
    passed = position[None, None, :] >= ends[:, :, None]
    start = jnp.sum(jnp.where(passed, doc_lengths[:, :, None], 0), axis=1)
    freqs = jnp.power(rope_base, -2.0 * jnp.arange(ROT // 2, dtype=F32) / ROT)
    angle = (position[None] - start).astype(F32)[:, None, :] * freqs[None, :, None]
    cosine, sine = jnp.cos(angle), jnp.sin(angle)
    start = start[:, None, :]

    ids_0, ids_s, ids_t = (4, 8, 5, 9), (0, 1, 2, 3), (6, 10, 7, 11)
    pair_outs, pair_plan = grad_layout(2, rows, wide)
    four_outs, four_plan = grad_layout(4, rows, wide)
    full = jax.ShapeDtypeStruct(tokens.shape, F32)
    low = jax.ShapeDtypeStruct(tokens.shape, BF)
    acts, dzs, dbs, place = [], [], [], {}
    Order.deps = ()

    def arrived(group, ids):
        for i, b in enumerate(ids):
            place[b] = (group, i)

    def chunk(j):
        group, first = place[4 + j]
        act, dz, db, grads = mlp_chunk(
            me, h_two, cotangent, vectors[8 + j : 9 + j], group, first, pair_outs, pair_plan
        )
        acts.append(act)
        dzs.append(dz)
        dbs.append(db)
        return grads

    def forth(j):
        return (acts[j], place[8 + j], False)

    def back(j):
        return (dzs[j], place[4 + j], True)

    w_0 = pack_owned(here, owners, masters, ids_0)
    r_0 = hop(w_0, INWARD)
    h_one, h_two = layer_norms(tokens, vectors)
    w_0 = total_of([w_0, r_0])
    r_0 = hop(w_0, ACROSS)
    w_s = pack_owned(here, owners, masters, ids_s)
    r_s = hop(w_s, INWARD)
    w_0 = total_of([w_0, r_0])
    r_0 = hop(w_0, OUTWARD)
    w_s = total_of([w_s, r_s])
    r_s = hop(w_s, ACROSS)
    w_0 = picked_end(here, w_0, r_0)
    arrived(gather_wide(w_0), ids_0)
    w_t = pack_owned(here, owners, masters, ids_t)
    r_t = hop(w_t, INWARD)
    w_s = total_of([w_s, r_s])
    r_s = hop(w_s, OUTWARD)
    w_t = total_of([w_t, r_t])
    r_t = hop(w_t, ACROSS)
    w_s = picked_end(here, w_s, r_s)
    arrived(gather_wide(w_s), ids_s)
    w_t = total_of([w_t, r_t])
    r_t = hop(w_t, OUTWARD)
    s_0 = give(chunk(0))
    s_1 = give(chunk(1))
    w_t = picked_end(here, w_t, r_t)
    arrived(gather_wide(w_t), ids_t)
    front = exchange(s_0, s_1)
    q, k, v, da = project(me, h_one, cotangent, vectors[4:7], cosine, sine, place[0][0])
    half = seqs // 2
    *inner, db_a = attention(q, k, v, da, start, cosine, sine, length, tuple(range(half)))
    a, *dqkv, db_b = attention(
        q, k, v, da, start, cosine, sine, length, tuple(range(half, seqs)), into=inner
    )
    front = total_of(front)
    r_f = near(front)
    s_s = give(attention_grads(me, h_one, a, cotangent, dqkv, four_outs, four_plan))
    s_2 = give(chunk(2))
    front = total_of([front, r_f])
    r_f = far(front)
    mid = exchange(s_s)
    middle, e_part, sums = products(
        me,
        [
            [(a, place[3], False), forth(2)],
            [(dqkv[n], place[n], True) for n in range(3)],
            [back(2)],
        ],
        middle_tail,
        [full, full, jax.ShapeDtypeStruct((5, D), F32)],
        extra=[(tokens, True), (cotangent, True), (vectors, False)],
    )
    third = exchange(s_2)
    mid = total_of(mid)
    r_m = near(mid)
    s_3 = chunk(3)
    mid = total_of([mid, r_m])
    r_m = far(mid)
    front, front_square = settled(front, r_f)
    third = total_of(third)
    r_h = near(third)
    last = exchange(give([*s_3[:-1], handed_on(s_3[-1])]))
    early = products(me, [[forth(0), forth(1)], [back(0), back(1)]], store_all, [full, full])
    last = total_of(last)
    r_l = near(last)
    third = total_of([third, r_h])
    r_h = far(third)
    layer_out, input_grad, last_sums = products(
        me,
        [[forth(3)], [back(3)]],
        last_tail,
        [low, full, jax.ShapeDtypeStruct((2, D), F32)],
        starts=[(middle, early[0]), (early[1],)],
        extra=[(tokens, True), (cotangent, True), (vectors, False), (e_part, True)],
    )
    last = total_of([last, r_l])
    r_l = far(last)
    third, third_square = settled(third, r_h)
    mid, mid_square = settled(mid, r_m)
    vector_total = vector_terms(sums, last_sums, db_a, db_b, dbs)
    masks = [(axis, 1 << n) for axis in ("wide", "narrow") for n in range(lax.axis_size(axis).bit_length() - 1)]

    def vector_step(value):
        return plus(value, swap(value, *masks.pop(0)))

    while masks[0][0] == "wide":
        vector_total = vector_step(vector_total)
    last, last_square = settled(last, r_l)
    while masks:
        vector_total = vector_step(vector_total)
    squares = total_axis(front_square + mid_square + third_square + last_square, "wide")
    summed = (front, mid, third, last)
    held = ((4, 8, 5, 9), ids_s, (6, 10), (7, 11))
    step_float = step_count[0].astype(F32)
    fixes = jnp.stack(
        [1.0 / (1.0 - jnp.power(beta_first, step_float)), 1.0 / (1.0 - jnp.power(beta_second, step_float))]
    )
    slot = jnp.arange(capacity, dtype=jnp.int32)
    hit = ((owners == narrow_index)[None, :] & (local[None, :] == slot[:, None])).astype(jnp.int32)
    which, inner = [0] * blocks, [0] * blocks
    for n, ids in enumerate(held):
        for i, b in enumerate(ids):
            which[b], inner[b] = n, i
    source = jnp.stack(
        [
            jnp.sum(hit * jnp.array(which, jnp.int32)[None], axis=1),
            jnp.sum(hit * jnp.array(inner, jnp.int32)[None], axis=1),
            jnp.sum(hit, axis=1),
        ]
    )
    norm, vector_grads, new_vectors, vector_first, vector_second, *new = update_all(
        source, fixes, squares, vector_total, (vectors, vector_one, vector_two), summed, masters, firsts, seconds
    )
    block_grads, new_master, new_first, new_second, new_copies = [jnp.swapaxes(m, 0, 1) for m in new]
    return (
        layer_out,
        input_grad,
        norm[0, 0],
        block_grads,
        new_master,
        new_first,
        new_second,
        new_copies,
        vector_grads,
        new_vectors,
        vector_first,
        vector_second,
    )


def solution(mesh):
    tok = P(("wide", "narrow"), None)
    own = P("wide", "narrow", None)
    return jax.shard_map(
        per_device,
        mesh=mesh,
        in_specs=(tok, tok, tok, P(), P(), own, own, own, P(), P(), P()),
        out_specs=(tok, tok, P(), own, own, own, own, own, P(), P(), P(), P()),
        check_vma=False,
    )
```

```python
from functools import partial

import jax
import jax.numpy as jnp
from jax import lax
from jax.experimental import pallas as pl
from jax.experimental.pallas import tpu as pltpu
from jax.sharding import PartitionSpec as P

D = 768
HEADS = 12
HEAD = 64
ROT = 16
FF = 3072
SPREAD = FF // D

norm_epsilon = 1e-05
beta_first = 0.5
beta_second = 0.5
adam_epsilon = 1e-08
learn_rate = 0.02
vector_rate = 0.1
weight_decay = 0.1
masked_fill = -1e30
rope_base = 10000.0
LOG2E = 1.4426950408889634

BF = jnp.bfloat16
F32 = jnp.float32
MB = 1 << 20
ANY = pl.BlockSpec(memory_space=pl.ANY)
HBM = pl.BlockSpec(memory_space=pltpu.HBM)
SMEM = pl.BlockSpec(memory_space=pltpu.SMEM)
VMEM = pl.BlockSpec(memory_space=pltpu.VMEM)


def dot(a, b):
    return lax.dot_general(a, b, (((1,), (0,)), ((), ())), preferred_element_type=F32)


def dot_nt(a, b):
    return lax.dot_general(a, b, (((1,), (1,)), ((), ())), preferred_element_type=F32)


def dot_tn(a, b):
    return lax.dot_general(a, b, (((0,), (0,)), ((), ())), preferred_element_type=F32)


def params(mib, flops=0, moved=0, **more):
    return dict(
        compiler_params=pltpu.CompilerParams(vmem_limit_bytes=int(mib * MB), **more),
        cost_estimate=pl.CostEstimate(
            flops=int(flops), bytes_accessed=int(moved), transcendentals=0
        ),
    )


class Order:
    deps = ()


def ordered(body, *, in_specs, out_specs, out_shape, scratch_shapes=(), **more):
    single = not isinstance(out_shape, (list, tuple))
    specs, shapes = ([out_specs], [out_shape]) if single else (list(out_specs), list(out_shape))
    deps, n_in, n_out = Order.deps, len(in_specs), len(shapes)

    def wrapped(*refs):
        rest = refs[n_in + len(deps) :]
        body(*refs[:n_in], *rest[:n_out], *rest[n_out + 1 :])
        rest[n_out][...] = jnp.zeros((8, 128), F32)

    mark = VMEM if more.get("grid") is None else pl.BlockSpec((8, 128), lambda *at: (0, 0))
    call = pl.pallas_call(
        wrapped,
        in_specs=[*in_specs, *[ANY] * len(deps)],
        out_specs=[*specs, mark],
        out_shape=[*shapes, jax.ShapeDtypeStruct((8, 128), F32)],
        scratch_shapes=list(scratch_shapes),
        **more,
    )

    def run(*args):
        *out, token = call(*args, *deps)
        Order.deps = (token,)
        return out[0] if single else out

    return run


class Group:
    def __init__(self, arrays, pieces):
        self.arrays = tuple(arrays)
        self.pieces = tuple(pieces)


def row_of(spec, rows, me):
    if spec[0] == "at":
        return spec[1]
    return pl.multiple_of((me ^ spec[1]) * rows, rows)


def weight_copies(group, refs, first, count, dst, sems, me):
    copies = []
    for n, (array, lead, rows, spec) in enumerate(group.pieces):
        src = refs[array].at[lead + (pl.ds(first, count),)]
        copies.append(
            pltpu.make_async_copy(src, dst.at[:, pl.ds(row_of(spec, rows, me), rows)], sems.at[n])
        )
    return copies


def grad_copies(plan, refs, first, count, src, sems, me):
    blocks = pl.ds(first, count)
    return [
        pltpu.make_async_copy(
            src.at[blocks, pl.ds(row_of(spec, rows, me), rows)], refs[array].at[lead + (blocks,)], sems.at[n]
        )
        for n, (array, lead, rows, spec) in enumerate(plan)
    ]


def norms_of(x):
    mean = jnp.mean(x, axis=-1, keepdims=True)
    centred = x - mean
    scale = lax.rsqrt(jnp.mean(centred * centred, axis=-1, keepdims=True) + norm_epsilon)
    return centred * scale, scale


def layer_norms(tokens, vectors, deps=()):
    rows = tokens.shape[0]
    tile = 256

    def body(x_ref, v_ref, *rest):
        one_ref, two_ref = rest[len(deps) :]
        xhat, _ = norms_of(x_ref[...].astype(F32))
        one_ref[...] = (xhat * v_ref[0:1] + v_ref[1:2]).astype(BF)
        two_ref[...] = (xhat * v_ref[2:3] + v_ref[3:4]).astype(BF)

    spec = pl.BlockSpec((tile, D), lambda t: (t, 0))
    return ordered(
        body,
        grid=(rows // tile,),
        in_specs=[spec, pl.BlockSpec(vectors.shape, lambda t: (0, 0))] + [ANY] * len(deps),
        out_specs=[spec, spec],
        out_shape=[jax.ShapeDtypeStruct((rows, D), BF)] * 2,
        **params(16, 20 * rows * D, 6 * rows * D),
    )(tokens, vectors, *deps)


def pack_owned(here, owners, masters, blocks):
    rows = masters.shape[1]
    nb = len(blocks)

    def body(h_ref, o_ref, m_ref, out, stage, sems):
        copies, mine = [], []
        for i, b in enumerate(blocks):
            owner = o_ref[b]
            slot = jnp.int32(0)
            for before in range(b):
                slot = slot + (o_ref[before] == owner).astype(jnp.int32)
            mine.append(owner == h_ref[0])
            copies.append(pltpu.make_async_copy(m_ref.at[slot], stage.at[i], sems.at[i]))
            copies[-1].start()
        for i in range(nb):
            copies[i].wait()
            out[i] = jnp.where(mine[i], stage[i], 0.0).astype(BF)

    return ordered(
        body,
        in_specs=[SMEM, SMEM, ANY],
        out_specs=VMEM,
        out_shape=jax.ShapeDtypeStruct((nb, rows, D), BF),
        scratch_shapes=[pltpu.VMEM((nb, rows, D), F32), pltpu.SemaphoreType.DMA((nb,))],
        **params(16, 1, 1),
    )(here, owners, masters)


def gelu_pair(z):
    size = jnp.abs(z)
    t = pl.reciprocal(1.0 + (0.3275911 * 0.7071067811865476) * size)
    bell = jnp.exp2((-0.5 * LOG2E) * (z * z))
    poly = 0.5 * 1.061405429
    for c in (-1.453152027, 1.421413741, -0.284496736, 0.254829592):
        poly = poly * t + 0.5 * c
    tail = poly * t * bell
    cdf = jnp.where(z >= 0.0, 1.0 - tail, tail)
    return z * cdf, cdf + z * (bell * 0.3989422804014327)


def mlp_chunk(me, h_two, cot, bias, group, first, outs, plan, deps=()):
    rows = h_two.shape[0]
    part = 256
    parts = rows // part
    na, no, nd = len(group.arrays), len(outs), len(deps)
    n_in, n_out = len(group.pieces), len(plan)

    def body(me_ref, h_ref, y_ref, b_ref, *rest):
        w_refs, rest = rest[:na], rest[na + nd :]
        act_ref, dz_ref, db_ref = rest[:3]
        o_refs = rest[3 : 3 + no]
        h, y, w, act, dz, low, in_sem, t_sem, out_sem = rest[3 + no :]
        me_id = me_ref[0]
        at = [pl.ds(p * part, part) for p in range(parts)]
        loads = weight_copies(group, w_refs, first, 2, w, in_sem, me_id)
        tokens = [
            [
                pltpu.make_async_copy(src.at[at[p]], dst.at[at[p]], t_sem.at[n, p])
                for n, (src, dst) in enumerate(((h_ref, h), (y_ref, y)))
            ]
            for p in range(parts)
        ]
        for c in loads:
            c.start()
        for pair in tokens:
            for c in pair:
                c.start()
        for c in loads:
            c.wait()
        for pair in tokens:
            for c in pair:
                c.wait()
        stores, z, u, sums = [], {}, {}, []

        def into(p):
            z[p] = dot(h[at[p]], w[0]) + b_ref[...]
            u[p] = dot_nt(y[at[p]], w[1])

        def slopes(p):
            value, slope = gelu_pair(z[p])
            act[at[p]] = value.astype(BF)
            low_dz = (u[p] * slope).astype(BF)
            dz[at[p]] = low_dz
            sums.append(jnp.sum(low_dz.astype(F32), axis=0, keepdims=True))
            for n, (src, dst) in enumerate(((act, act_ref), (dz, dz_ref))):
                stores.append(pltpu.make_async_copy(src.at[at[p]], dst.at[at[p]], t_sem.at[2 + n, p]))
                stores[-1].start()

        for turn in range(parts + 1):
            if turn < parts:
                into(turn)
            if turn:
                slopes(turn - 1)
        for i, (left, right) in enumerate(((h, dz), (act, y))):
            low[i] = dot_tn(left[...], right[...]).astype(BF)
        for c in grad_copies(plan, o_refs, 0, 2, low, out_sem, me_id):
            c.start()
            stores.append(c)
        db_ref[...] = sum(sums[1:], sums[0])
        for c in stores:
            c.wait()

    act, dz, db, *grads = ordered(
        body,
        in_specs=[SMEM, HBM, HBM, VMEM] + [HBM] * na + [ANY] * nd,
        out_specs=[HBM, HBM, VMEM] + [HBM] * no,
        out_shape=[
            jax.ShapeDtypeStruct((rows, D), BF),
            jax.ShapeDtypeStruct((rows, D), BF),
            jax.ShapeDtypeStruct((1, D), F32),
            *outs,
        ],
        scratch_shapes=[
            pltpu.VMEM((rows, D), BF),
            pltpu.VMEM((rows, D), BF),
            pltpu.VMEM((2, D, D), BF),
            pltpu.VMEM((rows, D), BF),
            pltpu.VMEM((rows, D), BF),
            pltpu.VMEM((2, D, D), BF),
            pltpu.SemaphoreType.DMA((n_in,)),
            pltpu.SemaphoreType.DMA((4, parts)),
            pltpu.SemaphoreType.DMA((n_out,)),
        ],
        **params(60, 8 * rows * D * D, 16 * rows * D),
    )(me, h_two, cot, bias, *group.arrays, *deps)
    return act, dz, db, grads


def turned(x, cosine, from_right, from_left):
    return (
        x * cosine
        + pltpu.roll(x, 128 - ROT // 2, 1) * from_right
        + pltpu.roll(x, ROT // 2, 1) * from_left
    )


def lanes_of(cosine, sine):
    half = ROT // 2
    lane = lax.broadcasted_iota(jnp.int32, (half, 128), 1) % HEAD
    row = lax.broadcasted_iota(jnp.int32, (half, 128), 0)
    one, two = (lane == row).astype(F32), (lane == row + half).astype(F32)

    def spread(values, mask):
        return lax.dot_general(
            values, mask, (((0,), (0,)), ((), ())), precision=lax.Precision.HIGHEST, preferred_element_type=F32
        )

    still = (lax.broadcasted_iota(jnp.int32, (1, 128), 1) % HEAD >= ROT).astype(F32)
    return spread(cosine, one + two) + still, spread(sine, one), spread(sine, two)


def project(me, h_one, cot, bias, cosine, sine, group, deps=()):
    rows = h_one.shape[0]
    tile = 256
    per = cosine.shape[2] // tile
    na, n_in = len(group.arrays), len(group.pieces)

    def body(me_ref, h_ref, y_ref, b_ref, c_ref, s_ref, *rest):
        w_refs, rest = rest[:na], rest[na + len(deps) :]
        outs = rest[:4]
        w_all, sems = rest[4:]
        step = pl.program_id(0)

        @pl.when(step == 0)
        def _():
            copies = weight_copies(group, w_refs, 0, 4, w_all, sems, me_ref[0])
            for c in copies:
                c.start()
            for c in copies:
                c.wait()

        cos_l, right, left = lanes_of(c_ref[0], s_ref[0])
        outs[3][...] = dot_nt(y_ref[...], w_all[3]).astype(BF)
        for i in range(3):
            value = dot(h_ref[...], w_all[i]) + b_ref[i : i + 1]
            if i == 2:
                outs[2][...] = value.astype(BF)
                continue
            for j in range(D // 128):
                outs[i][:, j * 128 : (j + 1) * 128] = turned(
                    value[:, j * 128 : (j + 1) * 128], cos_l, -right, left
                ).astype(BF)

    spec = pl.BlockSpec((tile, D), lambda t: (t, 0))
    table = pl.BlockSpec((1, ROT // 2, tile), lambda t: (t // per, 0, t % per))
    return ordered(
        body,
        grid=(rows // tile,),
        in_specs=[SMEM, spec, spec, pl.BlockSpec((3, D), lambda t: (0, 0)), table, table]
        + [HBM] * na
        + [ANY] * len(deps),
        out_specs=[spec] * 4,
        out_shape=[jax.ShapeDtypeStruct((rows, D), BF)] * 4,
        scratch_shapes=[pltpu.VMEM((4, D, D), BF), pltpu.SemaphoreType.DMA((n_in,))],
        **params(60, 8 * rows * D * D, 20 * rows * D),
    )(me, h_one, cot, bias, cosine, sine, *group.arrays, *deps)


def attention(q, k, v, da, starts, cosine, sine, length, which, into=(), deps=()):
    rows = q.shape[0]
    seqs = len(which)
    half = length // 2
    pair = 128

    def body(q_ref, k_ref, v_ref, d_ref, st_ref, hc_ref, hs_ref, *rest):
        a_ref, dq_ref, dk_ref, dv_ref, db_ref, mask, wheel = rest[len(into) + len(deps) :]

        @pl.when(pl.program_id(1) == 0)
        def _():
            key = lax.broadcasted_iota(jnp.int32, (length, length), 0)
            query = lax.broadcasted_iota(jnp.int32, (length, length), 1)
            seen = (key <= query) & (key >= st_ref[0])
            mask[...] = jnp.where(seen, 0.0, masked_fill)
            wheel[0], wheel[1], wheel[2] = lanes_of(hc_ref[0], hs_ref[0])

        q_all, k_all, v_all, d_all = q_ref[...], k_ref[...], v_ref[...], d_ref[...]
        vt, kt = v_all.T, k_all.T
        dt = d_all.T.astype(F32)
        lane = lax.broadcasted_iota(jnp.int32, (length, pair), 1)
        zero = jnp.zeros((), BF)
        dv = [jnp.zeros((half, pair), F32)] * 2
        dk = [jnp.zeros((half, pair), F32)] * 2
        jobs = []
        for h in range(2):
            mine = (lane >= h * HEAD) & (lane < (h + 1) * HEAD)
            qm = jnp.where(mine, q_all, zero)
            dm = jnp.where(mine, d_all, zero)
            for b in range(2):
                jobs.append((h, b, qm[b * half : (b + 1) * half], dm[b * half : (b + 1) * half]))
        raw, dp, prob, low, at, ds, dqt = {}, {}, {}, {}, {}, {}, {}

        def scores(i):
            h, b, qm, dm = jobs[i]
            n = half * (b + 1)
            raw[i] = dot_nt(k_all[:n], qm)
            dp[i] = dot_nt(v_all[:n], dm)

        def softmax(i):
            h, b, qm, dm = jobs[i]
            n = half * (b + 1)
            s = raw[i] * (HEAD**-0.5 * LOG2E) + mask[:n, b * half : (b + 1) * half]
            e = jnp.exp2(s - jnp.max(s, axis=0, keepdims=True))
            prob[i] = e * (1.0 / jnp.sum(e, axis=0, keepdims=True))
            low[i] = prob[i].astype(BF)
            at[i] = dot(vt[h * HEAD : (h + 1) * HEAD, :n], low[i])

        def slopes(i):
            h, b, qm, dm = jobs[i]
            dh = dt[h * HEAD : (h + 1) * HEAD, b * half : (b + 1) * half]
            total = jnp.sum(dh * at[i], axis=0, keepdims=True)
            ds[i] = (prob[i] * (dp[i] - total)).astype(BF)

        def grads(i):
            h, b, qm, dm = jobs[i]
            n = half * (b + 1)
            dqt[i] = dot(kt[h * HEAD : (h + 1) * HEAD, :n], ds[i])
            more_v, more_k = dot(low[i], dm), dot(ds[i], qm)
            for c in range(b + 1):
                dv[c] = dv[c] + more_v[c * half : (c + 1) * half]
                dk[c] = dk[c] + more_k[c * half : (c + 1) * half]

        stages = (scores, softmax, slopes, grads)
        for turn in range(len(jobs) + len(stages) - 1):
            for n, stage in reversed(list(enumerate(stages))):
                if 0 <= turn - n < len(jobs):
                    stage(turn - n)
        at_h, dq_h = [], []
        for h in range(2):
            at_h.append(jnp.concatenate([at[2 * h], at[2 * h + 1]], axis=1))
            dq = jnp.concatenate([dqt[2 * h], dqt[2 * h + 1]], axis=1) * HEAD**-0.5
            u, w, cos, sin = dq[0:8], dq[8:16], hc_ref[0], hs_ref[0]
            dq_h.append(jnp.concatenate([u * cos + w * sin, w * cos - u * sin, dq[16:]], axis=0))
        a_ref[...] = jnp.concatenate(at_h, axis=0).astype(BF).T
        dq = jnp.concatenate(dq_h, axis=0).astype(BF).T
        dq_ref[...] = dq
        sums = [jnp.sum(dq.astype(F32), axis=0, keepdims=True)]
        sum_k = sum_v = jnp.zeros((1, pair), F32)
        for c in range(2):
            at_k = slice(c * half, (c + 1) * half)
            back = turned(dk[c] * HEAD**-0.5, wheel[0, at_k], wheel[1, at_k], -wheel[2, at_k]).astype(BF)
            dk_ref[at_k] = back
            sum_k = sum_k + jnp.sum(back.astype(F32), axis=0, keepdims=True)
            value = dv[c].astype(BF)
            dv_ref[at_k] = value
            sum_v = sum_v + jnp.sum(value.astype(F32), axis=0, keepdims=True)
        db_ref[0] = jnp.concatenate(sums + [sum_k, sum_v], axis=0)

    base = which[0]
    spec = pl.BlockSpec((length, pair), lambda s, h: (s + base, h))
    table = pl.BlockSpec((1, ROT // 2, length), lambda s, h: (s + base, 0, 0))
    a, dq, dk, dv, db = ordered(
        body,
        grid=(seqs, D // pair),
        in_specs=[spec] * 4
        + [pl.BlockSpec((1, 1, length), lambda s, h: (s + base, 0, 0)), table, table]
        + [ANY] * (len(into) + len(deps)),
        out_specs=[spec, spec, spec, spec, pl.BlockSpec((1, 3, pair), lambda s, h: (s, 0, h))],
        out_shape=[jax.ShapeDtypeStruct((rows, D), BF)] * 4
        + [jax.ShapeDtypeStruct((seqs, 3, D), F32)],
        scratch_shapes=[pltpu.VMEM((length, length), F32), pltpu.VMEM((3, length, 128), F32)],
        input_output_aliases={7 + n: n for n in range(len(into))},
        **params(60, 10e9 * seqs, 20 * rows * D),
    )(q, k, v, da, starts, cosine, sine, *into, *deps)
    return a, dq, dk, dv, db


def attention_grads(me, h_one, a, cot, dqkv, outs, plan, deps=()):
    rows = h_one.shape[0]
    no, n_out = len(outs), len(plan)

    def body(me_ref, h_ref, a_ref, y_ref, dq_ref, dk_ref, dv_ref, *rest):
        rest = rest[len(deps) :]
        o_refs = rest[:no]
        low, sems = rest[no:]
        pending = []
        for i, (left, right) in enumerate(
            ((h_ref, dq_ref), (h_ref, dk_ref), (h_ref, dv_ref), (a_ref, y_ref))
        ):
            low[i] = dot_tn(left[...], right[...]).astype(BF)
            if i % 2:
                copies = grad_copies(plan, o_refs, i - 1, 2, low, sems.at[i // 2], me_ref[0])
                for c in copies:
                    c.start()
                pending += copies
        for c in pending:
            c.wait()

    whole = pl.BlockSpec(memory_space=pltpu.VMEM)
    return ordered(
        body,
        in_specs=[SMEM] + [whole] * 6 + [ANY] * len(deps),
        out_specs=[HBM] * no,
        out_shape=list(outs),
        scratch_shapes=[pltpu.VMEM((4, D, D), BF), pltpu.SemaphoreType.DMA((2, n_out))],
        **params(60, 8 * rows * D * D, 12 * rows * D),
    )(me, h_one, a, cot, *dqkv, *deps)


def products(me, jobs, tail, outs, starts=None, extra=(), deps=(), mib=48):
    starts = starts or [()] * len(jobs)
    rows = jobs[0][0][0].shape[0]
    tile = 256
    groups, used = [], {}
    for job in jobs:
        for _, (group, i), _ in job:
            if id(group) not in used:
                groups.append(group)
                used[id(group)] = []
            used[id(group)].append(i)
    first, flat, runs, slot, at = {}, [], [], {}, 0
    for group in groups:
        first[id(group)] = len(flat)
        flat += list(group.arrays)
        low, high = min(used[id(group)]), max(used[id(group)])
        runs.append((group, low, high - low + 1, at))
        for i in range(low, high + 1):
            slot[id(group), i] = at
            at += 1
    lefts = [left for job in jobs for left, _, _ in job]
    begun = [x for group in starts for x in group]
    n_in = max(len(g.pieces) for g in groups)
    nl, ns, ne, nw, no = len(lefts), len(begun), len(extra), len(flat), len(outs)

    def body(me_ref, *rest):
        l_refs, rest = rest[:nl], rest[nl:]
        s_refs, rest = list(rest[:ns]), rest[ns:]
        e_refs, rest = rest[:ne], rest[ne:]
        w_refs, rest = rest[:nw], rest[nw + len(deps) :]
        o_refs, (w_all, sems) = rest[:no], rest[no:]
        step = pl.program_id(0)

        @pl.when(step == 0)
        def _():
            copies = []
            for n, (group, low, count, to) in enumerate(runs):
                refs = w_refs[first[id(group)] :]
                copies += weight_copies(
                    group, refs, low, count, w_all.at[pl.ds(to, count)], sems.at[n], me_ref[0]
                )
            for c in copies:
                c.start()
            for c in copies:
                c.wait()

        results, n = [], 0
        for job, begin in zip(jobs, starts):
            total = None
            for _ in begin:
                more = s_refs.pop(0)[...]
                total = more if total is None else total + more
            for _, (group, i), transposed in job:
                term = (dot_nt if transposed else dot)(l_refs[n][...], w_all[slot[id(group), i]])
                total = term if total is None else total + term
                n += 1
            results.append(total)
        tail(e_refs, results, o_refs, step)

    spec = pl.BlockSpec((tile, D), lambda t: (t, 0))

    def whole(x):
        return pl.BlockSpec(x.shape, lambda t: (0,) * len(x.shape))

    return ordered(
        body,
        grid=(rows // tile,),
        in_specs=[SMEM]
        + [spec] * (nl + ns)
        + [spec if per_token else whole(x) for x, per_token in extra]
        + [HBM] * nw
        + [ANY] * len(deps),
        out_specs=[spec if x.shape[0] == rows else whole(x) for x in outs],
        out_shape=list(outs),
        scratch_shapes=[pltpu.VMEM((at, D, D), BF), pltpu.SemaphoreType.DMA((len(runs), n_in))],
        **params(mib, 2 * nl * rows * D * D, (2 * nl + 8) * rows * D),
    )(me, *lefts, *begun, *[x for x, _ in extra], *flat, *deps)


def store_all(e_refs, results, o_refs, step):
    for ref, value in zip(o_refs, results):
        ref[...] = value


def add_rows(ref, terms, step):
    sums = jnp.concatenate([jnp.sum(term, axis=0, keepdims=True) for term in terms], axis=0)

    @pl.when(step == 0)
    def _():
        ref[...] = sums

    @pl.when(step > 0)
    def _():
        ref[...] += sums


def middle_tail(e_refs, results, o_refs, step):
    x_ref, y_ref, v_ref = e_refs
    out_ref, e_ref, sum_ref = o_refs
    out, d_one, d_two = results
    x = x_ref[...].astype(F32)
    out_ref[...] = out + x + (v_ref[7:8] + v_ref[8 + SPREAD : 9 + SPREAD])
    xhat, _ = norms_of(x)
    e_ref[...] = d_one * v_ref[0:1] + d_two * v_ref[2:3]
    add_rows(sum_ref, (d_one * xhat, d_one, d_two * xhat, d_two, y_ref[...].astype(F32)), step)


def last_tail(e_refs, results, o_refs, step):
    x_ref, y_ref, v_ref, e_ref = e_refs
    out_ref, grad_ref, sum_ref = o_refs
    out, d_two = results
    out_ref[...] = out.astype(BF)
    xhat, scale = norms_of(x_ref[...].astype(F32))
    e = e_ref[...] + d_two * v_ref[2:3]
    inner = jnp.mean(e * xhat, axis=-1, keepdims=True)
    y = y_ref[...].astype(F32)
    grad_ref[...] = y + (e - jnp.mean(e, axis=-1, keepdims=True) - xhat * inner) * scale
    add_rows(sum_ref, (d_two * xhat, d_two), step)


def adam(gradient, weight, moment, square, rate, decay, one_fix, two_fix):
    moment_new = beta_first * moment + (1.0 - beta_first) * gradient
    square_new = beta_second * square + (1.0 - beta_second) * gradient * gradient
    update = (moment_new * one_fix) / (jnp.sqrt(square_new * two_fix) + adam_epsilon)
    return weight - rate * (update + decay * weight), moment_new, square_new


def update_all(source, fixes, squares, vector_total, vector_state, summed, masters, firsts, seconds):
    slots, rows, _ = masters.shape
    ng = len(summed)

    def body(src_ref, fix_ref, q_ref, t_ref, vw_ref, vm_ref, vv_ref, *rest):
        g_refs, (w_ref, m_ref, v_ref) = rest[:ng], rest[ng : ng + 3]
        norm_out, tg_out, tw_out, tm_out, tv_out, g_out, w_out, m_out, v_out, c_out, clip_ref = rest[ng + 3 :]
        slot = pl.program_id(0)
        one_fix, two_fix = fix_ref[0], fix_ref[1]

        @pl.when(slot == 0)
        def _():
            t = t_ref[...]
            norm = jnp.sqrt(jnp.sum(q_ref[...], keepdims=True) + jnp.sum(t * t, keepdims=True))
            clip = jnp.minimum(1.0, 1.0 / (norm + 1e-06))
            norm_out[...] = norm
            clip_ref[...] = jnp.broadcast_to(clip, clip_ref.shape)
            gradient = t * clip
            new, moment, square = adam(
                gradient, vw_ref[...], vm_ref[...], vv_ref[...], vector_rate, 0.0, one_fix, two_fix
            )
            tg_out[...], tw_out[...], tm_out[...], tv_out[...] = gradient, new, moment, square

        keep = src_ref[2, slot] > 0
        low = g_refs[0][0]
        for n in range(1, ng):
            low = jnp.where(src_ref[0, slot] == n, g_refs[n][0], low)
        gradient = low.astype(F32) * clip_ref[0:1, 0:1]
        new, moment, square = adam(
            gradient, w_ref[0], m_ref[0], v_ref[0], learn_rate, weight_decay, one_fix, two_fix
        )
        new = jnp.where(keep, new, 0.0)
        g_out[0] = jnp.where(keep, gradient, 0.0)
        w_out[0] = new
        m_out[0] = jnp.where(keep, moment, 0.0)
        v_out[0] = jnp.where(keep, square, 0.0)
        c_out[0] = new.astype(BF)

    def whole(shape):
        return pl.BlockSpec(shape, lambda s, src, fix: (0,) * len(shape))

    def picked(n):
        return pl.BlockSpec(
            (1, rows, D), lambda s, src, fix: (jnp.where(src[0, s] == n, src[1, s], 0), 0, 0)
        )

    own = pl.BlockSpec((1, rows, D), lambda s, src, fix: (s, 0, 0))
    vec = vector_total.shape
    return pl.pallas_call(
        body,
        grid_spec=pltpu.PrefetchScalarGridSpec(
            num_scalar_prefetch=2,
            grid=(slots,),
            in_specs=[whole((8, 128))] + [whole(vec)] * 4 + [picked(n) for n in range(ng)] + [own] * 3,
            out_specs=[whole((1, 1))] + [whole(vec)] * 4 + [own] * 5,
            scratch_shapes=[pltpu.VMEM((8, 128), F32)],
        ),
        out_shape=[jax.ShapeDtypeStruct((1, 1), F32)]
        + [jax.ShapeDtypeStruct(vec, F32)] * 4
        + [jax.ShapeDtypeStruct((slots, rows, D), F32)] * 4
        + [jax.ShapeDtypeStruct((slots, rows, D), BF)],
        **params(24, 20 * slots * rows * D, 32 * slots * rows * D),
    )(source, fixes, squares, vector_total, *vector_state, *summed, masters, firsts, seconds)


def stacked(pieces, deps=()):
    count = len(pieces)

    def body(*refs):
        out, sems = refs[count + len(deps) :]
        copies = [pltpu.make_async_copy(refs[n], out.at[n], sems.at[n]) for n in range(count)]
        for c in copies:
            c.start()
        for c in copies:
            c.wait()

    return ordered(
        body,
        in_specs=[ANY] * (count + len(deps)),
        out_specs=VMEM,
        out_shape=jax.ShapeDtypeStruct((count, *pieces[0].shape), pieces[0].dtype),
        scratch_shapes=[pltpu.SemaphoreType.DMA((count,))],
        **params(16, 1, 1),
    )(*pieces, *deps)


def pair_sums(pairs, deps=()):
    chips, each, rows, _ = pairs[0][0].shape
    count = len(pairs)

    def body(*refs):
        outs = refs[2 * count + len(deps) :]
        for n in range(chips):

            @pl.when(pl.program_id(0) == n)
            def _(n=n):
                for i in range(count):
                    keep, got = refs[2 * i], refs[2 * i + 1]
                    outs[n][i * each : (i + 1) * each] = (keep[0].astype(F32) + got[0].astype(F32)).astype(BF)

    spec = pl.BlockSpec((1, each, rows, D), lambda n: (n, 0, 0, 0))
    one = (count * each, rows, D)
    return ordered(
        body,
        grid=(chips,),
        in_specs=[spec] * (2 * count) + [ANY] * len(deps),
        out_specs=[pl.BlockSpec(one, lambda n: (0, 0, 0))] * chips,
        out_shape=[jax.ShapeDtypeStruct(one, BF)] * chips,
        **params(16, 1, 1),
    )(*[x for pair in pairs for x in pair], *deps)


def total_of(*groups):
    flat = [x for group in groups for x in group]
    _, rows, _ = flat[0].shape
    blocks = sum(group[0].shape[0] for group in groups)

    def body(*refs):
        out, n, at = refs[len(flat)], 0, 0
        for group in groups:
            total = refs[n][...].astype(F32)
            for ref in refs[n + 1 : n + len(group)]:
                total = total + ref[...].astype(F32)
            out[at : at + total.shape[0]] = total.astype(BF)
            n, at = n + len(group), at + total.shape[0]

    return ordered(
        body,
        in_specs=[VMEM] * len(flat),
        out_specs=VMEM,
        out_shape=jax.ShapeDtypeStruct((blocks, rows, D), BF),
        **params(16, 1, 1),
    )(*flat)


def handed_on(value):
    def body(value_ref, out):
        pass

    return ordered(
        body,
        in_specs=[ANY],
        out_specs=ANY,
        out_shape=jax.ShapeDtypeStruct(value.shape, value.dtype),
        input_output_aliases={0: 0},
        **params(1, 1, 1),
    )(value)


def vector_terms(sums, last_sums, db_a, db_b, dbs):
    def body(s_ref, l_ref, a_ref, b_ref, *rest):
        out = rest[SPREAD]
        out[0:2] = s_ref[0:2]
        out[2:4] = s_ref[2:4] + l_ref[...]
        qkv = a_ref[0] + b_ref[0]
        for n in range(1, a_ref.shape[0]):
            qkv = qkv + (a_ref[n] + b_ref[n])
        out[4:7] = qkv
        out[7:8] = s_ref[4:5]
        for n in range(SPREAD):
            out[8 + n : 9 + n] = rest[n][...]
        out[8 + SPREAD : 9 + SPREAD] = s_ref[4:5]

    return ordered(
        body,
        in_specs=[VMEM] * (4 + SPREAD),
        out_specs=VMEM,
        out_shape=jax.ShapeDtypeStruct((9 + SPREAD, D), F32),
        **params(16, 1, 1),
    )(sums, last_sums, db_a, db_b, *dbs)


def plus(a, b):
    def body(a_ref, b_ref, out):
        out[...] = a_ref[...] + b_ref[...]

    return ordered(
        body,
        in_specs=[VMEM] * 2,
        out_specs=VMEM,
        out_shape=jax.ShapeDtypeStruct(a.shape, F32),
        **params(16, 1, 1),
    )(a, b)


def picked_end(here, value, outer):
    def body(h_ref, v_ref, o_ref, out):
        ends = (h_ref[0] == 0) | (h_ref[0] == 3)
        out[...] = jnp.where(ends, o_ref[...], v_ref[...])

    return ordered(
        body,
        in_specs=[SMEM, VMEM, VMEM],
        out_specs=VMEM,
        out_shape=jax.ShapeDtypeStruct(value.shape, BF),
        **params(16, 1, 1),
    )(here, value, outer)


def settled(value, other):
    count, rows, _ = value.shape

    def body(v_ref, o_ref, out_ref, q_ref):
        total = jnp.zeros((8, 128), F32)
        for n in range(count):
            low = (v_ref[n].astype(F32) + o_ref[n].astype(F32)).astype(BF)
            out_ref[n] = low
            x = low.astype(F32)
            x = x * x
            for c in range(D // 128):
                part = x[:, c * 128 : (c + 1) * 128]
                for r in range(rows // 8):
                    total = total + part[r * 8 : (r + 1) * 8]
        q_ref[...] = total

    return ordered(
        body,
        in_specs=[VMEM, VMEM],
        out_specs=[VMEM, VMEM],
        out_shape=[jax.ShapeDtypeStruct(value.shape, BF), jax.ShapeDtypeStruct((8, 128), F32)],
        **params(16, 1, 1),
    )(value, other)


def swap(value, axis, bit):
    size = lax.axis_size(axis)
    return lax.ppermute(value, axis, [(i, i ^ bit) for i in range(size)])


CORE, SIDE, UP = 1, 2, 4
CHIPS = (0, SIDE, UP, SIDE | UP)


INWARD, ACROSS, OUTWARD = [(0, 1), (3, 2)], [(1, 2), (2, 1)], [(1, 0), (2, 3)]


def hop(value, pairs):
    if lax.axis_size("narrow") == 4:
        return lax.ppermute(value, "narrow", pairs)
    if pairs is INWARD:
        return (lax.psum(value.astype(F32), "narrow") - value.astype(F32)).astype(BF)
    return jnp.zeros_like(value) if pairs is ACROSS else value


def near(value):
    if lax.axis_size("narrow") == 4:
        return swap(value, "narrow", 1)
    return (lax.psum(value.astype(F32), "narrow") - value.astype(F32)).astype(BF)


def far(value):
    return swap(value, "narrow", 2) if lax.axis_size("narrow") == 4 else jnp.zeros_like(value)


def spread_wide(value):
    if lax.axis_size("wide") == 8:
        return [swap(value, "wide", m) for m in CHIPS[1:]]
    return None


def gather_wide(value):
    size = lax.axis_size("wide")
    count, rows, _ = value.shape
    full = lax.all_gather(value, "wide", axis=0, tiled=False)
    if rows % 16:
        full = jnp.swapaxes(full, 0, 1).reshape(1, count, D, D)
        size, rows = 1, D
    return Group((full,), [(0, (p,), rows, ("at", rows * p)) for p in range(size)])


def grad_layout(count, rows, size):
    if size != 8:
        return [jax.ShapeDtypeStruct((count, D, D), BF)], [(0, (), D, ("at", 0))]
    shape = jax.ShapeDtypeStruct((4, count, rows, D), BF)
    keep = [(0, (n,), rows, ("xor", m)) for n, m in enumerate(CHIPS)]
    give = [(1, (n,), rows, ("xor", m ^ CORE)) for n, m in enumerate(CHIPS)]
    return [shape] * 2, keep + give


def gathered(shard, parts):
    if parts is None:
        return gather_wide(shard)
    mine = stacked([shard, *parts])
    other = swap(mine, "wide", CORE)
    rows = shard.shape[1]
    masks = [(m, 0) for m in CHIPS] + [(m ^ CORE, 1) for m in CHIPS]
    return Group((mine, other), [(a, (n % 4,), rows, ("xor", m)) for n, (m, a) in enumerate(masks)])


def give(grads):
    if len(grads) == 1:
        return lax.psum_scatter(grads[0], "wide", scatter_dimension=1, tiled=True)
    return grads[0], swap(grads[1], "wide", CORE)


def exchange(*given):
    if not isinstance(given[0], tuple):
        return [given[0] if len(given) == 1 else jnp.concatenate(given, axis=0)]
    parts = pair_sums(list(given))
    return [parts[0]] + [swap(p, "wide", m) for p, m in zip(parts[1:], CHIPS[1:])]


def total_axis(value, axis):
    size = lax.axis_size(axis)
    bit = 1
    while bit < size:
        value = value + swap(value, axis, bit)
        bit *= 2
    return value


def slot_table(owners, capacity):
    number = owners.shape[0]
    order = jnp.arange(number, dtype=jnp.int32)
    before = (owners[:, None] == owners[None, :]) & (order[None, :] < order[:, None])
    return owners * capacity + jnp.sum(before.astype(jnp.int32), axis=1)


def per_device(tokens, doc_lengths, cotangent, owners, step_count, master, moment_one, moment_two, vectors, vector_one, vector_two):
    rows, capacity, _ = master.shape
    seqs = doc_lengths.shape[0]
    length = tokens.shape[0] // seqs
    blocks = owners.shape[0]
    wide = lax.axis_size("wide")
    narrow_index = lax.axis_index("narrow")
    me = lax.axis_index("wide").astype(jnp.int32).reshape(1)
    masters, firsts, seconds = [jnp.swapaxes(m, 0, 1) for m in (master, moment_one, moment_two)]

    here = narrow_index.astype(jnp.int32).reshape(1)
    local = slot_table(owners, capacity) - owners * capacity
    ends = jnp.cumsum(doc_lengths, axis=1)
    position = jnp.arange(length, dtype=jnp.int32)
    passed = position[None, None, :] >= ends[:, :, None]
    start = jnp.sum(jnp.where(passed, doc_lengths[:, :, None], 0), axis=1)
    freqs = jnp.power(rope_base, -2.0 * jnp.arange(ROT // 2, dtype=F32) / ROT)
    angle = (position[None] - start).astype(F32)[:, None, :] * freqs[None, :, None]
    cosine, sine = jnp.cos(angle), jnp.sin(angle)
    start = start[:, None, :]

    ids_0, ids_s, ids_t = (4, 8, 5, 9), (0, 1, 2, 3), (6, 10, 7, 11)
    pair_outs, pair_plan = grad_layout(2, rows, wide)
    four_outs, four_plan = grad_layout(4, rows, wide)
    full = jax.ShapeDtypeStruct(tokens.shape, F32)
    low = jax.ShapeDtypeStruct(tokens.shape, BF)
    acts, dzs, dbs, place = [], [], [], {}
    Order.deps = ()

    def arrived(group, ids):
        for i, b in enumerate(ids):
            place[b] = (group, i)

    def chunk(j):
        group, first = place[4 + j]
        act, dz, db, grads = mlp_chunk(
            me, h_two, cotangent, vectors[8 + j : 9 + j], group, first, pair_outs, pair_plan
        )
        acts.append(act)
        dzs.append(dz)
        dbs.append(db)
        return grads

    def forth(j):
        return (acts[j], place[8 + j], False)

    def back(j):
        return (dzs[j], place[4 + j], True)

    w_0 = pack_owned(here, owners, masters, ids_0)
    r_0 = hop(w_0, INWARD)
    h_one, h_two = layer_norms(tokens, vectors)
    w_0 = total_of([w_0, r_0])
    r_0 = hop(w_0, ACROSS)
    w_s = pack_owned(here, owners, masters, ids_s)
    r_s = hop(w_s, INWARD)
    w_0 = total_of([w_0, r_0])
    r_0 = hop(w_0, OUTWARD)
    w_s = total_of([w_s, r_s])
    r_s = hop(w_s, ACROSS)
    w_0 = picked_end(here, w_0, r_0)
    arrived(gather_wide(w_0), ids_0)
    w_t = pack_owned(here, owners, masters, ids_t)
    r_t = hop(w_t, INWARD)
    w_s = total_of([w_s, r_s])
    r_s = hop(w_s, OUTWARD)
    w_t = total_of([w_t, r_t])
    r_t = hop(w_t, ACROSS)
    w_s = picked_end(here, w_s, r_s)
    arrived(gather_wide(w_s), ids_s)
    w_t = total_of([w_t, r_t])
    r_t = hop(w_t, OUTWARD)
    s_0 = give(chunk(0))
    s_1 = give(chunk(1))
    w_t = picked_end(here, w_t, r_t)
    arrived(gather_wide(w_t), ids_t)
    front = exchange(s_0, s_1)
    q, k, v, da = project(me, h_one, cotangent, vectors[4:7], cosine, sine, place[0][0])
    half = seqs // 2
    *inner, db_a = attention(q, k, v, da, start, cosine, sine, length, tuple(range(half)))
    a, *dqkv, db_b = attention(
        q, k, v, da, start, cosine, sine, length, tuple(range(half, seqs)), into=inner
    )
    front = total_of(front)
    r_f = near(front)
    s_s = give(attention_grads(me, h_one, a, cotangent, dqkv, four_outs, four_plan))
    s_2 = give(chunk(2))
    front = total_of([front, r_f])
    r_f = far(front)
    mid = exchange(s_s)
    middle, e_part, sums = products(
        me,
        [
            [(a, place[3], False), forth(2)],
            [(dqkv[n], place[n], True) for n in range(3)],
            [back(2)],
        ],
        middle_tail,
        [full, full, jax.ShapeDtypeStruct((5, D), F32)],
        extra=[(tokens, True), (cotangent, True), (vectors, False)],
    )
    third = exchange(s_2)
    mid = total_of(mid)
    r_m = near(mid)
    s_3 = chunk(3)
    mid = total_of([mid, r_m])
    r_m = far(mid)
    front, front_square = settled(front, r_f)
    third = total_of(third)
    r_h = near(third)
    last = exchange(give([*s_3[:-1], handed_on(s_3[-1])]))
    early = products(me, [[forth(0), forth(1)], [back(0), back(1)]], store_all, [full, full])
    last = total_of(last)
    r_l = near(last)
    third = total_of([third, r_h])
    r_h = far(third)
    layer_out, input_grad, last_sums = products(
        me,
        [[forth(3)], [back(3)]],
        last_tail,
        [low, full, jax.ShapeDtypeStruct((2, D), F32)],
        starts=[(middle, early[0]), (early[1],)],
        extra=[(tokens, True), (cotangent, True), (vectors, False), (e_part, True)],
    )
    last = total_of([last, r_l])
    r_l = far(last)
    third, third_square = settled(third, r_h)
    mid, mid_square = settled(mid, r_m)
    vector_total = vector_terms(sums, last_sums, db_a, db_b, dbs)
    masks = [(axis, 1 << n) for axis in ("wide", "narrow") for n in range(lax.axis_size(axis).bit_length() - 1)]

    def vector_step(value):
        return plus(value, swap(value, *masks.pop(0)))

    while masks[0][0] == "wide":
        vector_total = vector_step(vector_total)
    last, last_square = settled(last, r_l)
    while masks:
        vector_total = vector_step(vector_total)
    squares = total_axis(front_square + mid_square + third_square + last_square, "wide")
    summed = (front, mid, third, last)
    held = ((4, 8, 5, 9), ids_s, (6, 10), (7, 11))
    step_float = step_count[0].astype(F32)
    fixes = jnp.stack(
        [1.0 / (1.0 - jnp.power(beta_first, step_float)), 1.0 / (1.0 - jnp.power(beta_second, step_float))]
    )
    slot = jnp.arange(capacity, dtype=jnp.int32)
    hit = ((owners == narrow_index)[None, :] & (local[None, :] == slot[:, None])).astype(jnp.int32)
    which, inner = [0] * blocks, [0] * blocks
    for n, ids in enumerate(held):
        for i, b in enumerate(ids):
            which[b], inner[b] = n, i
    source = jnp.stack(
        [
            jnp.sum(hit * jnp.array(which, jnp.int32)[None], axis=1),
            jnp.sum(hit * jnp.array(inner, jnp.int32)[None], axis=1),
            jnp.sum(hit, axis=1),
        ]
    )
    norm, vector_grads, new_vectors, vector_first, vector_second, *new = update_all(
        source, fixes, squares, vector_total, (vectors, vector_one, vector_two), summed, masters, firsts, seconds
    )
    block_grads, new_master, new_first, new_second, new_copies = [jnp.swapaxes(m, 0, 1) for m in new]
    return (
        layer_out,
        input_grad,
        norm[0, 0],
        block_grads,
        new_master,
        new_first,
        new_second,
        new_copies,
        vector_grads,
        new_vectors,
        vector_first,
        vector_second,
    )


def solution(mesh):
    tok = P(("wide", "narrow"), None)
    own = P("wide", "narrow", None)
    return jax.shard_map(
        per_device,
        mesh=mesh,
        in_specs=(tok, tok, tok, P(), P(), own, own, own, P(), P(), P()),
        out_specs=(tok, tok, P(), own, own, own, own, own, P(), P(), P(), P()),
        check_vma=False,
    )
```
